128 devices in a mesh: dp: 64 (over y, x, z), seq: 2 (over core).
Axes of the slice: x: 4, y: 4, z: 4, core: 2. Of those that a mesh axis runs over, the one named last changes fastest.
Arguments:
- inputs: bfloat16 [16384, 768], P(('dp', 'seq')), may hold values from -24 to 24
- history: bfloat16 [12, 16384, 768], P(None, ('dp', 'seq')), may hold values from -6 to 6
- alpha_mid: float32 [13], replicated, may hold values from 0.2 to 0.6
- alpha_last: float32 [14], replicated, may hold values from 0.2 to 0.6
- attn_gains: float32 [2, 768], replicated, may hold values from 0.5 to 1.5
- mlp_gains: float32 [2, 768], replicated, may hold values from 0.5 to 1.5
- w_qkv: bfloat16 [2, 768, 2304], replicated, may hold values from -0.21875 to 0.21875
- w_attn_out: bfloat16 [2, 768, 768], replicated, may hold values from -0.875 to 0.875
- w_up: bfloat16 [2, 768, 3072], replicated, may hold values from -0.21875 to 0.21875
- w_down: bfloat16 [2, 768, 3072], replicated, may hold values from -0.109375 to 0.109375
- doc_lengths: int32 [64, 3], P('dp'), may hold values from 1 to 192, 256 in all within a row
- cotangent: bfloat16 [16384, 768], P(('dp', 'seq')), may hold values from -24 to 24
Outputs:
- final_mix: bfloat16 [16384, 768], P(('dp', 'seq'))
- input_grad: float32 [16384, 768], P(('dp', 'seq'))
- history_grad: bfloat16 [12, 16384, 768], P(None, ('dp', 'seq'))
- alpha_mid_grad: float32 [13], replicated
- alpha_last_grad: float32 [14], replicated
- attn_gains_grad: float32 [2, 768], replicated
- mlp_gains_grad: float32 [2, 768], replicated
- w_qkv_grad: float32 [2, 768, 2304], P(None, ('dp', 'seq'))
- w_attn_out_grad: float32 [2, 768, 768], P(None, ('dp', 'seq'))
- w_up_grad: float32 [2, 768, 3072], P(None, ('dp', 'seq'))
- w_down_grad: float32 [2, 768, 3072], P(None, ('dp', 'seq'))
The draws below stay inside these ranges and needn't reach their ends.
Inputs may be any that keep to these rules, and one draw needn't show every extreme that they name: `doc_lengths`: row g holds the lengths of the 3 documents packed in order into the 256 tokens of group g; each row sums to 256 and its longest is exactly 192.
All inputs are finite; a program needn't handle non-finite values.
Results may differ from the reference program's by a relative error of at most 0.014.
Values may be sent and summed in bfloat16 or wider, within the bound.
No kernel may reach another device: no remote copies, remote signals or barrier semaphores. Data moves between devices by JAX's collectives and lax.ppermute only.
A program may use at most 320 MiB of HBM per device.

```python
import math
import jax
import jax.numpy as jnp
import numpy as np
from jax import lax

D = 768
HEADS = 12
HEAD = 64
FF = 3072
HIST = 12
NDOC = 3
GROUP = 256
TOKENS = 16384
N_DP = 64


def strengthened(array, own_key, source, target, blocks, factor):
    owner, partner = [(jnp.arange(array.shape[axis_at]) // (array.shape[axis_at] // blocks)).reshape([-1 if axis == axis_at else 1 for axis in range(array.ndim)]) for axis_at in (source, target)]
    chosen = jax.random.permutation(own_key, blocks)[partner]
    strong = (owner == chosen) | (owner == (partner + blocks // 2) % blocks)
    return jnp.where(strong, factor * array, array)


def block_scale(rng, extent, shards, smallest, top_value):
    level = 1.0
    for axis_at, blocks in shards:
        steps = jax.random.uniform(jax.random.fold_in(jax.random.fold_in(rng, 6), axis_at), (blocks,), jnp.float32, smallest / len(shards), top_value / len(shards))
        level = level * jnp.repeat(jnp.exp(steps), extent[axis_at] // blocks).reshape((-1,) + (1,) * (len(extent) - 1 - axis_at))
    return level


def profile(number_of, total, limit, skew):
    weights = [(1 << 20) // math.isqrt(standing ** skew) + 1 for standing in range(2, number_of + 1)]
    spare, holding = total - limit - (number_of - 1), [1] * (number_of - 1)
    while spare > 0:
        free = [i for i in range(number_of - 1) if holding[i] < limit]
        pool, remaining = sum([weights[i] for i in free]), spare
        for i in free:
            extra = min(limit - holding[i], max(1, remaining * weights[i] // pool), spare)
            holding[i] = holding[i] + extra
            spare = spare - extra
    return np.array([limit] + holding)


def uneven(rng, count, total, most, skew):
    if count == 2:
        one = jax.random.randint(rng, (), max(1, total - most), min(most, total - 1) + 1)
        return jnp.stack([one, total - one])
    sizes = jnp.asarray(profile(count, total, most, skew), jnp.int32)
    twos = (count - 1) // 2
    source_of, taker = sizes[1:1 + 2 * twos:2], sizes[2:2 + 2 * twos:2]
    slack = jnp.minimum(source_of - 1, most - taker)
    moved = jax.random.randint(jax.random.fold_in(rng, 1), (twos,), 0, 1 << 20) % (slack + 1)
    sizes = sizes.at[1:1 + 2 * twos:2].set(source_of - moved).at[2:2 + 2 * twos:2].set(taker + moved)
    return sizes[jax.random.permutation(jax.random.fold_in(rng, 2), count)]


def noise(stream_key, shape, scale, limit, cuts=(), held_as=jnp.bfloat16):
    loudness = block_scale(stream_key, shape, cuts, -0.22, 0.18) if cuts else 1.0
    drawn = jax.random.normal(stream_key, shape, jnp.float32) * scale * loudness
    return jnp.minimum(jnp.maximum(drawn, -limit), limit).astype(held_as)


def noise_with(rng, extent, scale, bound, cuts, heavy, held_as=jnp.bfloat16):
    result = scale * jax.random.normal(rng, extent, jnp.float32)
    if cuts:
        result = result * block_scale(rng, extent, cuts, -0.22, 0.18)
    return jnp.clip(strengthened(result, jax.random.fold_in(rng, 3), *heavy), -bound, bound).astype(held_as)


def setup_inputs(seed: int = 0) -> dict:
    seeds = jax.random.split(jax.random.key(seed), 13)
    inputs = noise_with(seeds[0], (TOKENS, D), 1.0, 24.0, ((0, 128),), (0, 1, 128, 5.5))
    history = noise(seeds[1], (HIST, TOKENS, D), 1.0, 6.0, ((1, 128),))
    alpha_mid = jnp.clip(jax.random.uniform(seeds[2], (HIST + 1,), jnp.float32, 0.2, 0.6), 0.2, 0.6)
    alpha_last = jnp.clip(jax.random.uniform(seeds[3], (HIST + 2,), jnp.float32, 0.2, 0.6), 0.2, 0.6)
    attn_gains = jnp.clip(1.0 + 0.1 * jax.random.normal(seeds[4], (2, D), jnp.float32), 0.5, 1.5)
    mlp_gains = jnp.clip(1.0 + 0.1 * jax.random.normal(seeds[5], (2, D), jnp.float32), 0.5, 1.5)
    w_qkv = noise(seeds[6], (2, D, 3 * D), D ** -0.5, 0.21875)
    w_attn_out = noise(seeds[7], (2, D, D), (D // 16) ** -0.5, 0.875)
    w_up = noise(seeds[8], (2, D, FF), D ** -0.5, 0.21875)
    w_down = noise(seeds[9], (2, D, FF), FF ** -0.5, 0.109375)
    doc_lengths = jax.vmap(lambda own: uneven(own, NDOC, GROUP, 3 * GROUP // 4, 2))(jax.random.split(seeds[10], N_DP)).reshape((N_DP, NDOC)).astype(jnp.int32)
    cotangent = noise_with(seeds[11], (TOKENS, D), 1.0, 24.0, ((0, 128),), (0, 1, 128, 5.5))
    return {"inputs": inputs, "history": history, "alpha_mid": alpha_mid, "alpha_last": alpha_last, "attn_gains": attn_gains, "mlp_gains": mlp_gains, "w_qkv": w_qkv, "w_attn_out": w_attn_out, "w_up": w_up, "w_down": w_down, "doc_lengths": doc_lengths, "cotangent": cotangent}


@jax.custom_vjp
def low(v):
    return lax.optimization_barrier(v.astype(jnp.bfloat16)).astype(jnp.float32)

@jax.custom_vjp
def low_back(v):
    return v

def low_keep(v):
    return (low(v), None)

def low_pass(kept, grad):
    return (grad,)

def back_keep(v):
    return (v, None)

def back_low(kept, grad):
    return (low(grad),)
low.defvjp(low_keep, low_pass)
low_back.defvjp(back_keep, back_low)
epsilon = 1e-05
masked_score = -1e+30
rotary_base = 10000.0

def dot_high(left, right):
    return jnp.dot(left, right, precision=lax.Precision.HIGHEST)

def layer_norm(stream, gain):
    center = lax.optimization_barrier(jnp.mean(stream, axis=-1, keepdims=True))
    shifted = stream - center
    spread = lax.optimization_barrier(jnp.mean(shifted * shifted, axis=-1, keepdims=True))
    return shifted * lax.rsqrt(spread + epsilon) * gain

def rotate(vectors, cosine, sine):
    half_dim = vectors.shape[-1] // 2
    front_half = vectors[..., :half_dim]
    back_half = vectors[..., half_dim:]
    return jnp.concatenate([front_half * cosine - back_half * sine, back_half * cosine + front_half * sine], axis=-1)

def doc_layout(lengths, row_count):
    doc_ends = jnp.cumsum(lengths).astype(jnp.int32)
    positions = jnp.arange(row_count, dtype=jnp.int32)
    doc_ids = lax.optimization_barrier(jnp.sum((positions[:, None] >= doc_ends[None, :]).astype(jnp.int32), axis=1)).astype(jnp.int32)
    doc_starts = (doc_ends - lengths).astype(jnp.int32)
    onehot = (doc_ids[:, None] == jnp.arange(lengths.shape[0], dtype=jnp.int32)[None, :]).astype(jnp.int32)
    first_rows = lax.optimization_barrier(jnp.sum(onehot * doc_starts[None, :], axis=1)).astype(jnp.int32)
    return (doc_ids, (positions - first_rows).astype(jnp.int32))

def rotary_tables(offsets, head_dim):
    half_dim = head_dim // 2
    frequency = jnp.exp(-math.log(rotary_base) * 2.0 * jnp.arange(half_dim, dtype=jnp.float32) / head_dim)
    angles = offsets.astype(jnp.float32)[:, None] * frequency[None, :]
    return (jnp.cos(angles)[:, None, :], jnp.sin(angles)[:, None, :])

def residual_block(stream, gain_attn, gain_mlp, weight_qkv, weight_out, weight_up, weight_down, cosine, sine, allowed):
    row_count = stream.shape[0]
    score_scale = 1.0 / math.sqrt(HEAD)
    highest = lax.Precision.HIGHEST
    normed = low(layer_norm(stream, gain_attn))
    packed = low(low_back(dot_high(normed, weight_qkv))).reshape(row_count, 3, HEADS, HEAD)
    queries = low(rotate(packed[:, 0], cosine, sine))
    keys_rot = low(rotate(packed[:, 1], cosine, sine))
    values = packed[:, 2]
    scores = low_back(jnp.einsum('qhd,khd->hqk', queries, keys_rot, precision=highest) * score_scale)
    scores = jnp.where(allowed[None], scores, masked_score)
    row_top = lax.optimization_barrier(jnp.max(scores, axis=-1, keepdims=True))
    weights = jnp.exp(scores - row_top)
    probabilities = weights / lax.optimization_barrier(jnp.sum(weights, axis=-1, keepdims=True))
    mixed = jnp.einsum('hqk,khd->qhd', low(probabilities), values, precision=highest)
    mixed = low(low_back(mixed)).reshape(row_count, D)
    after_attn = stream + low_back(dot_high(mixed, weight_out))
    normed_mlp = low(layer_norm(after_attn, gain_mlp))
    up_proj = low_back(dot_high(normed_mlp, weight_up))
    activated = low(jax.nn.gelu(up_proj, approximate=True))
    return after_attn + low_back(dot_high(activated, weight_down.T))

def reference(inputs, history, alpha_mid, alpha_last, attn_gains, mlp_gains, w_qkv, w_attn_out, w_up, w_down, doc_lengths, cotangent):
    group_rows = TOKENS // N_DP
    highest = lax.Precision.HIGHEST

    def forward(stream, earlier_all, mid_mix, last_mix, gains_attn, gains_mlp, qkv_all, out_all, up_all, down_all):
        streams = stream.reshape(N_DP, group_rows, D)
        earlier_groups = jnp.transpose(earlier_all.reshape(HIST, N_DP, group_rows, D), (1, 0, 2, 3))

        def one_group(pieces):
            group_in, earlier, lengths = pieces
            doc_ids, offsets = doc_layout(lengths, group_rows)
            cosine, sine = rotary_tables(offsets, HEAD)
            positions = jnp.arange(group_rows, dtype=jnp.int32)
            allowed = (doc_ids[:, None] == doc_ids[None, :]) & (positions[None, :] <= positions[:, None])
            block_mid = residual_block(group_in, gains_attn[0], gains_mlp[0], qkv_all[0], out_all[0], up_all[0], down_all[0], cosine, sine, allowed)
            mix_mid = jnp.einsum('k,ktd->td', mid_mix[:HIST], earlier, precision=highest) + mid_mix[HIST] * block_mid
            block_last = residual_block(mix_mid, gains_attn[1], gains_mlp[1], qkv_all[1], out_all[1], up_all[1], down_all[1], cosine, sine, allowed)
            return jnp.einsum('k,ktd->td', last_mix[:HIST], earlier, precision=highest) + last_mix[HIST] * block_mid + last_mix[HIST + 1] * block_last
        mixed_rows = lax.map(jax.checkpoint(one_group), (streams, earlier_groups, doc_lengths))
        return mixed_rows.reshape(TOKENS, D)
    primals = (inputs.astype(jnp.float32), history.astype(jnp.float32), alpha_mid, alpha_last, attn_gains, mlp_gains, w_qkv.astype(jnp.float32), w_attn_out.astype(jnp.float32), w_up.astype(jnp.float32), w_down.astype(jnp.float32))
    final, pullback = jax.vjp(forward, *primals)
    gradients = pullback(cotangent.astype(jnp.float32))
    return (final.astype(jnp.bfloat16), gradients[0], gradients[1].astype(jnp.bfloat16), gradients[2], gradients[3], gradients[4], gradients[5], gradients[6], gradients[7], gradients[8], gradients[9])
```

```python
import math
from functools import partial

import jax
import jax.numpy as jnp
from jax import lax
from jax.experimental import pallas as pl
from jax.experimental.pallas import tpu as pltpu
from jax.sharding import PartitionSpec as P

BF = jnp.bfloat16
F32 = jnp.float32
NN = (((1,), (0,)), ((), ()))
NT = (((1,), (1,)), ((), ()))
TN = (((0,), (0,)), ((), ()))
EPS = 1e-5
MASKED = -1e30
ROT_BASE = 10000.0
HEAD = 64
GELU_C = math.sqrt(2.0 / math.pi)

R = 256
T = 128
D = 768
HW = 384
FH = 1536
CH = 512
NCH = FH // CH
HIST = 12
LN_ROWS = 64

VMEM = pltpu.VMEM
V_SPEC = pl.BlockSpec(memory_space=pltpu.VMEM)
S_SPEC = pl.BlockSpec(memory_space=pltpu.SMEM)
H_SPEC = pl.BlockSpec(memory_space=pl.ANY)
LIMIT = 20 * 2**20


def dot(a, b, dims):
    return lax.dot_general(a, b, dims, preferred_element_type=F32)


def vm(shape, dtype):
    return pltpu.VMEM(shape, dtype)


def call(kernel, outs, ins, in_specs, scratch=(), us=2.0, name=None):
    many = isinstance(outs, (list, tuple))
    count = len(outs) if many else 1
    return pl.pallas_call(
        kernel,
        out_shape=outs,
        in_specs=in_specs,
        out_specs=[V_SPEC] * count if many else V_SPEC,
        scratch_shapes=list(scratch),
        compiler_params=pltpu.CompilerParams(vmem_limit_bytes=LIMIT),
        cost_estimate=pl.CostEstimate(
            flops=int(us * 8e8), bytes_accessed=int(us * 3e6), transcendentals=0
        ),
        name=name,
    )(*ins)


def normalized(v):
    mean = jnp.mean(v, axis=-1, keepdims=True)
    shifted = v - mean
    var = jnp.mean(shifted * shifted, axis=-1, keepdims=True)
    rstd = lax.rsqrt(var + EPS)
    return shifted * rstd, rstd


def norm_back(v, e, gain):
    n, rstd = normalized(v)
    q = e * gain
    back = (
        q - jnp.mean(q, axis=-1, keepdims=True) - n * jnp.mean(q * n, axis=-1, keepdims=True)
    ) * rstd
    return back, jnp.sum(e * n, axis=0, keepdims=True)


def swap_halves(x):
    lane = lax.broadcasted_iota(jnp.int32, x.shape, 1) % HEAD
    return jnp.where(lane < HEAD // 2, pltpu.roll(x, 128 - 32, 1), pltpu.roll(x, 32, 1))


def head_lanes(shape, head):
    lane = lax.broadcasted_iota(jnp.int32, shape, 1)
    return (lane >= HEAD * head) & (lane < HEAD * (head + 1))


def allowed_block(start_ref, half):
    rows, cols = T, T * (half + 1)
    t = lax.broadcasted_iota(jnp.int32, (rows, cols), 0) + T * half
    u = lax.broadcasted_iota(jnp.int32, (rows, cols), 1)
    first = start_ref[T * half : T * (half + 1), :]
    return (u >= first) & (u <= t)


def softmax_block(q, k, allowed):
    scores = jnp.where(allowed, dot(q, k, NT), MASKED)
    top = jnp.max(scores, axis=-1, keepdims=True)
    weights = jnp.exp(scores - top)
    return weights * (1.0 / jnp.sum(weights, axis=-1, keepdims=True))


def gelu_and_slope(v):
    square = v * v
    t = jnp.tanh(GELU_C * v * (1.0 + 0.044715 * square))
    half = 0.5 * (1.0 + t)
    slope = half + 0.5 * v * (1.0 - t * t) * (GELU_C * (1.0 + 3.0 * 0.044715 * square))
    return v * half, slope


def qkv_copies(core, layer, w_qkv, wq, sem):
    return [
        pltpu.make_async_copy(
            w_qkv.at[layer, :, pl.ds(pl.multiple_of(D * j + HW * core, 128), HW)],
            wq.at[:, pl.ds(HW * j, HW)],
            sem.at[j],
        )
        for j in range(3)
    ]


def ff_copies(core, layer, w, dst, sem, base):
    return [
        pltpu.make_async_copy(
            w.at[layer, :, pl.ds(pl.multiple_of(FH * core + CH * j, 128), CH)],
            dst.at[:, pl.ds(CH * j, CH)],
            sem.at[base + j],
        )
        for j in range(NCH)
    ]


def out_copies(core, layer, w_out, dst, sem, base):
    return [
        pltpu.make_async_copy(
            w_out.at[layer, pl.ds(pl.multiple_of(HW * part, 128), HW), :],
            dst.at[pl.ds(HW * j, HW), :],
            sem.at[base + j],
        )
        for j, part in enumerate((core, 1 - core))
    ]


def mix_kernel(am, al, history, mid, last):
    for r in range(0, T, 32):
        sl = slice(r, r + 32)
        acc_mid = jnp.zeros((32, D), F32)
        acc_last = jnp.zeros((32, D), F32)
        for k in range(HIST):
            h = history[k, sl, :].astype(F32)
            acc_mid += am[k] * h
            acc_last += al[k] * h
        mid[sl, :] = acc_mid
        last[sl, :] = acc_last


def attend_tail(core, layer, s_out, gain, w_qkv, cos, sin, start, normed, q, k, v, mixed, wq, sem, copies):
    g = gain[layer : layer + 1, :]
    for r in range(0, R, LN_ROWS):
        sl = slice(r, r + LN_ROWS)
        n, _ = normalized(s_out[sl, :])
        normed[sl, :] = (n * g).astype(BF)
    x = normed[...]
    for j, dst in enumerate((q, k, v)):
        copies[j].wait()
        for p in range(HW // 128):
            lanes = slice(128 * p, 128 * (p + 1))
            packed = dot(x, wq[:, HW * j + 128 * p : HW * j + 128 * (p + 1)], NN).astype(BF)
            if j == 2:
                dst[:, lanes] = packed
            else:
                f = packed.astype(F32)
                rot = f * cos[...] + swap_halves(f) * sin[...]
                if j == 0:
                    rot = rot * (1.0 / math.sqrt(HEAD))
                dst[:, lanes] = rot.astype(BF)
    for half in range(2):
        rows = slice(T * half, T * (half + 1))
        cols = slice(0, T * (half + 1))
        allowed = allowed_block(start, half)
        for p in range(HW // 128):
            lanes = slice(128 * p, 128 * (p + 1))
            qp = q[rows, lanes]
            kp = k[cols, lanes]
            vp = v[cols, lanes]
            acc = None
            for h in range(2):
                qh = jnp.where(head_lanes(qp.shape, h), qp, jnp.zeros_like(qp))
                vh = jnp.where(head_lanes(vp.shape, h), vp, jnp.zeros_like(vp))
                probs = softmax_block(qh, kp, allowed).astype(BF)
                part = dot(probs, vh, NN)
                acc = part if acc is None else acc + part
            mixed[rows, lanes] = acc.astype(BF)


def attend_first_kernel(cs, own, peer, gain, w_qkv, cos, sin, start, stream, normed, q, k, v, mixed, wq, sem):
    core = cs[0]
    copies = qkv_copies(core, 0, w_qkv, wq, sem)
    for cp in copies:
        cp.start()
    stream[pl.ds(pl.multiple_of(core * T, T), T), :] = own[...].astype(F32)
    stream[pl.ds(pl.multiple_of((1 - core) * T, T), T), :] = peer[...].astype(F32)
    attend_tail(core, 0, stream, gain, w_qkv, cos, sin, start, normed, q, k, v, mixed, wq, sem, copies)


def attend_second_kernel(cs, am, after, p_own, p_peer, h_own, h_peer, gain, w_qkv, cos, sin, start,
                         stream, block, normed, q, k, v, mixed, wq, sem):
    core = cs[0]
    copies = qkv_copies(core, 1, w_qkv, wq, sem)
    for cp in copies:
        cp.start()
    scale = am[HIST]
    stream[pl.ds(pl.multiple_of(core * T, T), T), :] = h_own[...]
    stream[pl.ds(pl.multiple_of((1 - core) * T, T), T), :] = h_peer[...]
    for r in range(0, R, LN_ROWS):
        sl = slice(r, r + LN_ROWS)
        b = after[sl, :] + (p_own[sl, :] + p_peer[sl, :])
        block[sl, :] = b
        stream[sl, :] = stream[sl, :] + scale * b
    attend_tail(core, 1, stream, gain, w_qkv, cos, sin, start, normed, q, k, v, mixed, wq, sem, copies)


def mlp_front(layer, stream, m_own, m_peer, gain, after, normed, wo, wo_copies):
    g = gain[layer : layer + 1, :]
    for cp in wo_copies:
        cp.wait()
    for r in range(0, R, 128):
        sl = slice(r, r + 128)
        a = stream[sl, :] + (
            dot(m_own[sl, :], wo[:HW, :], NN) + dot(m_peer[sl, :], wo[HW:, :], NN)
        )
        after[sl, :] = a
        n, _ = normalized(a)
        normed[sl, :] = (n * g).astype(BF)


def mlp_first_kernel(cs, stream, m_own, m_peer, gain, w_out, w_up, w_down,
                     after, normed, act, slope, part, wo, wu, wd, sem):
    core = cs[0]
    out_cp = out_copies(core, 0, w_out, wo, sem, 0)
    up_cp = ff_copies(core, 0, w_up, wu, sem, 2)
    down_cp = ff_copies(core, 0, w_down, wd, sem, 2 + NCH)
    for cp in out_cp + up_cp + down_cp:
        cp.start()
    mlp_front(0, stream, m_own, m_peer, gain, after, normed, wo, out_cp)
    x = normed[...]
    for j in range(NCH):
        up_cp[j].wait()
        for i in range(0, CH, 256):
            cols = slice(CH * j + i, CH * j + i + 256)
            u = dot(x, wu[:, cols], NN)
            a, s = gelu_and_slope(u)
            act[:, cols] = a.astype(BF)
            slope[:, cols] = s
    for cp in down_cp:
        cp.wait()
    part[...] = dot(act[...], wd[...], NT)


def mlp_last_kernel(cs, al, stream, m_own, m_peer, g_own, g_peer, gain, w_out, w_up, w_down,
                    after, normed, act, branch, gup, part, go, wo, wu, wd, sem):
    core = cs[0]
    out_cp = out_copies(core, 1, w_out, wo, sem, 0)
    up_cp = ff_copies(core, 1, w_up, wu, sem, 2)
    down_cp = ff_copies(core, 1, w_down, wd, sem, 2 + NCH)
    for cp in out_cp + up_cp + down_cp:
        cp.start()
    scale = al[HIST + 1]
    own_rows = pl.ds(pl.multiple_of(core * T, T), T)
    peer_rows = pl.ds(pl.multiple_of((1 - core) * T, T), T)
    go[own_rows, :] = scale * g_own[...].astype(F32)
    go[peer_rows, :] = scale * g_peer[...].astype(F32)
    branch[...] = go[...].astype(BF)
    mlp_front(1, stream, m_own, m_peer, gain, after, normed, wo, out_cp)
    x = normed[...]
    gb = branch[...]
    for j in range(NCH):
        up_cp[j].wait()
        down_cp[j].wait()
        for i in range(0, CH, 256):
            cols = slice(CH * j + i, CH * j + i + 256)
            u = dot(x, wu[:, cols], NN)
            a, s = gelu_and_slope(u)
            act[:, cols] = a.astype(BF)
            gup[:, cols] = (s * dot(gb, wd[:, cols], NN)).astype(BF)
    part[...] = dot(gup[...], wu[...], NT)


def down_kernel(cs, act, w_down, part, wd, sem):
    core = cs[0]
    cps = ff_copies(core, 1, w_down, wd, sem, 0)
    for cp in cps:
        cp.start()
    for cp in cps:
        cp.wait()
    part[...] = dot(act[...], wd[...], NT)


def attend_back_kernel(layer, cs, e_own, e_peer, go, after, gain, w_out, w_qkv, q, k, v, cos, sin, start,
                       grad_after, grad_attn, grad_packed, part, gain_grad, gm, acc, wo, wq, sem):
    core = cs[0]
    q_cp = qkv_copies(core, layer, w_qkv, wq, sem)
    o_cp = pltpu.make_async_copy(
        w_out.at[layer, pl.ds(pl.multiple_of(HW * core, 128), HW), :], wo, sem.at[3]
    )
    o_cp.start()
    for cp in q_cp:
        cp.start()
    g = gain[layer : layer + 1, :]
    total = jnp.zeros((1, D), F32)
    for r in range(0, R, LN_ROWS):
        sl = slice(r, r + LN_ROWS)
        back, piece = norm_back(after[sl, :], e_own[sl, :] + e_peer[sl, :], g)
        total += piece
        ga = go[sl, :] + back
        grad_after[sl, :] = ga
        grad_attn[sl, :] = ga.astype(BF)
    gain_grad[...] = total
    o_cp.wait()
    gm[...] = dot(grad_attn[...], wo[...], NT).astype(BF)
    scale = 1.0 / math.sqrt(HEAD)
    for p in range(HW // 128):
        lanes = slice(128 * p, 128 * (p + 1))
        for half in range(2):
            rows = slice(T * half, T * (half + 1))
            cols = slice(0, T * (half + 1))
            allowed = allowed_block(start, half)
            qp = q[rows, lanes]
            gp = gm[rows, lanes]
            kp = k[cols, lanes]
            vp = v[cols, lanes]
            dq = None
            for h in range(2):
                lane_q = head_lanes(qp.shape, h)
                qh = jnp.where(lane_q, qp, jnp.zeros_like(qp))
                gh = jnp.where(lane_q, gp, jnp.zeros_like(gp))
                kh = jnp.where(head_lanes(kp.shape, h), kp, jnp.zeros_like(kp))
                probs = softmax_block(qh, kp, allowed)
                dprob = dot(gh, vp, NT)
                center = jnp.sum(probs * dprob, axis=-1, keepdims=True)
                ds = (probs * (dprob - center)).astype(BF)
                dqh = dot(ds, kh, NN)
                dkh = dot(ds, qh, TN)
                dvh = dot(probs.astype(BF), gh, TN)
                dq = dqh if dq is None else dq + dqh
                if half == 0 and h == 0:
                    dk, dv = dkh, dvh
                elif half == 0:
                    dk, dv = dk + dkh, dv + dvh
                    acc[0, :T, :] = dk
                    acc[1, :T, :] = dv
                elif h == 0:
                    dk, dv = dkh, dvh
                else:
                    dk, dv = dk + dkh, dv + dvh
            dq = dq * scale
            rot = dq * cos[rows, :] - swap_halves(dq) * sin[rows, :]
            grad_packed[rows, lanes] = rot.astype(BF)
        for half in range(2):
            rows = slice(T * half, T * (half + 1))
            dkr, dvr = dk[rows, :], dv[rows, :]
            if half == 0:
                dkr = dkr + acc[0, :T, :]
                dvr = dvr + acc[1, :T, :]
            rot = dkr * cos[rows, :] - swap_halves(dkr) * sin[rows, :]
            grad_packed[rows, HW + 128 * p : HW + 128 * (p + 1)] = rot.astype(BF)
            grad_packed[rows, 2 * HW + 128 * p : 2 * HW + 128 * (p + 1)] = dvr.astype(BF)
    for cp in q_cp:
        cp.wait()
    part[...] = dot(grad_packed[...], wq[...], NT)


def mlp_back_kernel(cs, am, al, e_own, e_peer, grad_after, stream, gain, g_own, g_peer, slope, w_up, w_down,
                    grad_mix, go, branch, gup, part, gain_grad, wu, wd, sem):
    core = cs[0]
    down_cp = ff_copies(core, 0, w_down, wd, sem, 0)
    up_cp = ff_copies(core, 0, w_up, wu, sem, NCH)
    for cp in down_cp + up_cp:
        cp.start()
    a_last = al[HIST]
    a_mid = am[HIST]
    go[pl.ds(pl.multiple_of(core * T, T), T), :] = a_last * g_own[...].astype(F32)
    go[pl.ds(pl.multiple_of((1 - core) * T, T), T), :] = a_last * g_peer[...].astype(F32)
    g = gain[1:2, :]
    total = jnp.zeros((1, D), F32)
    for r in range(0, R, LN_ROWS):
        sl = slice(r, r + LN_ROWS)
        back, piece = norm_back(stream[sl, :], e_own[sl, :] + e_peer[sl, :], g)
        total += piece
        gx = grad_after[sl, :] + back
        grad_mix[sl, :] = gx
        out = go[sl, :] + a_mid * gx
        go[sl, :] = out
        branch[sl, :] = out.astype(BF)
    gain_grad[...] = total
    gb = branch[...]
    for j in range(NCH):
        down_cp[j].wait()
        for i in range(0, CH, 256):
            cols = slice(CH * j + i, CH * j + i + 256)
            gup[:, cols] = (slope[:, cols] * dot(gb, wd[:, cols], NN)).astype(BF)
    for cp in up_cp:
        cp.wait()
    part[...] = dot(gup[...], wu[...], NT)


def down_grad_kernel(branch, act, out):
    out[...] = dot(branch[...], act[...], TN).astype(BF)


def up_grad_kernel(normed, order, gup, out):
    x = dot(normed[...], order[...], NN).astype(BF)
    out[...] = dot(x, gup[...], TN).astype(BF)


def attn_grad_kernel(cs, normed, grad_packed, m_own, m_peer, grad_attn, out):
    core = cs[0]
    out[:, : 3 * HW] = dot(normed[...], grad_packed[...], TN).astype(BF)
    ga = grad_attn[:, pl.ds(pl.multiple_of(HW * core, 128), HW)]
    out[pl.ds(pl.multiple_of(HW * core, 128), HW), 3 * HW :] = dot(m_own[...], ga, TN).astype(BF)
    out[pl.ds(pl.multiple_of(HW * (1 - core), 128), HW), 3 * HW :] = dot(m_peer[...], ga, TN).astype(BF)


def input_grad_kernel(cs, e_part, e_peer, grad_after, own, gain, out, gain_grad):
    core = cs[0]
    rows = pl.ds(pl.multiple_of(core * T, T), T)
    back, piece = norm_back(own[...].astype(F32), e_part[rows, :] + e_peer[...], gain[0:1, :])
    out[...] = grad_after[rows, :] + back
    gain_grad[...] = piece


def final_kernel(cs, al, h_last, block, after, p_own, p_peer, g_own, out, sums):
    core = cs[0]
    rows = pl.ds(pl.multiple_of(core * T, T), T)
    b_mid = block[rows, :]
    b_last = after[rows, :] + (p_own[rows, :] + p_peer[...])
    out[...] = (h_last[...] + al[HIST] * b_mid + al[HIST + 1] * b_last).astype(BF)
    g = g_own[...].astype(F32)
    sums[0:1, :] = jnp.sum(g * b_mid, axis=0, keepdims=True)
    sums[1:2, :] = jnp.sum(g * b_last, axis=0, keepdims=True)


def history_kernel(cs, am, al, history, g_own, grad_mix, block, out, sums):
    k = pl.program_id(0)
    core = cs[0]
    rows = pl.ds(pl.multiple_of(core * T, T), T)
    gm = grad_mix[rows, :]
    g = g_own[...].astype(F32)
    out[0] = (al[k] * g + am[k] * gm).astype(BF)
    h = history[0].astype(F32)
    sums[0, 0:1, :] = jnp.sum(h * gm, axis=0, keepdims=True)
    sums[0, 1:2, :] = jnp.sum(h * g, axis=0, keepdims=True)
    sums[0, 2:3, :] = jnp.sum(block[rows, :] * gm, axis=0, keepdims=True)


def vector_kernel(h_sums, f_sums, ga0, ga1, gm0, gm1, out):
    for j in range(D // 128):
        lanes = slice(128 * j, 128 * (j + 1))
        out[4 * j : 4 * j + 1, :] = ga0[:, lanes]
        out[4 * j + 1 : 4 * j + 2, :] = 0.5 * ga1[:, lanes]
        out[4 * j + 2 : 4 * j + 3, :] = 0.5 * gm0[:, lanes]
        out[4 * j + 3 : 4 * j + 4, :] = 0.5 * gm1[:, lanes]
    for k in range(HIST):
        out[24 + k : 25 + k, :] = jnp.broadcast_to(
            jnp.sum(h_sums[k, 0:1, :], axis=-1, keepdims=True), (1, 128)
        )
        out[37 + k : 38 + k, :] = jnp.broadcast_to(
            jnp.sum(h_sums[k, 1:2, :], axis=-1, keepdims=True), (1, 128)
        )
    out[36:37, :] = jnp.broadcast_to(jnp.sum(h_sums[0, 2:3, :], axis=-1, keepdims=True), (1, 128))
    out[49:51, :] = jnp.broadcast_to(jnp.sum(f_sums[...], axis=-1, keepdims=True), (2, 128))
    out[51:56, :] = jnp.zeros((5, 128), F32)


def coords(i):
    return [i // 16, (i // 4) % 4, i % 4]


def partner_pairs(axis, step):
    pairs = []
    for chip in range(64):
        for core in range(2):
            flip = (1, 3)[(step + core) % 2]
            there = coords(chip)
            there[axis] ^= flip
            pairs.append((2 * chip + core, 2 * (there[0] * 16 + there[1] * 4 + there[2]) + core))
    return pairs


def trade(x, axis, step):
    return lax.ppermute(x, ("dp", "seq"), partner_pairs(axis, step))


def chip_place():
    chip = lax.axis_index("dp")
    return (chip // 16, (chip // 4) % 4, chip % 4)


def scatter_axis(pieces, axis, core, last):
    place = chip_place()[axis]
    near = jnp.where(core == 0, 1, 3)
    far = jnp.where(core == 0, 3, 1)
    keep = pieces(place)
    second = pieces(place ^ far)
    got = trade(jnp.stack([pieces(place ^ near), pieces(place ^ 2)]), axis, 0)
    other = (second.astype(F32) + got[1].astype(F32)).astype(BF)
    got2 = trade(other, axis, 1)
    total = keep.astype(F32) + got[0].astype(F32) + got2.astype(F32)
    return total if last else total.astype(BF)


def scatter_part(part, axes, core):
    width = part.shape[1]
    if axes[0] == 1:
        view = part.reshape(4, 4, 48, width)
        cur = scatter_axis(lambda i: lax.dynamic_index_in_dim(view, i, 1, keepdims=False), 1, core, False)
        cur = cur.reshape(192, width)
    else:
        view = part.reshape(4, 192, width)
        cur = scatter_axis(lambda i: lax.dynamic_index_in_dim(view, i, 0, keepdims=False), axes[0], core, False)
    mid = cur.reshape(4, 48, width)
    cur = scatter_axis(lambda i: lax.dynamic_index_in_dim(mid, i, 0, keepdims=False), axes[1], core, False)
    low = cur.reshape(4, 12, width)
    return scatter_axis(lambda i: lax.dynamic_index_in_dim(low, i, 0, keepdims=False), axes[2], core, True)


def sum_everywhere(vec):
    for axis in range(3):
        for step in range(2):
            vec = vec + trade(vec, axis, step)
    return vec + other_core(vec)


def other_core(x):
    return lax.ppermute(x, "seq", [(0, 1), (1, 0)])


def finish_block(down, up, attn, core):
    mine = jnp.concatenate([down, up, attn], axis=1).reshape(2, 6, 2 * FH + 4 * HW)
    own = lax.dynamic_index_in_dim(mine, core, 0, keepdims=False)
    got = other_core(lax.dynamic_index_in_dim(mine, 1 - core, 0, keepdims=False))
    first = jnp.where(core == 0, own, got)
    second = jnp.where(core == 0, got, own)

    def join(lo, width):
        return jnp.concatenate([first[:, lo : lo + width], second[:, lo : lo + width]], axis=1)

    base = 2 * FH
    qkv = jnp.concatenate([join(base + HW * j, HW) for j in range(3)], axis=1)
    return (qkv, join(base + 3 * HW, HW), join(FH, FH), join(0, FH))


def row_order():
    r = jnp.arange(D, dtype=jnp.int32)
    z, y, x, i = r // 192, (r // 48) % 4, (r // 12) % 4, r % 12
    source = 12 * (16 * y + 4 * x + z) + i
    return (jnp.arange(D, dtype=jnp.int32)[:, None] == source[None, :]).astype(BF)


def position_tables(lengths):
    ends = jnp.cumsum(lengths)
    places = jnp.arange(R, dtype=jnp.int32)
    starts = ends - lengths
    begun = places[:, None] >= starts[None, :]
    first = jnp.max(jnp.where(begun, starts[None, :], 0), axis=1)
    offset = (places - first).astype(F32)
    lane = jnp.arange(128, dtype=jnp.int32) % HEAD
    freq = jnp.exp(-math.log(ROT_BASE) * 2.0 * (lane % 32).astype(F32) / HEAD)
    angles = offset[:, None] * freq[None, :]
    sign = jnp.where(lane < 32, -1.0, 1.0)
    return first[:, None], jnp.cos(angles), jnp.sin(angles) * sign[None, :]


def shards(inputs, history, alpha_mid, alpha_last, attn_gains, mlp_gains, w_qkv, w_out, w_up, w_down,
           doc_lengths, cotangent):
    core = lax.axis_index("seq")
    cs = jnp.reshape(core, (1,)).astype(jnp.int32)
    w_qkv, w_out, w_up, w_down = (
        pltpu.with_memory_space_constraint(w, pltpu.HBM) for w in (w_qkv, w_out, w_up, w_down)
    )
    start, cos, sin = position_tables(doc_lengths[0])
    order = row_order()
    in_peer = other_core(inputs)
    g_peer = other_core(cotangent)
    h_mid, h_last = call(
        mix_kernel, [vm((T, D), F32)] * 2, (alpha_mid, alpha_last, history), [S_SPEC, S_SPEC, V_SPEC],
        us=2.0, name="mix_history",
    )
    h_peer = other_core(h_mid)

    dma = pltpu.SemaphoreType.DMA
    att_out = [vm((R, D), BF)] + [vm((R, HW), BF)] * 4
    att_scratch = [VMEM((D, 3 * HW), BF), dma((3,))]
    stream0, normed0, q0, k0, v0, m0 = call(
        attend_first_kernel, [vm((R, D), F32)] + att_out,
        (cs, inputs, in_peer, attn_gains, w_qkv, cos, sin, start),
        [S_SPEC, V_SPEC, V_SPEC, V_SPEC, H_SPEC, V_SPEC, V_SPEC, V_SPEC], att_scratch, us=4.0,
        name="attend_first",
    )
    m0p = other_core(m0)
    mlp_scratch = [VMEM((D, D), BF), VMEM((D, FH), BF), VMEM((D, FH), BF), dma((2 + 2 * NCH,))]
    after0, nm0, act0, slope0, part0 = call(
        mlp_first_kernel,
        [vm((R, D), F32), vm((R, D), BF), vm((R, FH), BF), vm((R, FH), F32), vm((R, D), F32)],
        (cs, stream0, m0, m0p, mlp_gains, w_out, w_up, w_down),
        [S_SPEC, V_SPEC, V_SPEC, V_SPEC, V_SPEC, H_SPEC, H_SPEC, H_SPEC], mlp_scratch, us=4.0,
        name="mlp_first",
    )
    part0p = other_core(part0)
    stream1, block0, normed1, q1, k1, v1, m1 = call(
        attend_second_kernel, [vm((R, D), F32)] * 2 + att_out,
        (cs, alpha_mid, after0, part0, part0p, h_mid, h_peer, attn_gains, w_qkv, cos, sin, start),
        [S_SPEC, S_SPEC] + [V_SPEC] * 6 + [H_SPEC] + [V_SPEC] * 3, att_scratch, us=4.0,
        name="attend_second",
    )
    m1p = other_core(m1)
    after1, nm1, act1, branch1, gup1, e1, go1 = call(
        mlp_last_kernel,
        [vm((R, D), F32), vm((R, D), BF), vm((R, FH), BF), vm((R, D), BF), vm((R, FH), BF), vm((R, D), F32),
         vm((R, D), F32)],
        (cs, alpha_last, stream1, m1, m1p, cotangent, g_peer, mlp_gains, w_out, w_up, w_down),
        [S_SPEC, S_SPEC] + [V_SPEC] * 6 + [H_SPEC] * 3, mlp_scratch, us=5.0, name="mlp_last",
    )
    e1p = other_core(e1)

    def weight_grads(branch, act, nm, gup):
        down = call(down_grad_kernel, vm((D, FH), BF), (branch, act), [V_SPEC] * 2, us=1.0, name="down_grad")
        up = call(up_grad_kernel, vm((D, FH), BF), (nm, order, gup), [V_SPEC] * 3, us=1.2, name="up_grad")
        return scatter_part(down, (0, 1, 2), core), scatter_part(up, (2, 0, 1), core)

    def attn_back(layer, e, ep, go, after, q, k, v):
        return call(
            partial(attend_back_kernel, layer),
            [vm((R, D), F32), vm((R, D), BF), vm((R, 3 * HW), BF), vm((R, D), F32), vm((1, D), F32)],
            (cs, e, ep, go, after, mlp_gains, w_out, w_qkv, q, k, v, cos, sin, start),
            [S_SPEC] + [V_SPEC] * 5 + [H_SPEC] * 2 + [V_SPEC] * 6,
            [VMEM((R, HW), BF), VMEM((2, T, 128), F32), VMEM((HW, D), BF), VMEM((D, 3 * HW), BF), dma((4,))],
            us=5.0, name="attend_back",
        )

    def attn_grads(normed, packed, m, mp, ga):
        grad = call(
            attn_grad_kernel, vm((D, FH), BF), (cs, normed, packed, m, mp, ga), [S_SPEC] + [V_SPEC] * 5,
            us=1.0, name="attn_grad",
        )
        return scatter_part(grad, (1, 0, 2), core)

    down1, up1 = weight_grads(branch1, act1, nm1, gup1)
    ga1, gb1, packed1, x1, gain_mlp1 = attn_back(1, e1, e1p, go1, after1, q1, k1, v1)
    x1p = other_core(x1)
    attn1 = attn_grads(normed1, packed1, m1, m1p, gb1)

    grad_mix, go0, branch0, gup0, e0, gain_attn1 = call(
        mlp_back_kernel,
        [vm((R, D), F32), vm((R, D), F32), vm((R, D), BF), vm((R, FH), BF), vm((R, D), F32), vm((1, D), F32)],
        (cs, alpha_mid, alpha_last, x1, x1p, ga1, stream1, attn_gains, cotangent, g_peer, slope0, w_up, w_down),
        [S_SPEC] * 3 + [V_SPEC] * 8 + [H_SPEC] * 2,
        [VMEM((D, FH), BF), VMEM((D, FH), BF), dma((2 * NCH,))], us=4.0, name="mlp_back",
    )
    e0p = other_core(e0)
    down0, up0 = weight_grads(branch0, act0, nm0, gup0)
    ga0, gb0, packed0, x0, gain_mlp0 = attn_back(0, e0, e0p, go0, after0, q0, k0, v0)
    x0p = other_core(lax.dynamic_slice_in_dim(x0, (1 - core) * T, T, 0))
    attn0 = attn_grads(normed0, packed0, m0, m0p, gb0)

    input_grad, gain_attn0 = call(
        input_grad_kernel, [jax.ShapeDtypeStruct((T, D), F32), vm((1, D), F32)],
        (cs, x0, x0p, ga0, inputs, attn_gains), [S_SPEC] + [V_SPEC] * 5, us=1.0, name="input_grad",
    )

    part1 = call(
        down_kernel, vm((R, D), F32), (cs, act1, w_down), [S_SPEC, V_SPEC, H_SPEC],
        [VMEM((D, FH), BF), dma((NCH,))], us=2.0, name="down_last",
    )
    part1p = other_core(lax.dynamic_slice_in_dim(part1, (1 - core) * T, T, 0))
    final, f_sums = call(
        final_kernel, [jax.ShapeDtypeStruct((T, D), BF), vm((2, D), F32)],
        (cs, alpha_last, h_last, block0, after1, part1, part1p, cotangent),
        [S_SPEC] * 2 + [V_SPEC] * 6, us=1.0, name="final_mix",
    )
    whole = lambda *shape: pl.BlockSpec(shape, lambda i: (0,) * len(shape))
    history_grad, h_sums = pl.pallas_call(
        history_kernel,
        grid=(HIST,),
        out_shape=[jax.ShapeDtypeStruct((HIST, T, D), BF), jax.ShapeDtypeStruct((HIST, 3, D), F32)],
        in_specs=[S_SPEC] * 3
        + [pl.BlockSpec((1, T, D), lambda i: (i, 0, 0)), whole(T, D), whole(R, D), whole(R, D)],
        out_specs=[pl.BlockSpec((1, T, D), lambda i: (i, 0, 0)), pl.BlockSpec((1, 3, D), lambda i: (i, 0, 0))],
        compiler_params=pltpu.CompilerParams(vmem_limit_bytes=LIMIT),
        cost_estimate=pl.CostEstimate(flops=int(2e9), bytes_accessed=int(5e6), transcendentals=0),
        name="history_grad",
    )(cs, alpha_mid, alpha_last, history, cotangent, grad_mix, block0)
    vec = call(
        vector_kernel, vm((56, 128), F32), (h_sums, f_sums, gain_attn0, gain_attn1, gain_mlp0, gain_mlp1),
        [V_SPEC] * 6, us=0.5, name="pack_sums",
    )
    vec = sum_everywhere(vec)
    gains = vec[:24].reshape(6, 4, 128).transpose(1, 0, 2).reshape(4, D)

    blocks = (finish_block(down0, up0, attn0, core), finish_block(down1, up1, attn1, core))
    qkv_grad, out_grad, up_grad, down_grad = (jnp.stack([a, b]) for a, b in zip(*blocks))
    return (
        final,
        input_grad,
        history_grad,
        vec[24:37, 0],
        vec[37:51, 0],
        gains[:2],
        gains[2:],
        qkv_grad,
        out_grad,
        up_grad,
        down_grad,
    )


def solution(mesh):
    both = P(("dp", "seq"), None)
    spread = P(None, ("dp", "seq"), None)
    return jax.shard_map(
        shards,
        mesh=mesh,
        in_specs=(both, spread) + (P(),) * 8 + (P("dp", None), both),
        out_specs=(both, both, spread) + (P(),) * 4 + (spread,) * 4,
        check_vma=False,
    )
```

```python
import math
from functools import partial

import jax
import jax.numpy as jnp
from jax import lax
from jax.experimental import pallas as pl
from jax.experimental.pallas import tpu as pltpu
from jax.sharding import PartitionSpec as P

BF = jnp.bfloat16
F32 = jnp.float32
NN = (((1,), (0,)), ((), ()))
NT = (((1,), (1,)), ((), ()))
TN = (((0,), (0,)), ((), ()))
EPS = 1e-5
MASKED = -1e30
ROT_BASE = 10000.0
HEAD = 64
GELU_C = math.sqrt(2.0 / math.pi)

R = 256
T = 128
D = 768
HW = 384
FH = 1536
CH = 512
THIRD = FH // 3
NCH = FH // CH
HIST = 12
LN_ROWS = 64

VMEM = pltpu.VMEM
V_SPEC = pl.BlockSpec(memory_space=pltpu.VMEM)
S_SPEC = pl.BlockSpec(memory_space=pltpu.SMEM)
H_SPEC = pl.BlockSpec(memory_space=pl.ANY)
COSTS = {
    "attend_first": 2.0, "mlp_first": 2.0, "attend_second": 2.0, "mlp_last": 2.0, "attend_back": 8.0, "mlp_back": 3.0,
    "up_grad": 1.0, "down_grad": 1.0, "attn_grad": 1.0, "attn_thirds": 1.0,
    "near_first": 0.3, "near_sum": 0.3, "axis_total": 0.3, "second_axis": 0.3, "third_axis": 0.3, "last_sum": 0.3,
}
SPARE = 6 * 2**20


def dot(a, b, dims):
    return lax.dot_general(a, b, dims, preferred_element_type=F32)


def vm(shape, dtype):
    return pltpu.VMEM(shape, dtype)


class Order:
    def __init__(self):
        self.token = None
        self.held = []

    def hold(self, *arrays):
        self.held += arrays

    def drop(self, *arrays):
        self.held = [x for x in self.held if not any(x is y for y in arrays)]

    def call(self, kernel, outs, ins, in_specs, scratch=(), name=None, out_specs=None, after=()):
        many = isinstance(outs, (list, tuple))
        shapes = list(outs) if many else [outs]
        ins, in_specs = list(ins), list(in_specs)
        count = len(ins)
        after = list(after) + ([] if self.token is None else [self.token])
        in_specs += [H_SPEC] * len(after)
        kept = [x for x in self.held if not any(x is y for y in ins)]
        ins += after + kept
        in_specs += [V_SPEC] * len(kept)
        total = len(ins)
        ins = [pltpu.with_memory_space_constraint(x, VMEM) if spec is V_SPEC else x for x, spec in zip(ins, in_specs)]

        def body(*refs):
            kernel(*refs[:count], *refs[total:])

        held = sum(
            math.prod(x.shape) * jnp.dtype(x.dtype).itemsize for x in scratch if x.memory_space == VMEM
        )
        result = pl.pallas_call(
            body,
            out_shape=shapes,
            in_specs=in_specs,
            out_specs=out_specs or [V_SPEC] * len(shapes),
            scratch_shapes=list(scratch),
            compiler_params=pltpu.CompilerParams(vmem_limit_bytes=SPARE + held),
            cost_estimate=pl.CostEstimate(flops=int(1e9 * COSTS.get(name, 0.01)), bytes_accessed=1000, transcendentals=0),
            name=name,
        )(*ins)
        sizes = [math.prod(shape.shape) for shape in shapes]
        self.token = result[sizes.index(min(sizes))]
        return result if many else result[0]


def normalized(v):
    mean = jnp.mean(v, axis=-1, keepdims=True)
    shifted = v - mean
    var = jnp.mean(shifted * shifted, axis=-1, keepdims=True)
    rstd = lax.rsqrt(var + EPS)
    return shifted * rstd, rstd


def norm_back(v, e, gain):
    n, rstd = normalized(v)
    q = e * gain
    back = (
        q - jnp.mean(q, axis=-1, keepdims=True) - n * jnp.mean(q * n, axis=-1, keepdims=True)
    ) * rstd
    return back, jnp.sum(e * n, axis=0, keepdims=True)


def swap_halves(x):
    lane = lax.broadcasted_iota(jnp.int32, x.shape, 1) % HEAD
    return jnp.where(lane < HEAD // 2, pltpu.roll(x, 128 - 32, 1), pltpu.roll(x, 32, 1))


def head_lanes(shape, head):
    lane = lax.broadcasted_iota(jnp.int32, shape, 1)
    return (lane >= HEAD * head) & (lane < HEAD * (head + 1))


def first_place(lengths, t):
    second = lengths[0, 0]
    third = second + lengths[0, 1]
    return jnp.where(t >= third, third, jnp.where(t >= second, second, 0))


def allowed_block(lengths, half):
    shape = (T, T * (half + 1))
    t = lax.broadcasted_iota(jnp.int32, shape, 0) + T * half
    u = lax.broadcasted_iota(jnp.int32, shape, 1)
    first = first_place(lengths, lax.broadcasted_iota(jnp.int32, (T, 1), 0) + T * half)
    return (u >= first) & (u <= t)


def write_tables(lengths, cos, sin):
    t = lax.broadcasted_iota(jnp.int32, (R, 1), 0)
    offset = (t - first_place(lengths, t)).astype(F32)
    lane = lax.broadcasted_iota(jnp.int32, (1, 128), 1) % HEAD
    freq = jnp.exp((-math.log(ROT_BASE) * 2.0 / HEAD) * (lane % 32).astype(F32))
    angles = offset * freq
    cos[...] = jnp.cos(angles)
    sin[...] = jnp.sin(angles) * jnp.where(lane < 32, -1.0, 1.0)


def softmax_block(q, k, allowed):
    scores = jnp.where(allowed, dot(q, k, NT), MASKED)
    top = jnp.max(scores, axis=-1, keepdims=True)
    weights = jnp.exp(scores - top)
    return weights * (1.0 / jnp.sum(weights, axis=-1, keepdims=True))


def gelu_and_slope(v):
    square = v * v
    t = jnp.tanh(GELU_C * v * (1.0 + 0.044715 * square))
    half = 0.5 * (1.0 + t)
    slope = half + 0.5 * v * (1.0 - t * t) * (GELU_C * (1.0 + 3.0 * 0.044715 * square))
    return v * half, slope


def qkv_copies(core, layer, w_qkv, wq, sem):
    return [
        pltpu.make_async_copy(
            w_qkv.at[layer, :, pl.ds(pl.multiple_of(D * j + HW * core, 128), HW)],
            wq.at[:, pl.ds(HW * j, HW)],
            sem.at[j],
        )
        for j in range(3)
    ]


def ff_copies(core, layer, w, dst, sem, base):
    return [
        pltpu.make_async_copy(
            w.at[layer, :, pl.ds(pl.multiple_of(FH * core + CH * j, 128), CH)],
            dst.at[:, pl.ds(CH * j, CH)],
            sem.at[base + j],
        )
        for j in range(NCH)
    ]


def out_copies(core, layer, w_out, dst, sem, base):
    return [
        pltpu.make_async_copy(
            w_out.at[layer, pl.ds(pl.multiple_of(HW * part, 128), HW), :],
            dst.at[pl.ds(HW * j, HW), :],
            sem.at[base + j],
        )
        for j, part in enumerate((core, 1 - core))
    ]


def mix_kernel(am, al, history, mid, last, held, sem):
    copies = [pltpu.make_async_copy(history.at[k], held.at[k], sem.at[k]) for k in range(HIST)]
    for cp in copies:
        cp.start()
    for k in range(HIST):
        copies[k].wait()
        for r in range(0, T, 32):
            sl = slice(r, r + 32)
            h = held[k, sl, :].astype(F32)
            if k == 0:
                mid[sl, :] = am[k] * h
                last[sl, :] = al[k] * h
            else:
                mid[sl, :] += am[k] * h
                last[sl, :] += al[k] * h


def attend_tail(core, layer, s_out, gain, w_qkv, cos, sin, lengths, normed, q, k, v, mixed, wq, sem, copies):
    g = gain[layer : layer + 1, :]
    for r in range(0, R, LN_ROWS):
        sl = slice(r, r + LN_ROWS)
        n, _ = normalized(s_out[sl, :])
        normed[sl, :] = (n * g).astype(BF)
    x = normed[...]
    for j, dst in enumerate((q, k, v)):
        copies[j].wait()
        for p in range(HW // 128):
            lanes = slice(128 * p, 128 * (p + 1))
            packed = dot(x, wq[:, HW * j + 128 * p : HW * j + 128 * (p + 1)], NN).astype(BF)
            if j == 2:
                dst[:, lanes] = packed
            else:
                f = packed.astype(F32)
                rot = f * cos[...] + swap_halves(f) * sin[...]
                if j == 0:
                    rot = rot * (1.0 / math.sqrt(HEAD))
                dst[:, lanes] = rot.astype(BF)
    for half in range(2):
        rows = slice(T * half, T * (half + 1))
        cols = slice(0, T * (half + 1))
        allowed = allowed_block(lengths, half)
        for p in range(HW // 128):
            lanes = slice(128 * p, 128 * (p + 1))
            qp = q[rows, lanes]
            kp = k[cols, lanes]
            vp = v[cols, lanes]
            acc = None
            for h in range(2):
                qh = jnp.where(head_lanes(qp.shape, h), qp, jnp.zeros_like(qp))
                vh = jnp.where(head_lanes(vp.shape, h), vp, jnp.zeros_like(vp))
                probs = softmax_block(qh, kp, allowed).astype(BF)
                part = dot(probs, vh, NN)
                acc = part if acc is None else acc + part
            mixed[rows, lanes] = acc.astype(BF)


def attend_first_kernel(place, lengths, inputs, peer, gains, w_qkv, stream, normed, q, k, v, mixed, cos, sin,
                        own, gain, wq, sem):
    core = place[0]
    first = [pltpu.make_async_copy(inputs, own, sem.at[3]), pltpu.make_async_copy(gains, gain, sem.at[4])]
    copies = qkv_copies(core, 0, w_qkv, wq, sem)
    for cp in first + copies:
        cp.start()
    write_tables(lengths, cos, sin)
    for cp in first:
        cp.wait()
    stream[pl.ds(pl.multiple_of(core * T, T), T), :] = own[...].astype(F32)
    stream[pl.ds(pl.multiple_of((1 - core) * T, T), T), :] = peer[...].astype(F32)
    attend_tail(core, 0, stream, gain, w_qkv, cos, sin, lengths, normed, q, k, v, mixed, wq, sem, copies)


def attend_second_kernel(place, am, after, p_own, p_peer, h_own, h_peer, gain, w_qkv, cos, sin, lengths,
                         stream, block, normed, q, k, v, mixed, wq, sem):
    core = place[0]
    copies = qkv_copies(core, 1, w_qkv, wq, sem)
    for cp in copies:
        cp.start()
    scale = am[HIST]
    stream[pl.ds(pl.multiple_of(core * T, T), T), :] = h_own[...]
    stream[pl.ds(pl.multiple_of((1 - core) * T, T), T), :] = h_peer[...]
    for r in range(0, R, LN_ROWS):
        sl = slice(r, r + LN_ROWS)
        b = after[sl, :] + (p_own[sl, :] + p_peer[sl, :].astype(F32))
        block[sl, :] = b
        stream[sl, :] = stream[sl, :] + scale * b
    attend_tail(core, 1, stream, gain, w_qkv, cos, sin, lengths, normed, q, k, v, mixed, wq, sem, copies)


def mlp_front(layer, stream, m_own, m_peer, gain, after, normed, wo, wo_copies):
    g = gain[layer : layer + 1, :]
    for cp in wo_copies:
        cp.wait()
    for r in range(0, R, 128):
        sl = slice(r, r + 128)
        a = stream[sl, :] + (
            dot(m_own[sl, :], wo[:HW, :], NN) + dot(m_peer[sl, :], wo[HW:, :], NN)
        )
        after[sl, :] = a
        n, _ = normalized(a)
        normed[sl, :] = (n * g).astype(BF)


def mlp_first_kernel(place, stream, m_own, m_peer, gain, w_out, w_up, w_down,
                     after, normed, act, slope, part, sent, wo, wu, wd, sem):
    core = place[0]
    out_cp = out_copies(core, 0, w_out, wo, sem, 0)
    up_cp = ff_copies(core, 0, w_up, wu, sem, 2)
    down_cp = ff_copies(core, 0, w_down, wd, sem, 2 + NCH)
    for cp in out_cp + up_cp + down_cp:
        cp.start()
    mlp_front(0, stream, m_own, m_peer, gain, after, normed, wo, out_cp)
    x = normed[...]
    for j in range(NCH):
        up_cp[j].wait()
        for i in range(0, CH, 256):
            cols = slice(CH * j + i, CH * j + i + 256)
            u = dot(x, wu[:, cols], NN)
            a, s = gelu_and_slope(u)
            act[:, cols] = a.astype(BF)
            slope[:, cols] = s
    for cp in down_cp:
        cp.wait()
    total = dot(act[...], wd[...], NT)
    part[...] = total
    sent[...] = total.astype(BF)


def mlp_last_kernel(place, al, stream, m_own, m_peer, g_own, g_peer, gain, w_out, w_up, w_down,
                    after, normed, act, branch, gup, part, sent, go, wo, wu, wd, sem):
    core = place[0]
    out_cp = out_copies(core, 1, w_out, wo, sem, 0)
    up_cp = ff_copies(core, 1, w_up, wu, sem, 2)
    down_cp = ff_copies(core, 1, w_down, wd, sem, 2 + NCH)
    for cp in out_cp + up_cp + down_cp:
        cp.start()
    scale = al[HIST + 1]
    own_rows = pl.ds(pl.multiple_of(core * T, T), T)
    peer_rows = pl.ds(pl.multiple_of((1 - core) * T, T), T)
    go[own_rows, :] = scale * g_own[...].astype(F32)
    go[peer_rows, :] = scale * g_peer[...].astype(F32)
    branch[...] = go[...].astype(BF)
    mlp_front(1, stream, m_own, m_peer, gain, after, normed, wo, out_cp)
    x = normed[...]
    gb = branch[...]
    for j in range(NCH):
        up_cp[j].wait()
        down_cp[j].wait()
        for i in range(0, CH, 256):
            cols = slice(CH * j + i, CH * j + i + 256)
            u = dot(x, wu[:, cols], NN)
            a, s = gelu_and_slope(u)
            act[:, cols] = a.astype(BF)
            gup[:, cols] = (s * dot(gb, wd[:, cols], NN)).astype(BF)
    total = dot(gup[...], wu[...], NT)
    part[...] = total
    sent[...] = total.astype(BF)


def down_kernel(place, act, w_down, part, sent, wd, sem):
    core = place[0]
    cps = ff_copies(core, 1, w_down, wd, sem, 0)
    for cp in cps:
        cp.start()
    for cp in cps:
        cp.wait()
    part[...] = dot(act[...], wd[...], NT)
    sent[...] = part[pl.ds(pl.multiple_of((1 - core) * T, T), T), :].astype(BF)


def attend_back_kernel(layer, place, e_own, e_peer, go, after, gain, w_out, w_qkv, q, k, v, cos, sin, lengths,
                       grad_after, grad_attn, grad_packed, part, sent, gain_grad, gm, acc, wo, wq, sem):
    core = place[0]
    q_cp = qkv_copies(core, layer, w_qkv, wq, sem)
    o_cp = pltpu.make_async_copy(
        w_out.at[layer, pl.ds(pl.multiple_of(HW * core, 128), HW), :], wo, sem.at[3]
    )
    o_cp.start()
    for cp in q_cp:
        cp.start()
    g = gain[layer : layer + 1, :]
    total = jnp.zeros((1, D), F32)
    for r in range(0, R, LN_ROWS):
        sl = slice(r, r + LN_ROWS)
        back, piece = norm_back(after[sl, :], e_own[sl, :] + e_peer[sl, :].astype(F32), g)
        total += piece
        ga = go[sl, :] + back
        grad_after[sl, :] = ga
        grad_attn[sl, :] = ga.astype(BF)
    gain_grad[...] = total
    o_cp.wait()
    gm[...] = dot(grad_attn[...], wo[...], NT).astype(BF)
    scale = 1.0 / math.sqrt(HEAD)
    for p in range(HW // 128):
        lanes = slice(128 * p, 128 * (p + 1))
        for half in range(2):
            rows = slice(T * half, T * (half + 1))
            cols = slice(0, T * (half + 1))
            allowed = allowed_block(lengths, half)
            qp = q[rows, lanes]
            gp = gm[rows, lanes]
            kp = k[cols, lanes]
            vp = v[cols, lanes]
            dq = None
            for h in range(2):
                lane_q = head_lanes(qp.shape, h)
                qh = jnp.where(lane_q, qp, jnp.zeros_like(qp))
                gh = jnp.where(lane_q, gp, jnp.zeros_like(gp))
                kh = jnp.where(head_lanes(kp.shape, h), kp, jnp.zeros_like(kp))
                probs = softmax_block(qh, kp, allowed)
                dprob = dot(gh, vp, NT)
                center = jnp.sum(probs * dprob, axis=-1, keepdims=True)
                ds = (probs * (dprob - center)).astype(BF)
                dqh = dot(ds, kh, NN)
                dkh = dot(ds, qh, TN)
                dvh = dot(probs.astype(BF), gh, TN)
                dq = dqh if dq is None else dq + dqh
                if half == 0 and h == 0:
                    dk, dv = dkh, dvh
                elif half == 0:
                    dk, dv = dk + dkh, dv + dvh
                    acc[0, :T, :] = dk
                    acc[1, :T, :] = dv
                elif h == 0:
                    dk, dv = dkh, dvh
                else:
                    dk, dv = dk + dkh, dv + dvh
            dq = dq * scale
            rot = dq * cos[rows, :] - swap_halves(dq) * sin[rows, :]
            grad_packed[rows, lanes] = rot.astype(BF)
        for half in range(2):
            rows = slice(T * half, T * (half + 1))
            dkr, dvr = dk[rows, :], dv[rows, :]
            if half == 0:
                dkr = dkr + acc[0, :T, :]
                dvr = dvr + acc[1, :T, :]
            rot = dkr * cos[rows, :] - swap_halves(dkr) * sin[rows, :]
            grad_packed[rows, HW + 128 * p : HW + 128 * (p + 1)] = rot.astype(BF)
            grad_packed[rows, 2 * HW + 128 * p : 2 * HW + 128 * (p + 1)] = dvr.astype(BF)
    for cp in q_cp:
        cp.wait()
    total = dot(grad_packed[...], wq[...], NT)
    part[...] = total
    if layer == 0:
        sent[...] = part[pl.ds(pl.multiple_of((1 - core) * T, T), T), :].astype(BF)
    else:
        sent[...] = total.astype(BF)


def mlp_back_kernel(place, am, al, e_own, e_peer, grad_after, stream, gain, g_own, g_peer, slope, w_up, w_down,
                    grad_mix, go, branch, gup, part, sent, gain_grad, wu, wd, sem):
    core = place[0]
    down_cp = ff_copies(core, 0, w_down, wd, sem, 0)
    up_cp = ff_copies(core, 0, w_up, wu, sem, NCH)
    for cp in down_cp + up_cp:
        cp.start()
    a_last = al[HIST]
    a_mid = am[HIST]
    go[pl.ds(pl.multiple_of(core * T, T), T), :] = a_last * g_own[...].astype(F32)
    go[pl.ds(pl.multiple_of((1 - core) * T, T), T), :] = a_last * g_peer[...].astype(F32)
    g = gain[1:2, :]
    total = jnp.zeros((1, D), F32)
    for r in range(0, R, LN_ROWS):
        sl = slice(r, r + LN_ROWS)
        back, piece = norm_back(stream[sl, :], e_own[sl, :] + e_peer[sl, :].astype(F32), g)
        total += piece
        gx = grad_after[sl, :] + back
        grad_mix[sl, :] = gx
        out = go[sl, :] + a_mid * gx
        go[sl, :] = out
        branch[sl, :] = out.astype(BF)
    gain_grad[...] = total
    gb = branch[...]
    for j in range(NCH):
        down_cp[j].wait()
        for i in range(0, CH, 256):
            cols = slice(CH * j + i, CH * j + i + 256)
            gup[:, cols] = (slope[:, cols] * dot(gb, wd[:, cols], NN)).astype(BF)
    for cp in up_cp:
        cp.wait()
    total = dot(gup[...], wu[...], NT)
    part[...] = total
    sent[...] = total.astype(BF)


def relations(place, axis):
    here = place[1 + axis]
    near = 1 + 2 * place[0]
    far = 3 - 2 * place[0]
    return here, here ^ far, here ^ near, here ^ 2


def rows_at(index, size):
    return pl.ds(pl.multiple_of(index * size, 16), size)


def split_rows(place, axis, grad, keep, send):
    for slot, quarter in enumerate(relations(place, axis)):
        dst = (keep, send)[slot // 2]
        dst[slot % 2] = grad[rows_at(quarter, 192), :]


def ordered_grad_kernel(axis, place, x, order, y, keep, send, grad):
    grad[...] = dot(dot(x[...], order[...], NN).astype(BF), y[...], TN).astype(BF)
    split_rows(place, axis, grad, keep, send)


def attn_grad_kernel(place, normed, grad_packed, m_own, m_peer, grad_attn, keep, send, grad):
    core = place[0]
    grad[:, : 3 * HW] = dot(normed[...], grad_packed[...], TN).astype(BF)
    ga = grad_attn[:, pl.ds(pl.multiple_of(HW * core, 128), HW)]
    grad[rows_at(core, HW), 3 * HW :] = dot(m_own[...], ga, TN).astype(BF)
    grad[rows_at(1 - core, HW), 3 * HW :] = dot(m_peer[...], ga, TN).astype(BF)
    split_rows(place, 0, grad, keep, send)


def attn_thirds_kernel(axes, place, normed, grad_packed, m_own, m_peer, grad_attn, second_order, third_order,
                       keep_a, send_a, keep_b, send_b, keep_c, send_c, grad_a, grad_b, grad_c):
    core = place[0]
    x = normed[...]
    grad_a[...] = dot(x, grad_packed[:, :THIRD], TN).astype(BF)
    split_rows(place, axes[0], grad_a, keep_a, send_a)
    ordered = dot(x, second_order[...], NN).astype(BF)
    grad_b[...] = dot(ordered, grad_packed[:, THIRD : 2 * THIRD], TN).astype(BF)
    split_rows(place, axes[1], grad_b, keep_b, send_b)
    ordered = dot(x, third_order[...], NN).astype(BF)
    rest = 3 * HW - 2 * THIRD
    grad_c[:, :rest] = dot(ordered, grad_packed[:, 2 * THIRD :], TN).astype(BF)
    mixed = (
        dot(m_own[...], third_order[rows_at(core, HW), :], NN)
        + dot(m_peer[...], third_order[rows_at(1 - core, HW), :], NN)
    ).astype(BF)
    ga = grad_attn[:, pl.ds(pl.multiple_of(HW * core, 128), HW)]
    grad_c[:, rest:] = dot(mixed, ga, TN).astype(BF)
    split_rows(place, axes[2], grad_c, keep_c, send_c)


def encode(vec, dst, row):
    rest = vec
    for c in range(3):
        piece = rest.astype(BF)
        rest = rest - piece.astype(F32)
        for j in range(4):
            lanes = slice(128 * (4 * c + j), 128 * (4 * c + j + 1))
            dst[row : row + 16, lanes] = piece[16 * j : 16 * (j + 1), :]


def decode(src, row):
    parts = []
    for j in range(4):
        block = [src[row : row + 16, 128 * (4 * c + j) : 128 * (4 * c + j + 1)].astype(F32) for c in range(3)]
        parts.append((block[0] + block[1]) + block[2])
    return jnp.concatenate(parts, axis=0)


def near_first_kernel(keep, got, out):
    out[...] = (keep[1].astype(F32) + got[1].astype(F32)).astype(BF)


def near_kernel(rows, with_vec, *refs):
    if with_vec:
        keep, got, vec, out, vec_out = refs
        total = vec[...] + decode(got, 2 * rows)
        vec_out[...] = total
        encode(total, out, rows)
    else:
        keep, got, out = refs
    out[0:rows, :] = (keep[1].astype(F32) + got[rows : 2 * rows, :].astype(F32)).astype(BF)


def last_kernel(with_vec, *refs):
    if with_vec:
        keep, got, got2, vec, out, vec_out = refs
        vec_out[...] = vec[...] + decode(got2, 16)
    else:
        keep, got, got2, out = refs
    out[...] = keep[0, 0:12, :].astype(F32) + got[0:12, :].astype(F32) + got2[0:12, :].astype(F32)


def axis_total_kernel(keep, got, got2, out):
    out[...] = (keep[0].astype(F32) + got[0].astype(F32) + got2[...].astype(F32)).astype(BF)


def second_axis_kernel(axis, widths, with_vec, place, *refs):
    keep, send = refs[-2:]
    if with_vec:
        encode(refs[len(widths)][...], send, 96)
    for slot, index in enumerate(relations(place, axis)):
        lo = 0
        for total, width in zip(refs, widths):
            lanes = slice(lo, lo + width)
            lo += width
            value = total[rows_at(index, 48), :]
            if slot < 2:
                keep[slot, :, lanes] = value
            else:
                send[48 * (slot - 2) : 48 * (slot - 1), lanes] = value


def third_axis_kernel(axis, with_vec, place, *refs):
    if with_vec:
        kept, got, got2, vec, keep, send, vec_out, scr = refs
        total = vec[...] + decode(got2, 48)
        vec_out[...] = total
        encode(total, send, 32)
    else:
        kept, got, got2, keep, send, scr = refs
    total = kept[0].astype(F32) + got[0:48, :].astype(F32) + got2[0:48, :].astype(F32)
    for i in range(4):
        scr[i, 0:12, :] = total[12 * i : 12 * (i + 1), :]
        scr[i, 12:16, :] = jnp.zeros((4, total.shape[1]), F32)
    for slot, index in enumerate(relations(place, axis)):
        value = scr[index].astype(BF)
        if slot < 2:
            keep[slot] = value
        else:
            send[16 * (slot - 2) : 16 * (slot - 1), :] = value


def pack_rows_kernel(place, down, up, attn, out):
    lo = 0
    for ref in (down, up, attn):
        width = ref.shape[1]
        out[:, lo : lo + width] = jnp.where(place[0] == 0, ref[6:12, :], ref[0:6, :])
        lo += width


def write_grads_kernel(place, down, up, attn, got, vec, vec_got,
                       qkv_out, out_out, up_out, down_out, attn_gains, mlp_gains, mid_out, last_out):
    first = place[0] == 0

    def put(dst, layer, lo, value):
        for row in range(6):
            dst[row, layer : layer + 1, lo : lo + value.shape[1]] = value[row : row + 1, :]

    def put_attn(layer, c, lo, value):
        at = 0
        while at < value.shape[1]:
            j = (lo + at) // HW
            width = min(HW * (j + 1) - (lo + at), value.shape[1] - at)
            inside = lo + at - HW * j
            dst, base = (qkv_out, D * j + HW * c) if j < 3 else (out_out, HW * c)
            put(dst, layer, base + inside, value[:, at : at + width])
            at += width

    base = 0
    for j, ref in enumerate((down, up, attn)):
        width = ref.shape[1]
        own = jnp.where(first, ref[0:6, :], ref[6:12, :])
        other = got[:, base : base + width]
        base += width
        for c, both in enumerate((jnp.where(first, own, other), jnp.where(first, other, own))):
            if j < 2:
                for layer in range(2):
                    put((down_out, up_out)[j], layer, FH * c, both[:, FH * (1 - layer) : FH * (2 - layer)])
                put_attn(0, c, THIRD * (j + 1), both[:, 2 * FH :])
            else:
                put_attn(1, c, 0, both[:, :FH])
                put_attn(0, c, 0, both[:, FH:])
    total = vec[...] + vec_got[...]
    for j in range(D // 128):
        lanes = slice(128 * j, 128 * (j + 1))
        attn_gains[:, lanes] = total[4 * j : 4 * j + 2, :]
        mlp_gains[:, lanes] = total[4 * j + 2 : 4 * j + 4, :]
    for dst, base, count in ((mid_out, 24, HIST + 1), (last_out, 37, HIST + 2)):
        lane = lax.broadcasted_iota(jnp.int32, (1, 128), 1)
        row = jnp.zeros((1, 128), F32)
        for i in range(count):
            row = jnp.where(lane == i, total[base + i : base + i + 1, :], row)
        dst[...] = row[:, :count]


def add_kernel(a, b, out):
    out[...] = a[...] + b[...]


def input_grad_kernel(place, e_part, e_peer, grad_after, own, gain, out, gain_grad):
    core = place[0]
    rows = pl.ds(pl.multiple_of(core * T, T), T)
    back, piece = norm_back(own[...].astype(F32), e_part[rows, :] + e_peer[...].astype(F32), gain[0:1, :])
    out[...] = grad_after[rows, :] + back
    gain_grad[...] = piece


def final_kernel(place, al, h_last, block, after, p_own, p_peer, g_own, out, sums):
    core = place[0]
    rows = pl.ds(pl.multiple_of(core * T, T), T)
    b_mid = block[rows, :]
    b_last = after[rows, :] + (p_own[rows, :] + p_peer[...].astype(F32))
    out[...] = (h_last[...] + al[HIST] * b_mid + al[HIST + 1] * b_last).astype(BF)
    g = g_own[...].astype(F32)
    sums[0:1, :] = jnp.sum(g * b_mid, axis=0, keepdims=True)
    sums[1:2, :] = jnp.sum(g * b_last, axis=0, keepdims=True)


def history_kernel(place, am, al, history, g_own, grad_mix, block, out, sums, staged, sem):
    base = place[0] * T
    copies = []
    for k in range(HIST):
        mid = jnp.zeros((8, D), F32)
        last = jnp.zeros((8, D), F32)
        for r in range(0, T, 32):
            sl = slice(r, r + 32)
            gm = grad_mix[pl.ds(pl.multiple_of(base + r, 32), 32), :]
            g = g_own[sl, :].astype(F32)
            staged[k, sl, :] = (al[k] * g + am[k] * gm).astype(BF)
            h = history[k, sl, :].astype(F32)
            mid += jnp.sum((h * gm).reshape(4, 8, D), axis=0)
            last += jnp.sum((h * g).reshape(4, 8, D), axis=0)
        copy = pltpu.make_async_copy(staged.at[k], out.at[k], sem.at[k])
        copy.start()
        copies.append(copy)
        sums[k, 0:1, :] = jnp.sum(mid, axis=0, keepdims=True)
        sums[k, 1:2, :] = jnp.sum(last, axis=0, keepdims=True)
    rows = pl.ds(pl.multiple_of(base, T), T)
    sums[0, 2:3, :] = jnp.sum(block[rows, :] * grad_mix[rows, :], axis=0, keepdims=True)
    for copy in copies:
        copy.wait()


def vector_kernel(h_sums, f_sums, ga0, ga1, gm0, gm1, out):
    for j in range(D // 128):
        lanes = slice(128 * j, 128 * (j + 1))
        out[4 * j : 4 * j + 1, :] = ga0[:, lanes]
        out[4 * j + 1 : 4 * j + 2, :] = 0.5 * ga1[:, lanes]
        out[4 * j + 2 : 4 * j + 3, :] = 0.5 * gm0[:, lanes]
        out[4 * j + 3 : 4 * j + 4, :] = 0.5 * gm1[:, lanes]
    for k in range(HIST):
        out[24 + k : 25 + k, :] = jnp.broadcast_to(
            jnp.sum(h_sums[k, 0:1, :], axis=-1, keepdims=True), (1, 128)
        )
        out[37 + k : 38 + k, :] = jnp.broadcast_to(
            jnp.sum(h_sums[k, 1:2, :], axis=-1, keepdims=True), (1, 128)
        )
    out[36:37, :] = jnp.broadcast_to(jnp.sum(h_sums[0, 2:3, :], axis=-1, keepdims=True), (1, 128))
    out[49:51, :] = jnp.broadcast_to(jnp.sum(f_sums[...], axis=-1, keepdims=True), (2, 128))
    out[51:64, :] = jnp.zeros((13, 128), F32)


def coords(i):
    return [i // 16, (i // 4) % 4, i % 4]


def partner_pairs(axis, step):
    pairs = []
    for chip in range(64):
        for core in range(2):
            flip = (1, 3)[(step + core) % 2]
            there = coords(chip)
            there[axis] ^= flip
            pairs.append((2 * chip + core, 2 * (there[0] * 16 + there[1] * 4 + there[2]) + core))
    return pairs


def trade(x, axis, step):
    return lax.ppermute(x, ("dp", "seq"), partner_pairs(axis, step))


class Chain:
    def __init__(self, order, place, axes, keep, send):
        self.order, self.place, self.axes = order, place, axes
        self.phase, self.vec = 0, None
        self.send_first(keep, send)

    def send_first(self, keep, send):
        self.keep = keep
        self.order.hold(keep)
        self.got = trade(send, self.axes[self.phase], 0)

    def near(self):
        width = self.keep.shape[2]
        self.order.hold(self.got)
        if self.phase == 0:
            other = self.order.call(
                near_first_kernel, vm((192, width), BF), (self.keep, self.got), [V_SPEC] * 2, name="near_first"
            )
        else:
            rows = (48, 16)[self.phase - 1]
            ins, outs = [self.keep, self.got], [vm((rows, width), BF)]
            if self.vec is not None:
                ins.append(self.vec)
                outs = [vm((rows + 16, width), BF), vm((64, 128), F32)]
            result = self.order.call(
                partial(near_kernel, rows, self.vec is not None), outs, ins, [V_SPEC] * len(ins), name="near_sum"
            )
            other = result[0]
            if self.vec is not None:
                self.vec = result[1]
        self.got2 = trade(other, self.axes[self.phase], 1)

    def fin(self):
        width = self.keep.shape[2]
        self.order.drop(self.keep, self.got)
        self.total = self.order.call(
            axis_total_kernel, vm((192, width), BF), (self.keep, self.got, self.got2), [V_SPEC] * 3, name="axis_total"
        )
        self.order.hold(self.total)

    def second(self, *joined, vec=None):
        self.order.drop(*[part.total for part in (self,) + joined])
        ins = [part.total for part in (self,) + joined]
        widths = [x.shape[1] for x in ins]
        total = sum(widths)
        if vec is not None:
            ins.append(vec)
            self.vec = vec
        keep, send = self.order.call(
            partial(second_axis_kernel, self.axes[1], widths, vec is not None),
            [vm((2, 48, total), BF), vm((112 if vec is not None else 96, total), BF)],
            [self.place] + ins, [S_SPEC] + [V_SPEC] * len(ins), name="second_axis",
        )
        self.phase = 1
        self.send_first(keep, send)

    def third(self):
        self.order.drop(self.keep, self.got)
        width = self.keep.shape[2]
        ins = [self.keep, self.got, self.got2]
        outs = [vm((2, 16, width), BF), vm((32, width), BF)]
        if self.vec is not None:
            ins.append(self.vec)
            outs = [vm((2, 16, width), BF), vm((48, width), BF), vm((64, 128), F32)]
        result = self.order.call(
            partial(third_axis_kernel, self.axes[2], self.vec is not None), outs, [self.place] + ins,
            [S_SPEC] + [V_SPEC] * len(ins), [VMEM((4, 16, width), F32)], name="third_axis",
        )
        if self.vec is not None:
            self.vec = result[2]
        self.phase = 2
        self.send_first(result[0], result[1])

    def end(self):
        self.order.drop(self.keep, self.got)
        ins, outs = [self.keep, self.got, self.got2], [vm((12, self.keep.shape[2]), F32)]
        if self.vec is not None:
            ins.append(self.vec)
            outs.append(vm((64, 128), F32))
        result = self.order.call(
            partial(last_kernel, self.vec is not None), outs, ins, [V_SPEC] * len(ins), name="last_sum"
        )
        return result if self.vec is not None else result[0]


def other_core(x):
    return lax.ppermute(x, "seq", [(0, 1), (1, 0)])


def row_order(axes):
    r = jnp.arange(D, dtype=jnp.int32)
    digit = {axes[0]: r // 192, axes[1]: (r // 48) % 4, axes[2]: (r // 12) % 4}
    source = 12 * (16 * digit[0] + 4 * digit[1] + digit[2]) + r % 12
    return (jnp.arange(D, dtype=jnp.int32)[:, None] == source[None, :]).astype(BF)


def shards(inputs, history, alpha_mid, alpha_last, attn_gains, mlp_gains, w_qkv, w_out, w_up, w_down,
           doc_lengths, cotangent):
    core = lax.axis_index("seq")
    chip = lax.axis_index("dp")
    place = jnp.stack([core, chip // 16, (chip // 4) % 4, chip % 4]).astype(jnp.int32)
    w_qkv, w_out, w_up, w_down = (
        pltpu.with_memory_space_constraint(w, pltpu.HBM) for w in (w_qkv, w_out, w_up, w_down)
    )
    order = Order()
    call = order.call
    lengths = doc_lengths
    up_axes, down_axes, attn_axes = (2, 0, 1), (1, 2, 0), (0, 1, 2)
    up_order, down_order = row_order(up_axes), row_order(down_axes)
    in_peer = other_core(inputs)
    g_peer = other_core(cotangent)

    dma = pltpu.SemaphoreType.DMA
    history, inputs, attn_gains = (pltpu.with_memory_space_constraint(x, pltpu.HBM) for x in (history, inputs, attn_gains))
    h_mid, h_last = call(
        mix_kernel, [vm((T, D), F32)] * 2, (alpha_mid, alpha_last, history), [S_SPEC, S_SPEC, H_SPEC],
        [VMEM((HIST, T, D), BF), dma((HIST,))], name="mix_history",
    )
    h_peer = other_core(h_mid)
    att_out = [vm((R, D), BF)] + [vm((R, HW), BF)] * 4
    att_scratch = [VMEM((D, 3 * HW), BF), dma((3,))]
    stream0, normed0, q0, k0, v0, m0, cos, sin = call(
        attend_first_kernel, [vm((R, D), F32)] + att_out + [vm((R, 128), F32)] * 2,
        (place, lengths, inputs, in_peer, attn_gains, w_qkv),
        [S_SPEC] * 2 + [H_SPEC, V_SPEC, H_SPEC, H_SPEC],
        [VMEM((T, D), BF), VMEM((2, D), F32), VMEM((D, 3 * HW), BF), dma((5,))], name="attend_first",
    )
    m0p = other_core(m0)
    order.hold(normed0, q0, k0, v0, cos, sin, m0, h_last)
    mlp_scratch = [VMEM((D, D), BF), VMEM((D, FH), BF), VMEM((D, FH), BF), dma((2 + 2 * NCH,))]
    after0, nm0, act0, slope0, part0, part0s = call(
        mlp_first_kernel,
        [vm((R, D), F32), vm((R, D), BF), vm((R, FH), BF), vm((R, FH), F32), vm((R, D), F32), vm((R, D), BF)],
        (place, stream0, m0, m0p, mlp_gains, w_out, w_up, w_down),
        [S_SPEC, V_SPEC, V_SPEC, V_SPEC, V_SPEC, H_SPEC, H_SPEC, H_SPEC], mlp_scratch, name="mlp_first",
        after=(h_peer, g_peer),
    )
    part0p = other_core(part0s)
    order.hold(m0p)
    order.hold(after0, nm0, act0, slope0)
    stream1, block0, normed1, q1, k1, v1, m1 = call(
        attend_second_kernel, [vm((R, D), F32)] * 2 + att_out,
        (place, alpha_mid, after0, part0, part0p, h_mid, h_peer, attn_gains, w_qkv, cos, sin, lengths),
        [S_SPEC, S_SPEC] + [V_SPEC] * 6 + [H_SPEC] + [V_SPEC] * 2 + [S_SPEC], att_scratch, name="attend_second",
    )
    m1p = other_core(m1)
    order.hold(block0, stream1, normed1, q1, k1, v1)
    after1, nm1, act1, branch1, gup1, e1, e1s, go1 = call(
        mlp_last_kernel,
        [vm((R, D), F32), vm((R, D), BF), vm((R, FH), BF), vm((R, D), BF), vm((R, FH), BF), vm((R, D), F32),
         vm((R, D), BF), vm((R, D), F32)],
        (place, alpha_last, stream1, m1, m1p, cotangent, g_peer, mlp_gains, w_out, w_up, w_down),
        [S_SPEC, S_SPEC] + [V_SPEC] * 6 + [H_SPEC] * 3, mlp_scratch, name="mlp_last",
    )
    e1p = other_core(e1s)
    order.hold(m1, m1p, act1, after1, go1)

    quarter = vm((2, 192, FH), BF)
    whole_grad = [VMEM((D, FH), BF)]

    def ordered_chain(axes, x, rows, y, name):
        keep, send = call(
            partial(ordered_grad_kernel, axes[0]), [quarter] * 2, (place, x, rows, y), [S_SPEC] + [V_SPEC] * 3,
            whole_grad, name=name,
        )
        return Chain(order, place, axes, keep, send)

    def down_chain(branch, act):
        return ordered_chain(down_axes, branch, down_order, act, "down_grad")

    def up_chain(nm, gup):
        return ordered_chain(up_axes, nm, up_order, gup, "up_grad")

    def attn_chain(normed, packed, m, mp, ga):
        keep, send = call(
            attn_grad_kernel, [quarter] * 2, (place, normed, packed, m, mp, ga), [S_SPEC] + [V_SPEC] * 5, whole_grad,
            name="attn_grad",
        )
        return Chain(order, place, attn_axes, keep, send)

    def attn_thirds(normed, packed, m, mp, ga):
        axes = (attn_axes, down_axes, up_axes)
        refs = call(
            partial(attn_thirds_kernel, [a[0] for a in axes]), [vm((2, 192, THIRD), BF)] * 6,
            (place, normed, packed, m, mp, ga, down_order, up_order), [S_SPEC] + [V_SPEC] * 7,
            [VMEM((D, THIRD), BF)] * 3, name="attn_thirds",
        )
        return [Chain(order, place, a, refs[2 * j], refs[2 * j + 1]) for j, a in enumerate(axes)]

    def attn_back(layer, e, ep, go, after, q, k, v):
        return call(
            partial(attend_back_kernel, layer),
            [vm((R, D), F32), vm((R, D), BF), vm((R, 3 * HW), BF), vm((R, D), F32), vm((R if layer else T, D), BF),
             vm((1, D), F32)],
            (place, e, ep, go, after, mlp_gains, w_out, w_qkv, q, k, v, cos, sin, lengths),
            [S_SPEC] + [V_SPEC] * 5 + [H_SPEC] * 2 + [V_SPEC] * 5 + [S_SPEC],
            [VMEM((R, HW), BF), VMEM((2, T, 128), F32), VMEM((HW, D), BF), VMEM((D, 3 * HW), BF), dma((4,))],
            name="attend_back",
        )

    up1 = up_chain(nm1, gup1)
    down1 = down_chain(branch1, act1)
    ga1, gb1, packed1, x1, x1s, gain_mlp1 = attn_back(1, e1, e1p, go1, after1, q1, k1, v1)
    x1p = other_core(x1s)
    order.drop(q1, k1, v1, go1)
    order.hold(ga1)
    attn1 = attn_chain(normed1, packed1, m1, m1p, gb1)
    order.drop(normed1, m1, m1p)
    up1.near()
    down1.near()
    grad_mix, go0, branch0, gup0, e0, e0s, gain_attn1 = call(
        mlp_back_kernel,
        [vm((R, D), F32), vm((R, D), F32), vm((R, D), BF), vm((R, FH), BF), vm((R, D), F32), vm((R, D), BF),
         vm((1, D), F32)],
        (place, alpha_mid, alpha_last, x1, x1p, ga1, stream1, attn_gains, cotangent, g_peer, slope0, w_up, w_down),
        [S_SPEC] * 3 + [V_SPEC] * 8 + [H_SPEC] * 2,
        [VMEM((D, FH), BF), VMEM((D, FH), BF), dma((2 * NCH,))], name="mlp_back",
    )
    e0p = other_core(e0s)
    order.drop(ga1, stream1, slope0)
    order.hold(go0, grad_mix)
    up0 = up_chain(nm0, gup0)
    down0 = down_chain(branch0, act0)
    order.drop(nm0, act0)
    attn1.near()
    up1.fin()
    down1.fin()
    ga0, gb0, packed0, x0, x0s, gain_mlp0 = attn_back(0, e0, e0p, go0, after0, q0, k0, v0)
    x0p = other_core(x0s)
    order.drop(q0, k0, v0, cos, sin, go0, after0)
    order.hold(x0, ga0)
    attn1.fin()
    third_a, third_b, third_c = attn_thirds(normed0, packed0, m0, m0p, gb0)
    order.drop(normed0, m0, m0p)
    up0.near()
    down0.near()
    part1, part1s = call(
        down_kernel, [vm((R, D), F32), vm((T, D), BF)], (place, act1, w_down), [S_SPEC, V_SPEC, H_SPEC],
        [VMEM((D, FH), BF), dma((NCH,))], name="down_last",
    )
    part1p = other_core(part1s)
    order.drop(act1)
    order.hold(part1)
    history_grad, h_sums = call(
        history_kernel, [jax.ShapeDtypeStruct((HIST, T, D), BF), vm((HIST, 3, D), F32)],
        (place, alpha_mid, alpha_last, history, cotangent, grad_mix, block0), [S_SPEC] * 3 + [V_SPEC] * 4,
        [VMEM((HIST, T, D), BF), dma((HIST,))], name="history_grad", out_specs=[H_SPEC, V_SPEC],
    )
    order.drop(grad_mix)
    third_a.near()
    third_b.near()
    third_c.near()
    up0.fin()
    down0.fin()
    input_grad, gain_attn0 = call(
        input_grad_kernel, [jax.ShapeDtypeStruct((T, D), F32), vm((1, D), F32)],
        (place, x0, x0p, ga0, inputs, attn_gains), [S_SPEC] + [V_SPEC] * 5, name="input_grad",
    )
    order.drop(x0, ga0)
    final, f_sums = call(
        final_kernel, [jax.ShapeDtypeStruct((T, D), BF), vm((2, D), F32)],
        (place, alpha_last, h_last, block0, after1, part1, part1p, cotangent),
        [S_SPEC] * 2 + [V_SPEC] * 6, name="final_mix",
    )
    order.drop(block0, after1, part1, h_last)
    vec = call(
        vector_kernel, vm((64, 128), F32), (h_sums, f_sums, gain_attn0, gain_attn1, gain_mlp0, gain_mlp1),
        [V_SPEC] * 6, name="pack_sums",
    )
    got = trade(vec, attn_axes[0], 0)
    third_a.fin()
    third_b.fin()
    third_c.fin()
    vec = call(add_kernel, vm((64, 128), F32), (vec, got), [V_SPEC] * 2, name="add_sums")
    got = trade(vec, attn_axes[0], 1)
    down1.second(down0, third_b)
    up1.second(up0, third_c)
    vec = call(add_kernel, vm((64, 128), F32), (vec, got), [V_SPEC] * 2, name="add_sums")
    attn1.second(third_a, vec=vec)
    chains = (down1, up1, attn1)
    for chain in chains:
        chain.near()
    for chain in chains:
        chain.third()
    for chain in chains:
        chain.near()
    down_sum, up_sum = down1.end(), up1.end()
    attn_sum, vec = attn1.end()
    sums = (down_sum, up_sum, attn_sum)
    vec_got = other_core(vec)
    packed = call(pack_rows_kernel, vm((6, 6 * FH), F32), (place,) + sums, [S_SPEC] + [V_SPEC] * 3, name="pack_rows")
    got = other_core(packed)
    pairs = lambda n: jax.ShapeDtypeStruct((6, 2, n), F32)
    flat = lambda *shape: jax.ShapeDtypeStruct(shape, F32)
    qkv_grad, out_grad, up_grad, down_grad, attn_gains_grad, mlp_gains_grad, mid_grad, last_grad = call(
        write_grads_kernel,
        [pairs(3 * D), pairs(D), pairs(2 * FH), pairs(2 * FH), flat(2, D), flat(2, D), flat(1, HIST + 1),
         flat(1, HIST + 2)],
        (place,) + sums + (got, vec, vec_got), [S_SPEC] + [V_SPEC] * 6, name="write_grads",
    )
    swap = lambda x: jnp.transpose(x, (1, 0, 2))
    return (
        final,
        input_grad,
        history_grad,
        mid_grad.reshape(HIST + 1),
        last_grad.reshape(HIST + 2),
        attn_gains_grad,
        mlp_gains_grad,
        swap(qkv_grad),
        swap(out_grad),
        swap(up_grad),
        swap(down_grad),
    )


def solution(mesh):
    both = P(("dp", "seq"), None)
    spread = P(None, ("dp", "seq"), None)
    return jax.shard_map(
        shards,
        mesh=mesh,
        in_specs=(both, spread) + (P(),) * 8 + (P("dp", None), both),
        out_specs=(both, both, spread) + (P(),) * 4 + (spread,) * 4,
        check_vma=False,
    )
```

```python
import math
from functools import partial

import jax
import jax.numpy as jnp
from jax import lax
from jax.experimental import pallas as pl
from jax.experimental.pallas import tpu as pltpu
from jax.sharding import PartitionSpec as P

BF = jnp.bfloat16
F32 = jnp.float32
NN = (((1,), (0,)), ((), ()))
NT = (((1,), (1,)), ((), ()))
TN = (((0,), (0,)), ((), ()))
EPS = 1e-5
MASKED = -1e30
ROT_BASE = 10000.0
HEAD = 64
GELU_C = math.sqrt(2.0 / math.pi)

R = 256
T = 128
D = 768
HW = 384
FH = 1536
CH = 512
NCH = FH // CH
HIST = 12
LN_ROWS = 64

VMEM = pltpu.VMEM
V_SPEC = pl.BlockSpec(memory_space=pltpu.VMEM)
S_SPEC = pl.BlockSpec(memory_space=pltpu.SMEM)
H_SPEC = pl.BlockSpec(memory_space=pl.ANY)
COSTS = {
    "attend_first": 2.0, "mlp_first": 2.0, "attend_second": 2.0, "mlp_last": 2.0, "attend_back": 8.0, "mlp_back": 8.0,
    "up_grad": 1.0, "down_grad": 1.0, "attn_grad": 1.0,
    "near_first": 1.5, "near_sum": 1.5, "axis_total": 0.5, "second_axis": 0.5, "third_axis": 1.5, "last_sum": 0.5,
}
LIMIT = 14 * 2**20


def dot(a, b, dims):
    return lax.dot_general(a, b, dims, preferred_element_type=F32)


def vm(shape, dtype):
    return pltpu.VMEM(shape, dtype)


class Order:
    def __init__(self):
        self.token = None
        self.held = []

    def hold(self, *arrays):
        self.held += arrays

    def drop(self, *arrays):
        self.held = [x for x in self.held if not any(x is y for y in arrays)]

    def call(self, kernel, outs, ins, in_specs, scratch=(), name=None, out_specs=None, after=()):
        many = isinstance(outs, (list, tuple))
        shapes = list(outs) if many else [outs]
        ins, in_specs = list(ins), list(in_specs)
        count = len(ins)
        after = list(after) + ([] if self.token is None else [self.token])
        in_specs += [H_SPEC] * len(after)
        kept = [x for x in self.held if not any(x is y for y in ins)]
        ins += after + kept
        in_specs += [V_SPEC] * len(kept)
        total = len(ins)
        ins = [pltpu.with_memory_space_constraint(x, VMEM) if spec is V_SPEC else x for x, spec in zip(ins, in_specs)]

        def body(*refs):
            kernel(*refs[:count], *refs[total:])

        result = pl.pallas_call(
            body,
            out_shape=shapes,
            in_specs=in_specs,
            out_specs=out_specs or [V_SPEC] * len(shapes),
            scratch_shapes=list(scratch),
            compiler_params=pltpu.CompilerParams(vmem_limit_bytes=LIMIT),
            cost_estimate=pl.CostEstimate(flops=int(1e9 * COSTS.get(name, 0.01)), bytes_accessed=1000, transcendentals=0),
            name=name,
        )(*ins)
        sizes = [math.prod(shape.shape) for shape in shapes]
        self.token = result[sizes.index(min(sizes))]
        return result if many else result[0]


def normalized(v):
    mean = jnp.mean(v, axis=-1, keepdims=True)
    shifted = v - mean
    var = jnp.mean(shifted * shifted, axis=-1, keepdims=True)
    rstd = lax.rsqrt(var + EPS)
    return shifted * rstd, rstd


def norm_back(v, e, gain):
    n, rstd = normalized(v)
    q = e * gain
    back = (
        q - jnp.mean(q, axis=-1, keepdims=True) - n * jnp.mean(q * n, axis=-1, keepdims=True)
    ) * rstd
    return back, jnp.sum(e * n, axis=0, keepdims=True)


def swap_halves(x):
    lane = lax.broadcasted_iota(jnp.int32, x.shape, 1) % HEAD
    return jnp.where(lane < HEAD // 2, pltpu.roll(x, 128 - 32, 1), pltpu.roll(x, 32, 1))


def head_lanes(shape, head):
    lane = lax.broadcasted_iota(jnp.int32, shape, 1)
    return (lane >= HEAD * head) & (lane < HEAD * (head + 1))


def first_place(lengths, t):
    second = lengths[0, 0]
    third = second + lengths[0, 1]
    return jnp.where(t >= third, third, jnp.where(t >= second, second, 0))


def allowed_block(lengths, half):
    shape = (T, T * (half + 1))
    t = lax.broadcasted_iota(jnp.int32, shape, 0) + T * half
    u = lax.broadcasted_iota(jnp.int32, shape, 1)
    first = first_place(lengths, lax.broadcasted_iota(jnp.int32, (T, 1), 0) + T * half)
    return (u >= first) & (u <= t)


def write_tables(lengths, cos, sin):
    t = lax.broadcasted_iota(jnp.int32, (R, 1), 0)
    offset = (t - first_place(lengths, t)).astype(F32)
    lane = lax.broadcasted_iota(jnp.int32, (1, 128), 1) % HEAD
    freq = jnp.exp((-math.log(ROT_BASE) * 2.0 / HEAD) * (lane % 32).astype(F32))
    angles = offset * freq
    cos[...] = jnp.cos(angles)
    sin[...] = jnp.sin(angles) * jnp.where(lane < 32, -1.0, 1.0)


def probs_columns(half):
    return slice(T * half, T * (2 * half + 1))


def softmax_block(q, k, allowed):
    scores = jnp.where(allowed, dot(q, k, NT), MASKED)
    top = jnp.max(scores, axis=-1, keepdims=True)
    weights = jnp.exp(scores - top)
    return weights * (1.0 / jnp.sum(weights, axis=-1, keepdims=True))


def gelu_and_slope(v):
    square = v * v
    t = jnp.tanh(GELU_C * v * (1.0 + 0.044715 * square))
    half = 0.5 * (1.0 + t)
    slope = half + 0.5 * v * (1.0 - t * t) * (GELU_C * (1.0 + 3.0 * 0.044715 * square))
    return v * half, slope


def qkv_copies(core, layer, w_qkv, wq, sem):
    return [
        pltpu.make_async_copy(
            w_qkv.at[layer, :, pl.ds(pl.multiple_of(D * j + HW * core, 128), HW)],
            wq.at[:, pl.ds(HW * j, HW)],
            sem.at[j],
        )
        for j in range(3)
    ]


def ff_copies(core, layer, w, dst, sem, base):
    return [
        pltpu.make_async_copy(
            w.at[layer, :, pl.ds(pl.multiple_of(FH * core + CH * j, 128), CH)],
            dst.at[:, pl.ds(CH * j, CH)],
            sem.at[base + j],
        )
        for j in range(NCH)
    ]


def out_copies(core, layer, w_out, dst, sem, base):
    return [
        pltpu.make_async_copy(
            w_out.at[layer, pl.ds(pl.multiple_of(HW * part, 128), HW), :],
            dst.at[pl.ds(HW * j, HW), :],
            sem.at[base + j],
        )
        for j, part in enumerate((core, 1 - core))
    ]


def mix_kernel(am, al, history, mid, last):
    for r in range(0, T, 16):
        sl = slice(r, r + 16)
        acc_mid = jnp.zeros((16, D), F32)
        acc_last = jnp.zeros((16, D), F32)
        for k in range(HIST):
            h = history[k, sl, :].astype(F32)
            acc_mid += am[k] * h
            acc_last += al[k] * h
        mid[sl, :] = acc_mid
        last[sl, :] = acc_last


def attend_tail(core, layer, s_out, gain, w_qkv, cos, sin, lengths, normed, q, k, v, mixed, probs_out, wq, sem, copies):
    g = gain[layer : layer + 1, :]
    for r in range(0, R, LN_ROWS):
        sl = slice(r, r + LN_ROWS)
        n, _ = normalized(s_out[sl, :])
        normed[sl, :] = (n * g).astype(BF)
    x = normed[...]
    for j, dst in enumerate((q, k, v)):
        copies[j].wait()
        for p in range(HW // 128):
            lanes = slice(128 * p, 128 * (p + 1))
            packed = dot(x, wq[:, HW * j + 128 * p : HW * j + 128 * (p + 1)], NN).astype(BF)
            if j == 2:
                dst[:, lanes] = packed
            else:
                f = packed.astype(F32)
                rot = f * cos[...] + swap_halves(f) * sin[...]
                if j == 0:
                    rot = rot * (1.0 / math.sqrt(HEAD))
                dst[:, lanes] = rot.astype(BF)
    for half in range(2):
        rows = slice(T * half, T * (half + 1))
        cols = slice(0, T * (half + 1))
        allowed = allowed_block(lengths, half)
        for p in range(HW // 128):
            lanes = slice(128 * p, 128 * (p + 1))
            qp = q[rows, lanes]
            kp = k[cols, lanes]
            vp = v[cols, lanes]
            acc = None
            for h in range(2):
                qh = jnp.where(head_lanes(qp.shape, h), qp, jnp.zeros_like(qp))
                vh = jnp.where(head_lanes(vp.shape, h), vp, jnp.zeros_like(vp))
                probs = softmax_block(qh, kp, allowed)
                probs_out[2 * p + h, :, probs_columns(half)] = probs
                part = dot(probs.astype(BF), vh, NN)
                acc = part if acc is None else acc + part
            mixed[rows, lanes] = acc.astype(BF)


def attend_first_kernel(place, lengths, inputs, peer, gains, w_qkv, stream, normed, q, k, v, mixed, probs,
                        cos, sin, own, gain, wq, sem):
    core = place[0]
    first = [pltpu.make_async_copy(inputs, own, sem.at[3]), pltpu.make_async_copy(gains, gain, sem.at[4])]
    copies = qkv_copies(core, 0, w_qkv, wq, sem)
    for cp in first + copies:
        cp.start()
    write_tables(lengths, cos, sin)
    for cp in first:
        cp.wait()
    stream[pl.ds(pl.multiple_of(core * T, T), T), :] = own[...].astype(F32)
    stream[pl.ds(pl.multiple_of((1 - core) * T, T), T), :] = peer[...].astype(F32)
    attend_tail(core, 0, stream, gain, w_qkv, cos, sin, lengths, normed, q, k, v, mixed, probs, wq, sem, copies)


def attend_second_kernel(place, am, after, p_own, p_peer, h_own, h_peer, gain, w_qkv, cos, sin, lengths,
                         stream, block, normed, q, k, v, mixed, probs, wq, sem):
    core = place[0]
    copies = qkv_copies(core, 1, w_qkv, wq, sem)
    for cp in copies:
        cp.start()
    scale = am[HIST]
    stream[pl.ds(pl.multiple_of(core * T, T), T), :] = h_own[...]
    stream[pl.ds(pl.multiple_of((1 - core) * T, T), T), :] = h_peer[...]
    for r in range(0, R, LN_ROWS):
        sl = slice(r, r + LN_ROWS)
        b = after[sl, :] + (p_own[sl, :] + p_peer[sl, :].astype(F32))
        block[sl, :] = b
        stream[sl, :] = stream[sl, :] + scale * b
    attend_tail(core, 1, stream, gain, w_qkv, cos, sin, lengths, normed, q, k, v, mixed, probs, wq, sem, copies)


def mlp_front(layer, stream, m_own, m_peer, gain, after, normed, wo, wo_copies):
    g = gain[layer : layer + 1, :]
    for cp in wo_copies:
        cp.wait()
    for r in range(0, R, 128):
        sl = slice(r, r + 128)
        a = stream[sl, :] + (
            dot(m_own[sl, :], wo[:HW, :], NN) + dot(m_peer[sl, :], wo[HW:, :], NN)
        )
        after[sl, :] = a
        n, _ = normalized(a)
        normed[sl, :] = (n * g).astype(BF)


def mlp_first_kernel(place, stream, m_own, m_peer, gain, w_out, w_up, w_down,
                     after, normed, act, slope, part, sent, wo, wu, wd, sem):
    core = place[0]
    out_cp = out_copies(core, 0, w_out, wo, sem, 0)
    up_cp = ff_copies(core, 0, w_up, wu, sem, 2)
    down_cp = ff_copies(core, 0, w_down, wd, sem, 2 + NCH)
    for cp in out_cp + up_cp + down_cp:
        cp.start()
    mlp_front(0, stream, m_own, m_peer, gain, after, normed, wo, out_cp)
    x = normed[...]
    for j in range(NCH):
        up_cp[j].wait()
        for i in range(0, CH, 256):
            cols = slice(CH * j + i, CH * j + i + 256)
            u = dot(x, wu[:, cols], NN)
            a, s = gelu_and_slope(u)
            act[:, cols] = a.astype(BF)
            slope[:, cols] = s
    for cp in down_cp:
        cp.wait()
    total = dot(act[...], wd[...], NT)
    part[...] = total
    sent[...] = total.astype(BF)


def mlp_last_kernel(place, al, stream, m_own, m_peer, g_own, g_peer, gain, w_out, w_up, w_down,
                    after, normed, act, branch, gup, part, sent, go, down, down_sent, wo, wu, wd, sem):
    core = place[0]
    out_cp = out_copies(core, 1, w_out, wo, sem, 0)
    up_cp = ff_copies(core, 1, w_up, wu, sem, 2)
    down_cp = ff_copies(core, 1, w_down, wd, sem, 2 + NCH)
    for cp in out_cp + up_cp + down_cp:
        cp.start()
    scale = al[HIST + 1]
    own_rows = pl.ds(pl.multiple_of(core * T, T), T)
    peer_rows = pl.ds(pl.multiple_of((1 - core) * T, T), T)
    go[own_rows, :] = scale * g_own[...].astype(F32)
    go[peer_rows, :] = scale * g_peer[...].astype(F32)
    branch[...] = go[...].astype(BF)
    mlp_front(1, stream, m_own, m_peer, gain, after, normed, wo, out_cp)
    x = normed[...]
    gb = branch[...]
    for j in range(NCH):
        up_cp[j].wait()
        down_cp[j].wait()
        for i in range(0, CH, 256):
            cols = slice(CH * j + i, CH * j + i + 256)
            u = dot(x, wu[:, cols], NN)
            a, s = gelu_and_slope(u)
            act[:, cols] = a.astype(BF)
            gup[:, cols] = (s * dot(gb, wd[:, cols], NN)).astype(BF)
    total = dot(gup[...], wu[...], NT)
    part[...] = total
    sent[...] = total.astype(BF)
    down[...] = dot(act[...], wd[...], NT)
    down_sent[...] = down[peer_rows, :].astype(BF)


def attend_back_kernel(layer, place, e_own, e_peer, go, after, gain, w_out, w_qkv, q, k, v, probs_in, cos, sin,
                       grad_after, grad_attn, grad_packed, part, sent, gain_grad, gm, acc, wo, wq, sem):
    core = place[0]
    q_cp = qkv_copies(core, layer, w_qkv, wq, sem)
    o_cp = pltpu.make_async_copy(
        w_out.at[layer, pl.ds(pl.multiple_of(HW * core, 128), HW), :], wo, sem.at[3]
    )
    o_cp.start()
    for cp in q_cp:
        cp.start()
    g = gain[layer : layer + 1, :]
    total = jnp.zeros((1, D), F32)
    for r in range(0, R, LN_ROWS):
        sl = slice(r, r + LN_ROWS)
        back, piece = norm_back(after[sl, :], e_own[sl, :] + e_peer[sl, :].astype(F32), g)
        total += piece
        ga = go[sl, :] + back
        grad_after[sl, :] = ga
        grad_attn[sl, :] = ga.astype(BF)
    gain_grad[...] = total
    o_cp.wait()
    gm[...] = dot(grad_attn[...], wo[...], NT).astype(BF)
    scale = 1.0 / math.sqrt(HEAD)
    for p in range(HW // 128):
        lanes = slice(128 * p, 128 * (p + 1))
        for half in range(2):
            rows = slice(T * half, T * (half + 1))
            cols = slice(0, T * (half + 1))
            qp = q[rows, lanes]
            gp = gm[rows, lanes]
            kp = k[cols, lanes]
            vp = v[cols, lanes]
            dq = None
            for h in range(2):
                lane_q = head_lanes(qp.shape, h)
                qh = jnp.where(lane_q, qp, jnp.zeros_like(qp))
                gh = jnp.where(lane_q, gp, jnp.zeros_like(gp))
                kh = jnp.where(head_lanes(kp.shape, h), kp, jnp.zeros_like(kp))
                probs = probs_in[2 * p + h, :, probs_columns(half)]
                dprob = dot(gh, vp, NT)
                center = jnp.sum(probs * dprob, axis=-1, keepdims=True)
                ds = (probs * (dprob - center)).astype(BF)
                dqh = dot(ds, kh, NN)
                dkh = dot(ds, qh, TN)
                dvh = dot(probs.astype(BF), gh, TN)
                dq = dqh if dq is None else dq + dqh
                if half == 0 and h == 0:
                    dk, dv = dkh, dvh
                elif half == 0:
                    dk, dv = dk + dkh, dv + dvh
                    acc[0, :T, :] = dk
                    acc[1, :T, :] = dv
                elif h == 0:
                    dk, dv = dkh, dvh
                else:
                    dk, dv = dk + dkh, dv + dvh
            dq = dq * scale
            rot = dq * cos[rows, :] - swap_halves(dq) * sin[rows, :]
            grad_packed[rows, lanes] = rot.astype(BF)
        for half in range(2):
            rows = slice(T * half, T * (half + 1))
            dkr, dvr = dk[rows, :], dv[rows, :]
            if half == 0:
                dkr = dkr + acc[0, :T, :]
                dvr = dvr + acc[1, :T, :]
            rot = dkr * cos[rows, :] - swap_halves(dkr) * sin[rows, :]
            grad_packed[rows, HW + 128 * p : HW + 128 * (p + 1)] = rot.astype(BF)
            grad_packed[rows, 2 * HW + 128 * p : 2 * HW + 128 * (p + 1)] = dvr.astype(BF)
    for cp in q_cp:
        cp.wait()
    total = dot(grad_packed[...], wq[...], NT)
    part[...] = total
    if layer == 0:
        sent[...] = part[pl.ds(pl.multiple_of((1 - core) * T, T), T), :].astype(BF)
    else:
        sent[...] = total.astype(BF)


def mlp_back_kernel(place, am, al, e_own, e_peer, grad_after, stream, gain, g_own, g_peer, slope, w_up, w_down,
                    grad_mix, go, branch, gup, part, sent, gain_grad, wu, wd, sem):
    core = place[0]
    down_cp = ff_copies(core, 0, w_down, wd, sem, 0)
    up_cp = ff_copies(core, 0, w_up, wu, sem, NCH)
    for cp in down_cp + up_cp:
        cp.start()
    a_last = al[HIST]
    a_mid = am[HIST]
    go[pl.ds(pl.multiple_of(core * T, T), T), :] = a_last * g_own[...].astype(F32)
    go[pl.ds(pl.multiple_of((1 - core) * T, T), T), :] = a_last * g_peer[...].astype(F32)
    g = gain[1:2, :]
    total = jnp.zeros((1, D), F32)
    for r in range(0, R, LN_ROWS):
        sl = slice(r, r + LN_ROWS)
        back, piece = norm_back(stream[sl, :], e_own[sl, :] + e_peer[sl, :].astype(F32), g)
        total += piece
        gx = grad_after[sl, :] + back
        grad_mix[sl, :] = gx
        out = go[sl, :] + a_mid * gx
        go[sl, :] = out
        branch[sl, :] = out.astype(BF)
    gain_grad[...] = total
    gb = branch[...]
    for j in range(NCH):
        down_cp[j].wait()
        for i in range(0, CH, 256):
            cols = slice(CH * j + i, CH * j + i + 256)
            gup[:, cols] = (slope[:, cols] * dot(gb, wd[:, cols], NN)).astype(BF)
    for cp in up_cp:
        cp.wait()
    total = dot(gup[...], wu[...], NT)
    part[...] = total
    sent[...] = total.astype(BF)


def relations(place, axis):
    here = place[1 + axis]
    near = 1 + 2 * place[0]
    far = 3 - 2 * place[0]
    return here, here ^ far, here ^ near, here ^ 2


def rows_at(index, size):
    return pl.ds(pl.multiple_of(index * size, 16), size)


def split_rows(place, axis, grad, keep, send):
    for slot, quarter in enumerate(relations(place, axis)):
        dst = (keep, send)[slot // 2]
        dst[slot % 2] = grad[rows_at(quarter, 192), :]


def row_order_kernel(all_axes, place, *outs):
    r = lax.broadcasted_iota(jnp.int32, (1, D), 1)
    for axes, out in zip(all_axes, outs):
        slots = relations(place, axes[0])
        first = jnp.where(r < 192, slots[0], jnp.where(r < 384, slots[1], jnp.where(r < 576, slots[2], slots[3])))
        digit = {axes[0]: first, axes[1]: (r // 48) % 4, axes[2]: (r // 12) % 4}
        source = 12 * (16 * digit[0] + 4 * digit[1] + digit[2]) + r % 12
        for base in range(0, D, 64):
            row = lax.broadcasted_iota(jnp.int32, (64, D), 0) + base
            out[base : base + 64, :] = jnp.where(row == source, 1.0, 0.0).astype(BF)


def ordered_grad_kernel(x, order, y, keep, send):
    ordered = dot(x[...], order[...], NN).astype(BF)
    for j, dst in enumerate((keep, send)):
        half = dot(ordered[:, 384 * j : 384 * (j + 1)], y[...], TN).astype(BF)
        dst[0] = half[:192]
        dst[1] = half[192:]


def attn_grad_kernel(place, normed, grad_packed, m_own, m_peer, grad_attn, keep, send, grad):
    core = place[0]
    grad[:, : 3 * HW] = dot(normed[...], grad_packed[...], TN).astype(BF)
    ga = grad_attn[:, pl.ds(pl.multiple_of(HW * core, 128), HW)]
    grad[rows_at(core, HW), 3 * HW :] = dot(m_own[...], ga, TN).astype(BF)
    grad[rows_at(1 - core, HW), 3 * HW :] = dot(m_peer[...], ga, TN).astype(BF)
    split_rows(place, 0, grad, keep, send)


def encode(vec, dst, row):
    rest = vec
    for c in range(3):
        piece = rest.astype(BF)
        rest = rest - piece.astype(F32)
        for j in range(4):
            lanes = slice(128 * (4 * c + j), 128 * (4 * c + j + 1))
            dst[row : row + 16, lanes] = piece[16 * j : 16 * (j + 1), :]


def decode(src, row):
    parts = []
    for j in range(4):
        block = [src[row : row + 16, 128 * (4 * c + j) : 128 * (4 * c + j + 1)].astype(F32) for c in range(3)]
        parts.append((block[0] + block[1]) + block[2])
    return jnp.concatenate(parts, axis=0)


def near_first_kernel(with_vec, *refs):
    if with_vec:
        keep, got, vec, vec_got, out, vec_out = refs
        total = vec[...] + vec_got[...]
        vec_out[...] = total
        encode(total, out, 192)
    else:
        keep, got, out = refs
    out[0:192, :] = (keep[1].astype(F32) + got[1].astype(F32)).astype(BF)


def near_kernel(rows, with_vec, *refs):
    if with_vec:
        keep, got, vec, out, vec_out = refs
        total = vec[...] + decode(got, 2 * rows)
        vec_out[...] = total
        encode(total, out, rows)
    else:
        keep, got, out = refs
    out[0:rows, :] = (keep[1].astype(F32) + got[rows : 2 * rows, :].astype(F32)).astype(BF)


def last_kernel(with_vec, *refs):
    if with_vec:
        keep, got, got2, vec, out, vec_out = refs
        vec_out[...] = vec[...] + decode(got2, 16)
    else:
        keep, got, got2, out = refs
    out[...] = keep[0, 0:12, :].astype(F32) + got[0:12, :].astype(F32) + got2[0:12, :].astype(F32)


def axis_total_kernel(with_vec, *refs):
    if with_vec:
        keep, got, got2, vec, out, vec_out = refs
        vec_out[...] = vec[...] + decode(got2, 192)
    else:
        keep, got, got2, out = refs
    out[...] = (keep[0].astype(F32) + got[0].astype(F32) + got2[0:192, :].astype(F32)).astype(BF)


def second_axis_kernel(axis, widths, with_vec, place, *refs):
    keep, send = refs[-2:]
    if with_vec:
        encode(refs[len(widths)][...], send, 96)
    for slot, index in enumerate(relations(place, axis)):
        lo = 0
        for total, width in zip(refs, widths):
            lanes = slice(lo, lo + width)
            lo += width
            value = total[rows_at(index, 48), :]
            if slot < 2:
                keep[slot, :, lanes] = value
            else:
                send[48 * (slot - 2) : 48 * (slot - 1), lanes] = value


def third_axis_kernel(axis, widths, with_vec, place, *refs):
    count = 3 * len(widths)
    keep, send = refs[count + with_vec : count + with_vec + 2]
    scr = refs[-1]
    lo = 0
    for j, width in enumerate(widths):
        kept, got, got2 = refs[3 * j : 3 * j + 3]
        total = kept[0].astype(F32) + got[0:48, :].astype(F32) + got2[0:48, :].astype(F32)
        for i in range(4):
            scr[i, 0:12, lo : lo + width] = total[12 * i : 12 * (i + 1), :]
            scr[i, 12:16, lo : lo + width] = jnp.zeros((4, width), F32)
        lo += width
    for slot, index in enumerate(relations(place, axis)):
        value = scr[index].astype(BF)
        if slot < 2:
            keep[slot] = value
        else:
            send[16 * (slot - 2) : 16 * (slot - 1), :] = value
    if with_vec:
        vec, vec_out = refs[count], refs[-2]
        total = vec[...] + decode(refs[2], 48)
        vec_out[...] = total
        encode(total, send, 32)


def pack_rows_kernel(place, ref, out):
    out[...] = jnp.where(place[0] == 0, ref[6:12, :], ref[0:6, :])


def with_token(kernel):
    def body(*refs):
        kernel(*refs[:-1])
        refs[-1][...] = jnp.zeros_like(refs[-1])

    return body


def put(dst, layer, lo, value):
    for row in range(6):
        dst[row, layer : layer + 1, lo : lo + value.shape[1]] = value[row : row + 1, :]


def both_cores(first, ref, got):
    own = jnp.where(first, ref[0:6, :], ref[6:12, :])
    other = got[...]
    return jnp.where(first, own, other), jnp.where(first, other, own)


def write_mlp_kernel(place, ref, got, up_out, down_out):
    for c, both in enumerate(both_cores(place[0] == 0, ref, got)):
        for j, dst in enumerate((down_out, up_out)):
            for layer in range(2):
                lo = 2 * FH * j + FH * (1 - layer)
                put(dst, layer, FH * c, both[:, lo : lo + FH])


def write_attn_kernel(place, attn, got, vec, vec_got, qkv_out, out_out, attn_gains, mlp_gains, mid_out, last_out):
    for c, both in enumerate(both_cores(place[0] == 0, attn, got)):
        for layer in range(2):
            value = both[:, FH * (1 - layer) : FH * (2 - layer)]
            for i in range(3):
                put(qkv_out, layer, D * i + HW * c, value[:, HW * i : HW * (i + 1)])
            put(out_out, layer, HW * c, value[:, 3 * HW :])
    total = vec[...] + vec_got[...]
    for j in range(D // 128):
        lanes = slice(128 * j, 128 * (j + 1))
        attn_gains[:, lanes] = total[4 * j : 4 * j + 2, :]
        mlp_gains[:, lanes] = total[4 * j + 2 : 4 * j + 4, :]
    for dst, base, count in ((mid_out, 24, HIST + 1), (last_out, 37, HIST + 2)):
        lane = lax.broadcasted_iota(jnp.int32, (1, 128), 1)
        row = jnp.zeros((1, 128), F32)
        for i in range(count):
            row = jnp.where(lane == i, total[base + i : base + i + 1, :], row)
        dst[...] = row[:, :count]


def input_grad_kernel(place, e_part, e_peer, grad_after, own, gain, out):
    core = place[0]
    rows = pl.ds(pl.multiple_of(core * T, T), T)
    back, _ = norm_back(own[...].astype(F32), e_part[rows, :] + e_peer[...].astype(F32), gain[0:1, :])
    out[...] = grad_after[rows, :] + back


def final_kernel(place, al, h_last, block, after, p_own, p_peer, out):
    core = place[0]
    rows = pl.ds(pl.multiple_of(core * T, T), T)
    b_last = after[rows, :] + (p_own[rows, :] + p_peer[...].astype(F32))
    out[...] = (h_last[...] + al[HIST] * block[rows, :] + al[HIST + 1] * b_last).astype(BF)


def history_kernel(place, am, al, history, g_own, g_peer, grad_mix, block, after, part, out, sums, f_sums, g32, gm32, staged,
                   sem):
    own = pl.ds(pl.multiple_of(place[0] * T, T), T)
    peer = pl.ds(pl.multiple_of((1 - place[0]) * T, T), T)
    g32[...] = g_own[...].astype(F32)
    gm32[...] = grad_mix[own, :]
    copies = []
    for k in range(HIST):
        mid = jnp.zeros((8, D), F32)
        last = jnp.zeros((8, D), F32)
        for r in range(0, T, 16):
            sl = slice(r, r + 16)
            gm, g = gm32[sl, :], g32[sl, :]
            staged[k, sl, :] = (al[k] * g + am[k] * gm).astype(BF)
            h = history[k, sl, :].astype(F32)
            a, b = h * gm, h * g
            mid += a[:8] + a[8:]
            last += b[:8] + b[8:]
        copies.append(pltpu.make_async_copy(staged.at[k], out.at[k], sem.at[k]))
        copies[k].start()
        sums[k, 0:1, :] = jnp.sum(mid, axis=0, keepdims=True)
        sums[k, 1:2, :] = jnp.sum(last, axis=0, keepdims=True)
    b_own = block[own, :]
    sums[0, 2:3, :] = jnp.sum(b_own * gm32[...], axis=0, keepdims=True)
    f_sums[0:1, :] = jnp.sum(g32[...] * b_own, axis=0, keepdims=True)
    f_sums[1:2, :] = jnp.sum(g32[...] * (after[own, :] + part[own, :]), axis=0, keepdims=True) + jnp.sum(
        g_peer[...].astype(F32) * part[peer, :], axis=0, keepdims=True
    )
    for copy in copies:
        copy.wait()


def vector_kernel(h_sums, f_sums, own, peer, x_part, place, ga1, gm0, gm1, out):
    ga0 = jnp.zeros((1, D), F32)
    for ref, core in ((own, place[0]), (peer, 1 - place[0])):
        n, _ = normalized(ref[...].astype(F32))
        ga0 += jnp.sum(x_part[pl.ds(pl.multiple_of(core * T, T), T), :] * n, axis=0, keepdims=True)
    for j in range(D // 128):
        lanes = slice(128 * j, 128 * (j + 1))
        out[4 * j : 4 * j + 1, :] = ga0[:, lanes]
        out[4 * j + 1 : 4 * j + 2, :] = 0.5 * ga1[:, lanes]
        out[4 * j + 2 : 4 * j + 3, :] = 0.5 * gm0[:, lanes]
        out[4 * j + 3 : 4 * j + 4, :] = 0.5 * gm1[:, lanes]
    for k in range(HIST):
        out[24 + k : 25 + k, :] = jnp.broadcast_to(
            jnp.sum(h_sums[k, 0:1, :], axis=-1, keepdims=True), (1, 128)
        )
        out[37 + k : 38 + k, :] = jnp.broadcast_to(
            jnp.sum(h_sums[k, 1:2, :], axis=-1, keepdims=True), (1, 128)
        )
    out[36:37, :] = jnp.broadcast_to(jnp.sum(h_sums[0, 2:3, :], axis=-1, keepdims=True), (1, 128))
    out[49:51, :] = jnp.broadcast_to(jnp.sum(f_sums[...], axis=-1, keepdims=True), (2, 128))
    out[51:64, :] = jnp.zeros((13, 128), F32)


def coords(i):
    return [i // 16, (i // 4) % 4, i % 4]


def partner_pairs(axis, step):
    pairs = []
    for chip in range(64):
        for core in range(2):
            flip = (1, 3)[(step + core) % 2]
            there = coords(chip)
            there[axis] ^= flip
            pairs.append((2 * chip + core, 2 * (there[0] * 16 + there[1] * 4 + there[2]) + core))
    return pairs


def trade(x, axis, step):
    return lax.ppermute(x, ("dp", "seq"), partner_pairs(axis, step))


class Chain:
    def __init__(self, order, place, axes, keep, send):
        self.order, self.place, self.axes = order, place, axes
        self.phase, self.vec = 0, None
        self.send_first(keep, send)

    def send_first(self, keep, send):
        self.keep = keep
        self.order.hold(keep)
        self.got = trade(send, self.axes[self.phase], 0)

    def near(self, vec=None):
        width = self.keep.shape[2]
        self.order.hold(self.got)
        if self.phase == 0:
            ins, outs = [self.keep, self.got], [vm((192, width), BF)]
            if vec is not None:
                ins += vec
                outs = [vm((208, width), BF), vm((64, 128), F32)]
            result = self.order.call(
                partial(near_first_kernel, vec is not None), outs, ins, [V_SPEC] * len(ins), name="near_first"
            )
            other = result[0]
            if vec is not None:
                self.vec = result[1]
        else:
            rows = (48, 16)[self.phase - 1]
            ins, outs = [self.keep, self.got], [vm((rows, width), BF)]
            if self.vec is not None:
                ins.append(self.vec)
                outs = [vm((rows + 16, width), BF), vm((64, 128), F32)]
            result = self.order.call(
                partial(near_kernel, rows, self.vec is not None), outs, ins, [V_SPEC] * len(ins), name="near_sum"
            )
            other = result[0]
            if self.vec is not None:
                self.vec = result[1]
        self.got2 = trade(other, self.axes[self.phase], 1)

    def fin(self):
        width = self.keep.shape[2]
        self.order.drop(self.keep, self.got)
        ins, outs = [self.keep, self.got, self.got2], [vm((192, width), BF)]
        if self.vec is not None:
            ins.append(self.vec)
            outs.append(vm((64, 128), F32))
        result = self.order.call(
            partial(axis_total_kernel, self.vec is not None), outs, ins, [V_SPEC] * len(ins), name="axis_total"
        )
        self.total = result[0]
        if self.vec is not None:
            self.vec = result[1]
        self.order.hold(self.total)

    def second(self, *joined, vec=None):
        self.order.drop(*[part.total for part in (self,) + joined])
        ins = [part.total for part in (self,) + joined]
        widths = [x.shape[1] for x in ins]
        total = sum(widths)
        if vec is not None:
            ins.append(vec)
            self.vec = vec
        keep, send = self.order.call(
            partial(second_axis_kernel, self.axes[1], widths, vec is not None),
            [vm((2, 48, total), BF), vm((112 if vec is not None else 96, total), BF)],
            [self.place] + ins, [S_SPEC] + [V_SPEC] * len(ins), name="second_axis",
        )
        self.phase = 1
        self.send_first(keep, send)

    def third(self, *joined):
        parts = (self,) + joined
        for part in parts:
            self.order.drop(part.keep, part.got)
        widths = [part.keep.shape[2] for part in parts]
        width = sum(widths)
        ins = [x for part in parts for x in (part.keep, part.got, part.got2)]
        outs = [vm((2, 16, width), BF), vm((32, width), BF)]
        if self.vec is not None:
            ins.append(self.vec)
            outs = [vm((2, 16, width), BF), vm((48, width), BF), vm((64, 128), F32)]
        result = self.order.call(
            partial(third_axis_kernel, self.axes[2], widths, self.vec is not None), outs, [self.place] + ins,
            [S_SPEC] + [V_SPEC] * len(ins), [VMEM((4, 16, width), F32)], name="third_axis",
        )
        if self.vec is not None:
            self.vec = result[2]
        self.phase = 2
        self.send_first(result[0], result[1])

    def end(self):
        self.order.drop(self.keep, self.got)
        ins, outs = [self.keep, self.got, self.got2], [vm((12, self.keep.shape[2]), F32)]
        if self.vec is not None:
            ins.append(self.vec)
            outs.append(vm((64, 128), F32))
        result = self.order.call(
            partial(last_kernel, self.vec is not None), outs, ins, [V_SPEC] * len(ins), name="last_sum"
        )
        return result if self.vec is not None else result[0]


def other_core(x):
    return lax.ppermute(x, "seq", [(0, 1), (1, 0)])


def shards(inputs, history, alpha_mid, alpha_last, attn_gains, mlp_gains, w_qkv, w_out, w_up, w_down,
           doc_lengths, cotangent):
    core = lax.axis_index("seq")
    chip = lax.axis_index("dp")
    place = jnp.stack([core, chip // 16, (chip // 4) % 4, chip % 4]).astype(jnp.int32)
    w_qkv, w_out, w_up, w_down = (
        pltpu.with_memory_space_constraint(w, pltpu.HBM) for w in (w_qkv, w_out, w_up, w_down)
    )
    order = Order()
    call = order.call
    lengths = doc_lengths
    up_axes, down_axes, attn_axes = (2, 1, 0), (1, 2, 0), (0, 1, 2)
    in_peer = other_core(inputs)
    g_peer = other_core(cotangent)

    dma = pltpu.SemaphoreType.DMA
    inputs_hbm, gains_hbm = (pltpu.with_memory_space_constraint(x, pltpu.HBM) for x in (inputs, attn_gains))
    order.hold(history)
    att_out = [vm((R, D), BF)] + [vm((R, HW), BF)] * 4 + [vm((2 * HW // 128, T, 3 * T), F32)]
    att_scratch = [VMEM((D, 3 * HW), BF), dma((3,))]
    stream0, normed0, q0, k0, v0, m0, probs0, cos, sin = call(
        attend_first_kernel, [vm((R, D), F32)] + att_out + [vm((R, 128), F32)] * 2,
        (place, lengths, inputs_hbm, in_peer, gains_hbm, w_qkv),
        [S_SPEC] * 2 + [H_SPEC, V_SPEC, H_SPEC, H_SPEC],
        [VMEM((T, D), BF), VMEM((2, D), F32), VMEM((D, 3 * HW), BF), dma((5,))], name="attend_first",
    )
    m0p = other_core(m0)
    order.hold(normed0, q0, k0, v0, probs0, cos, sin, m0)
    h_mid, h_last = call(
        mix_kernel, [vm((T, D), F32)] * 2, (alpha_mid, alpha_last, history), [S_SPEC, S_SPEC, V_SPEC],
        name="mix_history",
    )
    h_peer = other_core(h_mid)
    order.hold(h_last)
    order.hold(inputs, in_peer, cotangent, g_peer, attn_gains, mlp_gains)
    mlp_scratch = [VMEM((D, D), BF), VMEM((D, FH), BF), VMEM((D, FH), BF), dma((2 + 2 * NCH,))]
    after0, nm0, act0, slope0, part0, part0s = call(
        mlp_first_kernel,
        [vm((R, D), F32), vm((R, D), BF), vm((R, FH), BF), vm((R, FH), F32), vm((R, D), F32), vm((R, D), BF)],
        (place, stream0, m0, m0p, mlp_gains, w_out, w_up, w_down),
        [S_SPEC, V_SPEC, V_SPEC, V_SPEC, V_SPEC, H_SPEC, H_SPEC, H_SPEC], mlp_scratch, name="mlp_first",
        after=(g_peer,),
    )
    part0p = other_core(part0s)
    up_order, down_order = call(
        partial(row_order_kernel, (up_axes, down_axes)), [vm((D, D), BF)] * 2, (place,), [S_SPEC], name="row_order"
    )
    order.hold(up_order, down_order)
    order.hold(m0p)
    order.hold(after0, nm0, act0, slope0)
    stream1, block0, normed1, q1, k1, v1, m1, probs1 = call(
        attend_second_kernel, [vm((R, D), F32)] * 2 + att_out,
        (place, alpha_mid, after0, part0, part0p, h_mid, h_peer, attn_gains, w_qkv, cos, sin, lengths),
        [S_SPEC, S_SPEC] + [V_SPEC] * 6 + [H_SPEC] + [V_SPEC] * 2 + [S_SPEC], att_scratch, name="attend_second",
    )
    m1p = other_core(m1)
    order.hold(block0, stream1, normed1, q1, k1, v1, probs1)
    after1, nm1, act1, branch1, gup1, e1, e1s, go1, part1, part1s = call(
        mlp_last_kernel,
        [vm((R, D), F32), vm((R, D), BF), vm((R, FH), BF), vm((R, D), BF), vm((R, FH), BF), vm((R, D), F32),
         vm((R, D), BF), vm((R, D), F32), vm((R, D), F32), vm((T, D), BF)],
        (place, alpha_last, stream1, m1, m1p, cotangent, g_peer, mlp_gains, w_out, w_up, w_down),
        [S_SPEC, S_SPEC] + [V_SPEC] * 6 + [H_SPEC] * 3, mlp_scratch, name="mlp_last",
    )
    e1p = other_core(e1s)
    part1p = other_core(part1s)
    order.hold(m1, m1p, after1, go1, part1, part1s)

    quarter = vm((2, 192, FH), BF)
    whole_grad = [VMEM((D, FH), BF)]

    def ordered_chain(axes, x, rows, y, name):
        keep, send = call(
            ordered_grad_kernel, [quarter] * 2, (x, rows, y), [V_SPEC] * 3, name=name,
        )
        return Chain(order, place, axes, keep, send)

    def down_chain(branch, act):
        return ordered_chain(down_axes, branch, down_order, act, "down_grad")

    def up_chain(nm, gup):
        return ordered_chain(up_axes, nm, up_order, gup, "up_grad")

    def attn_chain(normed, packed, m, mp, ga):
        keep, send = call(
            attn_grad_kernel, [quarter] * 2, (place, normed, packed, m, mp, ga), [S_SPEC] + [V_SPEC] * 5, whole_grad,
            name="attn_grad",
        )
        return Chain(order, place, attn_axes, keep, send)

    def attn_back(layer, e, ep, go, after, q, k, v, probs):
        return call(
            partial(attend_back_kernel, layer),
            [vm((R, D), F32), vm((R, D), BF), vm((R, 3 * HW), BF), vm((R, D), F32), vm((R if layer else T, D), BF),
             vm((1, D), F32)],
            (place, e, ep, go, after, mlp_gains, w_out, w_qkv, q, k, v, probs, cos, sin),
            [S_SPEC] + [V_SPEC] * 5 + [H_SPEC] * 2 + [V_SPEC] * 6,
            [VMEM((R, HW), BF), VMEM((2, T, 128), F32), VMEM((HW, D), BF), VMEM((D, 3 * HW), BF), dma((4,))],
            name="attend_back",
        )

    up1 = up_chain(nm1, gup1)
    down1 = down_chain(branch1, act1)
    ga1, gb1, packed1, x1, x1s, gain_mlp1 = attn_back(1, e1, e1p, go1, after1, q1, k1, v1, probs1)
    x1p = other_core(x1s)
    order.drop(q1, k1, v1, probs1, go1)
    order.hold(ga1)
    attn1 = attn_chain(normed1, packed1, m1, m1p, gb1)
    order.drop(normed1, m1, m1p)
    up1.near()
    down1.near()
    grad_mix, go0, branch0, gup0, e0, e0s, gain_attn1 = call(
        mlp_back_kernel,
        [vm((R, D), F32), vm((R, D), F32), vm((R, D), BF), vm((R, FH), BF), vm((R, D), F32), vm((R, D), BF),
         vm((1, D), F32)],
        (place, alpha_mid, alpha_last, x1, x1p, ga1, stream1, attn_gains, cotangent, g_peer, slope0, w_up, w_down),
        [S_SPEC] * 3 + [V_SPEC] * 8 + [H_SPEC] * 2,
        [VMEM((D, FH), BF), VMEM((D, FH), BF), dma((2 * NCH,))], name="mlp_back",
    )
    e0p = other_core(e0s)
    order.drop(ga1, stream1, slope0)
    order.hold(go0, grad_mix)
    up0 = up_chain(nm0, gup0)
    down0 = down_chain(branch0, act0)
    order.drop(nm0, act0, up_order, down_order)
    attn1.near()
    up1.fin()
    down1.fin()
    ga0, gb0, packed0, x0, x0s, gain_mlp0 = attn_back(0, e0, e0p, go0, after0, q0, k0, v0, probs0)
    x0p = other_core(x0s)
    order.drop(q0, k0, v0, probs0, cos, sin, go0, after0)
    order.hold(x0, ga0)
    attn1.fin()
    attn0 = attn_chain(normed0, packed0, m0, m0p, gb0)
    order.drop(normed0, m0, m0p)
    up0.near()
    down0.near()
    history_grad, h_sums, f_sums = call(
        history_kernel, [jax.ShapeDtypeStruct((HIST, T, D), BF), vm((HIST, 3, D), F32), vm((2, D), F32)],
        (place, alpha_mid, alpha_last, history, cotangent, g_peer, grad_mix, block0, after1, part1),
        [S_SPEC] * 3 + [V_SPEC] * 7, [VMEM((T, D), F32)] * 2 + [VMEM((HIST, T, D), BF), dma((HIST,))],
        name="history_grad", out_specs=[H_SPEC, V_SPEC, V_SPEC],
    )
    order.drop(history)
    order.drop(grad_mix)
    vec = call(
        vector_kernel, vm((64, 128), F32), (h_sums, f_sums, inputs, in_peer, x0, place, gain_attn1, gain_mlp0, gain_mlp1),
        [V_SPEC] * 5 + [S_SPEC] + [V_SPEC] * 3, name="pack_sums",
    )
    got = trade(vec, attn_axes[0], 0)
    up0.fin()
    down0.fin()
    attn0.near(vec=[vec, got])
    up1.second(up0)
    down1.second(down0)
    input_grad, _ = call(
        with_token(input_grad_kernel), [jax.ShapeDtypeStruct((T, D), F32), vm((8, 128), F32)],
        (place, x0, x0p, ga0, inputs, attn_gains), [S_SPEC] + [V_SPEC] * 5, name="input_grad",
    )
    final, _ = call(
        with_token(final_kernel), [jax.ShapeDtypeStruct((T, D), BF), vm((8, 128), F32)],
        (place, alpha_last, h_last, block0, after1, part1, part1p),
        [S_SPEC] * 2 + [V_SPEC] * 5, name="final_mix",
    )
    order.drop(x0, ga0, block0, after1, part1, h_last)
    attn0.fin()
    attn1.second(attn0, vec=attn0.vec)
    up1.near()
    down1.near()
    attn1.near()
    down1.third(up1)
    attn1.third()
    down1.near()
    attn1.near()
    mlp_sum = down1.end()
    pairs = lambda n: pltpu.HBM((6, 2, n), F32)
    flat = lambda *shape: pltpu.HBM(shape, F32)
    token = vm((8, 128), F32)

    def packed(x):
        return other_core(
            call(pack_rows_kernel, vm((6, x.shape[1]), F32), (place, x), [S_SPEC, V_SPEC], name="pack_rows")
        )

    mlp_got = packed(mlp_sum)
    up_grad, down_grad, _ = call(
        with_token(write_mlp_kernel), [pairs(2 * FH), pairs(2 * FH), token], (place, mlp_sum, mlp_got),
        [S_SPEC] + [V_SPEC] * 2, name="write_mlp",
    )
    attn_sum, vec = attn1.end()
    vec_got = other_core(vec)
    attn_got = packed(attn_sum)
    qkv_grad, out_grad, attn_gains_grad, mlp_gains_grad, mid_grad, last_grad = call(
        write_attn_kernel,
        [pairs(3 * D), pairs(D), flat(2, D), flat(2, D), flat(1, HIST + 1), flat(1, HIST + 2)],
        (place, attn_sum, attn_got, vec, vec_got), [S_SPEC] + [V_SPEC] * 4, name="write_attn",
    )
    swap = lambda x: jnp.transpose(x, (1, 0, 2))
    return (
        final,
        input_grad,
        history_grad,
        mid_grad.reshape(HIST + 1),
        last_grad.reshape(HIST + 2),
        attn_gains_grad,
        mlp_gains_grad,
        swap(qkv_grad),
        swap(out_grad),
        swap(up_grad),
        swap(down_grad),
    )


def solution(mesh):
    both = P(("dp", "seq"), None)
    spread = P(None, ("dp", "seq"), None)
    return jax.shard_map(
        shards,
        mesh=mesh,
        in_specs=(both, spread) + (P(),) * 8 + (P("dp", None), both),
        out_specs=(both, both, spread) + (P(),) * 4 + (spread,) * 4,
        check_vma=False,
    )
```

```python
import math
from functools import partial

import jax
import jax.numpy as jnp
from jax import lax
from jax.experimental import pallas as pl
from jax.experimental.pallas import tpu as pltpu
from jax.sharding import PartitionSpec as P

BF = jnp.bfloat16
F32 = jnp.float32
NN = (((1,), (0,)), ((), ()))
NT = (((1,), (1,)), ((), ()))
TN = (((0,), (0,)), ((), ()))
EPS = 1e-5
MASKED = -1e30
ROT_BASE = 10000.0
HEAD = 64
GELU_C = math.sqrt(2.0 / math.pi)

R = 256
T = 128
D = 768
HW = 384
FH = 1536
CH = 512
NCH = FH // CH
HIST = 12
LN_ROWS = 64

VMEM = pltpu.VMEM
V_SPEC = pl.BlockSpec(memory_space=pltpu.VMEM)
S_SPEC = pl.BlockSpec(memory_space=pltpu.SMEM)
H_SPEC = pl.BlockSpec(memory_space=pl.ANY)
COSTS = {
    "attend_first": 2.0, "mlp_first": 2.0, "attend_second": 2.0, "mlp_last": 2.0, "attend_back": 8.0, "mlp_back": 8.0,
    "up_grad": 1.0, "down_grad": 1.0, "attn_grad": 1.0, "attn_parts": 1.0,
    "near_first": 1.5, "near_sum": 1.5, "axis_total": 0.5, "second_axis": 0.5, "third_axis": 1.5, "last_sum": 0.5,
}
LIMIT = 10 * 2**20


def dot(a, b, dims):
    return lax.dot_general(a, b, dims, preferred_element_type=F32)


def vm(shape, dtype):
    return pltpu.VMEM(shape, dtype)


class Order:
    def __init__(self):
        self.token = None
        self.held = []

    def hold(self, *arrays):
        self.held += arrays

    def drop(self, *arrays):
        self.held = [x for x in self.held if not any(x is y for y in arrays)]

    def call(self, kernel, outs, ins, in_specs, scratch=(), name=None, out_specs=None, after=()):
        many = isinstance(outs, (list, tuple))
        shapes = list(outs) if many else [outs]
        ins, in_specs = list(ins), list(in_specs)
        count = len(ins)
        after = list(after) + ([] if self.token is None else [self.token])
        in_specs += [H_SPEC] * len(after)
        kept = [x for x in self.held if not any(x is y for y in ins)]
        ins += after + kept
        in_specs += [V_SPEC] * len(kept)
        total = len(ins)
        ins = [pltpu.with_memory_space_constraint(x, VMEM) if spec is V_SPEC else x for x, spec in zip(ins, in_specs)]

        def body(*refs):
            kernel(*refs[:count], *refs[total:])

        result = pl.pallas_call(
            body,
            out_shape=shapes,
            in_specs=in_specs,
            out_specs=out_specs or [V_SPEC] * len(shapes),
            scratch_shapes=list(scratch),
            compiler_params=pltpu.CompilerParams(vmem_limit_bytes=LIMIT),
            cost_estimate=pl.CostEstimate(flops=int(1e9 * COSTS.get(name, 0.01)), bytes_accessed=1000, transcendentals=0),
            name=name,
        )(*ins)
        sizes = [math.prod(shape.shape) for shape in shapes]
        self.token = result[sizes.index(min(sizes))]
        return result if many else result[0]


def normalized(v):
    mean = jnp.mean(v, axis=-1, keepdims=True)
    shifted = v - mean
    var = jnp.mean(shifted * shifted, axis=-1, keepdims=True)
    rstd = lax.rsqrt(var + EPS)
    return shifted * rstd, rstd


def norm_back(v, e, gain):
    n, rstd = normalized(v)
    q = e * gain
    back = (
        q - jnp.mean(q, axis=-1, keepdims=True) - n * jnp.mean(q * n, axis=-1, keepdims=True)
    ) * rstd
    return back, jnp.sum(e * n, axis=0, keepdims=True)


def swap_halves(x):
    lane = lax.broadcasted_iota(jnp.int32, x.shape, 1) % HEAD
    return jnp.where(lane < HEAD // 2, pltpu.roll(x, 128 - 32, 1), pltpu.roll(x, 32, 1))


def head_lanes(shape, head):
    lane = lax.broadcasted_iota(jnp.int32, shape, 1)
    return (lane >= HEAD * head) & (lane < HEAD * (head + 1))


def first_place(lengths, t):
    second = lengths[0, 0]
    third = second + lengths[0, 1]
    return jnp.where(t >= third, third, jnp.where(t >= second, second, 0))


def allowed_block(lengths, half):
    shape = (T, T * (half + 1))
    t = lax.broadcasted_iota(jnp.int32, shape, 0) + T * half
    u = lax.broadcasted_iota(jnp.int32, shape, 1)
    first = first_place(lengths, lax.broadcasted_iota(jnp.int32, (T, 1), 0) + T * half)
    return (u >= first) & (u <= t)


def write_tables(lengths, cos, sin):
    t = lax.broadcasted_iota(jnp.int32, (R, 1), 0)
    offset = (t - first_place(lengths, t)).astype(F32)
    lane = lax.broadcasted_iota(jnp.int32, (1, 128), 1) % HEAD
    freq = jnp.exp((-math.log(ROT_BASE) * 2.0 / HEAD) * (lane % 32).astype(F32))
    angles = offset * freq
    cos[...] = jnp.cos(angles)
    sin[...] = jnp.sin(angles) * jnp.where(lane < 32, -1.0, 1.0)


def probs_columns(half):
    return slice(T * half, T * (2 * half + 1))


def softmax_block(q, k, allowed):
    scores = jnp.where(allowed, dot(q, k, NT), MASKED)
    top = jnp.max(scores, axis=-1, keepdims=True)
    weights = jnp.exp(scores - top)
    return weights * (1.0 / jnp.sum(weights, axis=-1, keepdims=True))


def gelu_and_slope(v):
    square = v * v
    t = jnp.tanh(GELU_C * v * (1.0 + 0.044715 * square))
    half = 0.5 * (1.0 + t)
    slope = half + 0.5 * v * (1.0 - t * t) * (GELU_C * (1.0 + 3.0 * 0.044715 * square))
    return v * half, slope


def qkv_copies(core, layer, w_qkv, wq, sem):
    return [
        pltpu.make_async_copy(
            w_qkv.at[layer, :, pl.ds(pl.multiple_of(D * j + HW * core, 128), HW)],
            wq.at[:, pl.ds(HW * j, HW)],
            sem.at[j],
        )
        for j in range(3)
    ]


def qkv_columns(w_qkv, layer, core, j, lo=0, width=HW):
    return w_qkv[layer, :, pl.ds(pl.multiple_of(D * j + HW * core + lo, 128), width)]


def out_rows(w_out, layer, part):
    return w_out[layer, pl.ds(pl.multiple_of(part * HW, 128), HW), :]


def ff_copies(core, layer, w, dst, sem, base):
    return [
        pltpu.make_async_copy(
            w.at[layer, :, pl.ds(pl.multiple_of(FH * core + CH * j, 128), CH)],
            dst.at[:, pl.ds(CH * j, CH)],
            sem.at[base + j],
        )
        for j in range(NCH)
    ]


def mix_kernel(am, al, history, mid, last):
    for r in range(0, T, 16):
        sl = slice(r, r + 16)
        acc_mid = jnp.zeros((16, D), F32)
        acc_last = jnp.zeros((16, D), F32)
        for k in range(HIST):
            h = history[k, sl, :].astype(F32)
            acc_mid += am[k] * h
            acc_last += al[k] * h
        mid[sl, :] = acc_mid
        last[sl, :] = acc_last


def attend_tail(layer, s_out, gain, columns, cos, sin, lengths, normed, q, k, v, mixed, probs_out):
    g = gain[layer : layer + 1, :]
    for r in range(0, R, LN_ROWS):
        sl = slice(r, r + LN_ROWS)
        n, _ = normalized(s_out[sl, :])
        normed[sl, :] = (n * g).astype(BF)
    x = normed[...]
    for j, dst in enumerate((q, k, v)):
        for p in range(HW // 128):
            lanes = slice(128 * p, 128 * (p + 1))
            packed = dot(x, columns(j, p), NN).astype(BF)
            if j == 2:
                dst[:, lanes] = packed
            else:
                f = packed.astype(F32)
                rot = f * cos[...] + swap_halves(f) * sin[...]
                if j == 0:
                    rot = rot * (1.0 / math.sqrt(HEAD))
                dst[:, lanes] = rot.astype(BF)
    for half in range(2):
        rows = slice(T * half, T * (half + 1))
        cols = slice(0, T * (half + 1))
        allowed = allowed_block(lengths, half)
        for p in range(HW // 128):
            lanes = slice(128 * p, 128 * (p + 1))
            qp = q[rows, lanes]
            kp = k[cols, lanes]
            vp = v[cols, lanes]
            acc = None
            for h in range(2):
                qh = jnp.where(head_lanes(qp.shape, h), qp, jnp.zeros_like(qp))
                vh = jnp.where(head_lanes(vp.shape, h), vp, jnp.zeros_like(vp))
                probs = softmax_block(qh, kp, allowed)
                probs_out[2 * p + h, :, probs_columns(half)] = probs
                part = dot(probs.astype(BF), vh, NN)
                acc = part if acc is None else acc + part
            mixed[rows, lanes] = acc.astype(BF)


def attend_first_kernel(place, lengths, inputs, peer, gains, w_qkv, stream, normed, q, k, v, mixed, probs,
                        cos, sin, own, gain, wq, sem):
    core = place[0]
    first = [pltpu.make_async_copy(inputs, own, sem.at[3]), pltpu.make_async_copy(gains, gain, sem.at[4])]
    copies = qkv_copies(core, 0, w_qkv, wq, sem)
    for cp in first + copies:
        cp.start()
    write_tables(lengths, cos, sin)
    for cp in first:
        cp.wait()
    stream[pl.ds(pl.multiple_of(core * T, T), T), :] = own[...].astype(F32)
    stream[pl.ds(pl.multiple_of((1 - core) * T, T), T), :] = peer[...].astype(F32)

    def columns(j, p):
        if p == 0:
            copies[j].wait()
        return wq[:, HW * j + 128 * p : HW * j + 128 * (p + 1)]

    attend_tail(0, stream, gain, columns, cos, sin, lengths, normed, q, k, v, mixed, probs)


def attend_second_kernel(place, am, after, p_own, p_peer, h_own, h_peer, gain, w_qkv, cos, sin, lengths,
                         stream, block, normed, q, k, v, mixed, probs):
    core = place[0]
    scale = am[HIST]
    stream[pl.ds(pl.multiple_of(core * T, T), T), :] = h_own[...]
    stream[pl.ds(pl.multiple_of((1 - core) * T, T), T), :] = h_peer[...]
    for r in range(0, R, LN_ROWS):
        sl = slice(r, r + LN_ROWS)
        b = after[sl, :] + (p_own[sl, :] + p_peer[sl, :].astype(F32))
        block[sl, :] = b
        stream[sl, :] = stream[sl, :] + scale * b
    columns = lambda j, p: qkv_columns(w_qkv, 1, core, j, 128 * p, 128)
    attend_tail(1, stream, gain, columns, cos, sin, lengths, normed, q, k, v, mixed, probs)


def mlp_front(core, layer, stream, m_own, m_peer, gain, after, normed, w_out):
    g = gain[layer : layer + 1, :]
    wo_own, wo_peer = out_rows(w_out, layer, core), out_rows(w_out, layer, 1 - core)
    for r in range(0, R, 128):
        sl = slice(r, r + 128)
        a = stream[sl, :] + (
            dot(m_own[sl, :], wo_own, NN) + dot(m_peer[sl, :], wo_peer, NN)
        )
        after[sl, :] = a
        n, _ = normalized(a)
        normed[sl, :] = (n * g).astype(BF)


def mlp_first_kernel(place, stream, m_own, m_peer, gain, w_out, w_up, w_down,
                     after, normed, act, slope, part, sent, wu, wd, sem):
    core = place[0]
    up_cp = ff_copies(core, 0, w_up, wu, sem, 0)
    down_cp = ff_copies(core, 0, w_down, wd, sem, NCH)
    for cp in up_cp + down_cp:
        cp.start()
    mlp_front(core, 0, stream, m_own, m_peer, gain, after, normed, w_out)
    x = normed[...]
    for j in range(NCH):
        up_cp[j].wait()
        for i in range(0, CH, 256):
            cols = slice(CH * j + i, CH * j + i + 256)
            u = dot(x, wu[:, cols], NN)
            a, s = gelu_and_slope(u)
            act[:, cols] = a.astype(BF)
            slope[:, cols] = s
    for cp in down_cp:
        cp.wait()
    total = dot(act[...], wd[...], NT)
    part[...] = total
    sent[...] = total.astype(BF)


def mlp_last_kernel(place, al, stream, m_own, m_peer, g_own, g_peer, gain, w_out, w_up, w_down,
                    after, normed, act, branch, gup, part, sent, go, down, down_sent, wu, wd, sem):
    core = place[0]
    up_cp = ff_copies(core, 1, w_up, wu, sem, 0)
    down_cp = ff_copies(core, 1, w_down, wd, sem, NCH)
    for cp in up_cp + down_cp:
        cp.start()
    scale = al[HIST + 1]
    own_rows = pl.ds(pl.multiple_of(core * T, T), T)
    peer_rows = pl.ds(pl.multiple_of((1 - core) * T, T), T)
    go[own_rows, :] = scale * g_own[...].astype(F32)
    go[peer_rows, :] = scale * g_peer[...].astype(F32)
    branch[...] = go[...].astype(BF)
    mlp_front(core, 1, stream, m_own, m_peer, gain, after, normed, w_out)
    x = normed[...]
    gb = branch[...]
    for j in range(NCH):
        up_cp[j].wait()
        down_cp[j].wait()
        for i in range(0, CH, 256):
            cols = slice(CH * j + i, CH * j + i + 256)
            u = dot(x, wu[:, cols], NN)
            a, s = gelu_and_slope(u)
            act[:, cols] = a.astype(BF)
            gup[:, cols] = (s * dot(gb, wd[:, cols], NN)).astype(BF)
    total = dot(gup[...], wu[...], NT)
    part[...] = total
    sent[...] = total.astype(BF)
    down[...] = dot(act[...], wd[...], NT)
    down_sent[...] = down[peer_rows, :].astype(BF)


def attend_back_kernel(layer, place, e_own, e_peer, go, after, gain, w_out, w_qkv, q, k, v, probs_in, cos, sin,
                       grad_after, grad_attn, grad_packed, part, sent, gain_grad, gm, acc):
    core = place[0]
    g = gain[layer : layer + 1, :]
    total = jnp.zeros((1, D), F32)
    for r in range(0, R, LN_ROWS):
        sl = slice(r, r + LN_ROWS)
        back, piece = norm_back(after[sl, :], e_own[sl, :] + e_peer[sl, :].astype(F32), g)
        total += piece
        ga = go[sl, :] + back
        grad_after[sl, :] = ga
        grad_attn[sl, :] = ga.astype(BF)
    gain_grad[...] = total
    gm[...] = dot(grad_attn[...], out_rows(w_out, layer, core), NT).astype(BF)
    scale = 1.0 / math.sqrt(HEAD)
    for p in range(HW // 128):
        lanes = slice(128 * p, 128 * (p + 1))
        for half in range(2):
            rows = slice(T * half, T * (half + 1))
            cols = slice(0, T * (half + 1))
            qp = q[rows, lanes]
            gp = gm[rows, lanes]
            kp = k[cols, lanes]
            vp = v[cols, lanes]
            dq = None
            for h in range(2):
                lane_q = head_lanes(qp.shape, h)
                qh = jnp.where(lane_q, qp, jnp.zeros_like(qp))
                gh = jnp.where(lane_q, gp, jnp.zeros_like(gp))
                kh = jnp.where(head_lanes(kp.shape, h), kp, jnp.zeros_like(kp))
                probs = probs_in[2 * p + h, :, probs_columns(half)]
                dprob = dot(gh, vp, NT)
                center = jnp.sum(probs * dprob, axis=-1, keepdims=True)
                ds = (probs * (dprob - center)).astype(BF)
                dqh = dot(ds, kh, NN)
                dkh = dot(ds, qh, TN)
                dvh = dot(probs.astype(BF), gh, TN)
                dq = dqh if dq is None else dq + dqh
                if half == 0 and h == 0:
                    dk, dv = dkh, dvh
                elif half == 0:
                    dk, dv = dk + dkh, dv + dvh
                    acc[0, :T, :] = dk
                    acc[1, :T, :] = dv
                elif h == 0:
                    dk, dv = dkh, dvh
                else:
                    dk, dv = dk + dkh, dv + dvh
            dq = dq * scale
            rot = dq * cos[rows, :] - swap_halves(dq) * sin[rows, :]
            grad_packed[rows, lanes] = rot.astype(BF)
        for half in range(2):
            rows = slice(T * half, T * (half + 1))
            dkr, dvr = dk[rows, :], dv[rows, :]
            if half == 0:
                dkr = dkr + acc[0, :T, :]
                dvr = dvr + acc[1, :T, :]
            rot = dkr * cos[rows, :] - swap_halves(dkr) * sin[rows, :]
            grad_packed[rows, HW + 128 * p : HW + 128 * (p + 1)] = rot.astype(BF)
            grad_packed[rows, 2 * HW + 128 * p : 2 * HW + 128 * (p + 1)] = dvr.astype(BF)
    total = dot(grad_packed[:, :HW], qkv_columns(w_qkv, layer, core, 0), NT)
    for j in range(1, 3):
        total += dot(grad_packed[:, HW * j : HW * (j + 1)], qkv_columns(w_qkv, layer, core, j), NT)
    part[...] = total
    if layer == 0:
        sent[...] = part[pl.ds(pl.multiple_of((1 - core) * T, T), T), :].astype(BF)
    else:
        sent[...] = total.astype(BF)


def mlp_back_kernel(place, am, al, e_own, e_peer, grad_after, stream, gain, g_own, g_peer, slope, w_up, w_down,
                    grad_mix, go, branch, gup, part, sent, gain_grad, wu, wd, sem):
    core = place[0]
    down_cp = ff_copies(core, 0, w_down, wd, sem, 0)
    up_cp = ff_copies(core, 0, w_up, wu, sem, NCH)
    for cp in down_cp + up_cp:
        cp.start()
    a_last = al[HIST]
    a_mid = am[HIST]
    go[pl.ds(pl.multiple_of(core * T, T), T), :] = a_last * g_own[...].astype(F32)
    go[pl.ds(pl.multiple_of((1 - core) * T, T), T), :] = a_last * g_peer[...].astype(F32)
    g = gain[1:2, :]
    total = jnp.zeros((1, D), F32)
    for r in range(0, R, LN_ROWS):
        sl = slice(r, r + LN_ROWS)
        back, piece = norm_back(stream[sl, :], e_own[sl, :] + e_peer[sl, :].astype(F32), g)
        total += piece
        gx = grad_after[sl, :] + back
        grad_mix[sl, :] = gx
        out = go[sl, :] + a_mid * gx
        go[sl, :] = out
        branch[sl, :] = out.astype(BF)
    gain_grad[...] = total
    gb = branch[...]
    for j in range(NCH):
        down_cp[j].wait()
        for i in range(0, CH, 256):
            cols = slice(CH * j + i, CH * j + i + 256)
            gup[:, cols] = (slope[:, cols] * dot(gb, wd[:, cols], NN)).astype(BF)
    for cp in up_cp:
        cp.wait()
    total = dot(gup[...], wu[...], NT)
    part[...] = total
    sent[...] = total.astype(BF)


def relations(place, axis):
    here = place[1 + axis]
    near = 1 + 2 * place[0]
    far = 3 - 2 * place[0]
    return here, here ^ far, here ^ near, here ^ 2


def rows_at(index, size):
    return pl.ds(pl.multiple_of(index * size, 16), size)


def split_rows(place, axis, grad, keep, send):
    for slot, quarter in enumerate(relations(place, axis)):
        dst = (keep, send)[slot // 2]
        dst[slot % 2] = grad[rows_at(quarter, 192), :]


def row_order_kernel(all_axes, place, *outs):
    r = lax.broadcasted_iota(jnp.int32, (1, D), 1)
    for axes, out in zip(all_axes, outs):
        slots = relations(place, axes[0])
        first = jnp.where(r < 192, slots[0], jnp.where(r < 384, slots[1], jnp.where(r < 576, slots[2], slots[3])))
        digit = {axes[0]: first, axes[1]: (r // 48) % 4, axes[2]: (r // 12) % 4}
        source = 12 * (16 * digit[0] + 4 * digit[1] + digit[2]) + r % 12
        for base in range(0, D, 64):
            row = lax.broadcasted_iota(jnp.int32, (64, D), 0) + base
            out[base : base + 64, :] = jnp.where(row == source, 1.0, 0.0).astype(BF)


def ordered_grad_kernel(x, order, y, keep, send):
    ordered = dot(x[...], order[...], NN).astype(BF)
    for j, dst in enumerate((keep, send)):
        half = dot(ordered[:, 384 * j : 384 * (j + 1)], y[...], TN).astype(BF)
        dst[0] = half[:192]
        dst[1] = half[192:]


def attn_grad_kernel(place, normed, grad_packed, m_own, m_peer, grad_attn, keep, send, grad):
    core = place[0]
    grad[:, : 3 * HW] = dot(normed[...], grad_packed[...], TN).astype(BF)
    ga = grad_attn[:, pl.ds(pl.multiple_of(HW * core, 128), HW)]
    grad[rows_at(core, HW), 3 * HW :] = dot(m_own[...], ga, TN).astype(BF)
    grad[rows_at(1 - core, HW), 3 * HW :] = dot(m_peer[...], ga, TN).astype(BF)
    split_rows(place, 0, grad, keep, send)


def attn_parts_kernel(place, normed, grad_packed, m_own, m_peer, grad_attn, by_x, by_z,
                      keep_a, send_a, keep_b, send_b, keep_c, send_c, grad):
    core = place[0]
    x = normed[...]
    grad[...] = dot(x, grad_packed[:, : 2 * HW], TN).astype(BF)
    split_rows(place, 0, grad, keep_a, send_a)
    values = dot(x, by_x[...], NN).astype(BF)
    mixed = (dot(m_own[...], by_z[rows_at(core, HW), :], NN) + dot(m_peer[...], by_z[rows_at(1 - core, HW), :], NN)).astype(BF)
    ga = grad_attn[:, pl.ds(pl.multiple_of(HW * core, 128), HW)]
    for left, right, keep, send in (
        (values, grad_packed[:, 2 * HW :], keep_b, send_b),
        (mixed, ga, keep_c, send_c),
    ):
        for j, dst in enumerate((keep, send)):
            half = dot(left[:, 384 * j : 384 * (j + 1)], right, TN).astype(BF)
            dst[0] = half[:192]
            dst[1] = half[192:]


def add_kernel(a, b, out):
    out[...] = a[...] + b[...]


def encode(vec, dst, row):
    rest = vec
    for c in range(3):
        piece = rest.astype(BF)
        rest = rest - piece.astype(F32)
        for j in range(4):
            lanes = slice(128 * (4 * c + j), 128 * (4 * c + j + 1))
            dst[row : row + 16, lanes] = piece[16 * j : 16 * (j + 1), :]


def decode(src, row):
    parts = []
    for j in range(4):
        block = [src[row : row + 16, 128 * (4 * c + j) : 128 * (4 * c + j + 1)].astype(F32) for c in range(3)]
        parts.append((block[0] + block[1]) + block[2])
    return jnp.concatenate(parts, axis=0)


def near_first_kernel(with_vec, *refs):
    if with_vec:
        keep, got, vec, vec_got, out, vec_out = refs
        total = vec[...] + vec_got[...]
        vec_out[...] = total
        encode(total, out, 192)
    else:
        keep, got, out = refs
    out[0:192, :] = (keep[1].astype(F32) + got[1].astype(F32)).astype(BF)


def near_kernel(rows, with_vec, *refs):
    if with_vec:
        keep, got, vec, out, vec_out = refs
        total = vec[...] + decode(got, 2 * rows)
        vec_out[...] = total
        encode(total, out, rows)
    else:
        keep, got, out = refs
    out[0:rows, :] = (keep[1].astype(F32) + got[rows : 2 * rows, :].astype(F32)).astype(BF)


def last_kernel(with_vec, *refs):
    if with_vec:
        keep, got, got2, vec, out, vec_out = refs
        vec_out[...] = vec[...] + decode(got2, 16)
    else:
        keep, got, got2, out = refs
    out[...] = keep[0, 0:12, :].astype(F32) + got[0:12, :].astype(F32) + got2[0:12, :].astype(F32)


def axis_total_kernel(with_vec, *refs):
    if with_vec:
        keep, got, got2, vec, out, vec_out = refs
        vec_out[...] = vec[...] + decode(got2, 192)
    else:
        keep, got, got2, out = refs
    out[...] = (keep[0].astype(F32) + got[0].astype(F32) + got2[0:192, :].astype(F32)).astype(BF)


def second_axis_kernel(axis, widths, with_vec, place, *refs):
    keep, send = refs[-2:]
    if with_vec:
        encode(refs[len(widths)][...], send, 96)
    for slot, index in enumerate(relations(place, axis)):
        lo = 0
        for total, width in zip(refs, widths):
            lanes = slice(lo, lo + width)
            lo += width
            value = total[rows_at(index, 48), :]
            if slot < 2:
                keep[slot, :, lanes] = value
            else:
                send[48 * (slot - 2) : 48 * (slot - 1), lanes] = value


def third_axis_kernel(axis, widths, with_vec, place, *refs):
    count = 3 * len(widths)
    keep, send = refs[count + with_vec : count + with_vec + 2]
    scr = refs[-1]
    lo = 0
    for j, width in enumerate(widths):
        kept, got, got2 = refs[3 * j : 3 * j + 3]
        total = kept[0].astype(F32) + got[0:48, :].astype(F32) + got2[0:48, :].astype(F32)
        for i in range(4):
            scr[i, 0:12, lo : lo + width] = total[12 * i : 12 * (i + 1), :]
            scr[i, 12:16, lo : lo + width] = jnp.zeros((4, width), F32)
        lo += width
    for slot, index in enumerate(relations(place, axis)):
        value = scr[index].astype(BF)
        if slot < 2:
            keep[slot] = value
        else:
            send[16 * (slot - 2) : 16 * (slot - 1), :] = value
    if with_vec:
        vec, vec_out = refs[count], refs[-2]
        total = vec[...] + decode(refs[2], 48)
        vec_out[...] = total
        encode(total, send, 32)


def pack_rows_kernel(place, *refs):
    out = refs[-1]
    lo = 0
    for ref in refs[:-1]:
        width = ref.shape[1]
        out[:, lo : lo + width] = jnp.where(place[0] == 0, ref[6:12, :], ref[0:6, :])
        lo += width


def with_token(kernel):
    def body(*refs):
        kernel(*refs[:-1])
        refs[-1][...] = jnp.zeros_like(refs[-1])

    return body


def put(dst, layer, lo, value):
    for row in range(6):
        dst[row, layer : layer + 1, lo : lo + value.shape[1]] = value[row : row + 1, :]


def both_cores(first, ref, got):
    own = jnp.where(first, ref[0:6, :], ref[6:12, :])
    other = got[...]
    return jnp.where(first, own, other), jnp.where(first, other, own)


def write_mlp_kernel(place, down, up, got, up_out, down_out, value_out, attn_out_out):
    first = place[0] == 0
    width = 2 * FH + HW
    for ref, other, dst, rest in (
        (down, got.at[:, :width], down_out, value_out),
        (up, got.at[:, width : 2 * width], up_out, attn_out_out),
    ):
        for c, both in enumerate(both_cores(first, ref, other)):
            for layer in range(2):
                put(dst, layer, FH * c, both[:, FH * (1 - layer) : FH * (2 - layer)])
            rest[:, HW * c : HW * (c + 1)] = both[:, 2 * FH :]


def write_attn_kernel(place, attn, got, vec, vec_got, value_in, out_in,
                      qkv_out, out_out, attn_gains, mlp_gains, mid_out, last_out):
    for c, both in enumerate(both_cores(place[0] == 0, attn, got.at[:, 2 * (2 * FH + HW) :])):
        for i in range(3):
            put(qkv_out, 1, D * i + HW * c, both[:, HW * i : HW * (i + 1)])
        put(out_out, 1, HW * c, both[:, 3 * HW : 4 * HW])
        for i in range(2):
            put(qkv_out, 0, D * i + HW * c, both[:, FH + HW * i : FH + HW * (i + 1)])
    put(qkv_out, 0, 2 * D, value_in[...])
    put(out_out, 0, 0, out_in[...])
    total = vec[...] + vec_got[...]
    for j in range(D // 128):
        lanes = slice(128 * j, 128 * (j + 1))
        attn_gains[:, lanes] = total[4 * j : 4 * j + 2, :]
        mlp_gains[:, lanes] = total[4 * j + 2 : 4 * j + 4, :]
    for dst, base, count in ((mid_out, 24, HIST + 1), (last_out, 37, HIST + 2)):
        lane = lax.broadcasted_iota(jnp.int32, (1, 128), 1)
        row = jnp.zeros((1, 128), F32)
        for i in range(count):
            row = jnp.where(lane == i, total[base + i : base + i + 1, :], row)
        dst[...] = row[:, :count]


def input_grad_kernel(place, e_part, e_peer, grad_after, own, gain, out):
    core = place[0]
    rows = pl.ds(pl.multiple_of(core * T, T), T)
    back, _ = norm_back(own[...].astype(F32), e_part[rows, :] + e_peer[...].astype(F32), gain[0:1, :])
    out[...] = grad_after[rows, :] + back


def final_kernel(place, al, h_last, block, after, p_own, p_peer, out):
    core = place[0]
    rows = pl.ds(pl.multiple_of(core * T, T), T)
    b_last = after[rows, :] + (p_own[rows, :] + p_peer[...].astype(F32))
    out[...] = (h_last[...] + al[HIST] * block[rows, :] + al[HIST + 1] * b_last).astype(BF)


def history_kernel(place, am, al, history, g_own, g_peer, grad_mix, block, after, part, out, sums, f_sums, g32, gm32, staged,
                   sem):
    own = pl.ds(pl.multiple_of(place[0] * T, T), T)
    peer = pl.ds(pl.multiple_of((1 - place[0]) * T, T), T)
    g32[...] = g_own[...].astype(F32)
    gm32[...] = grad_mix[own, :]
    copies = []
    for k in range(HIST):
        mid = jnp.zeros((8, D), F32)
        last = jnp.zeros((8, D), F32)
        for r in range(0, T, 16):
            sl = slice(r, r + 16)
            gm, g = gm32[sl, :], g32[sl, :]
            staged[k, sl, :] = (al[k] * g + am[k] * gm).astype(BF)
            h = history[k, sl, :].astype(F32)
            a, b = h * gm, h * g
            mid += a[:8] + a[8:]
            last += b[:8] + b[8:]
        copies.append(pltpu.make_async_copy(staged.at[k], out.at[k], sem.at[k]))
        copies[k].start()
        sums[k, 0:1, :] = jnp.sum(mid, axis=0, keepdims=True)
        sums[k, 1:2, :] = jnp.sum(last, axis=0, keepdims=True)
    b_own = block[own, :]
    sums[0, 2:3, :] = jnp.sum(b_own * gm32[...], axis=0, keepdims=True)
    f_sums[0:1, :] = jnp.sum(g32[...] * b_own, axis=0, keepdims=True)
    f_sums[1:2, :] = jnp.sum(g32[...] * (after[own, :] + part[own, :]), axis=0, keepdims=True) + jnp.sum(
        g_peer[...].astype(F32) * part[peer, :], axis=0, keepdims=True
    )
    for copy in copies:
        copy.wait()


def vector_kernel(h_sums, f_sums, own, peer, x_part, place, ga1, gm0, gm1, out):
    ga0 = jnp.zeros((1, D), F32)
    for ref, core in ((own, place[0]), (peer, 1 - place[0])):
        n, _ = normalized(ref[...].astype(F32))
        ga0 += jnp.sum(x_part[pl.ds(pl.multiple_of(core * T, T), T), :] * n, axis=0, keepdims=True)
    for j in range(D // 128):
        lanes = slice(128 * j, 128 * (j + 1))
        out[4 * j : 4 * j + 1, :] = ga0[:, lanes]
        out[4 * j + 1 : 4 * j + 2, :] = 0.5 * ga1[:, lanes]
        out[4 * j + 2 : 4 * j + 3, :] = 0.5 * gm0[:, lanes]
        out[4 * j + 3 : 4 * j + 4, :] = 0.5 * gm1[:, lanes]
    for k in range(HIST):
        out[24 + k : 25 + k, :] = jnp.broadcast_to(
            jnp.sum(h_sums[k, 0:1, :], axis=-1, keepdims=True), (1, 128)
        )
        out[37 + k : 38 + k, :] = jnp.broadcast_to(
            jnp.sum(h_sums[k, 1:2, :], axis=-1, keepdims=True), (1, 128)
        )
    out[36:37, :] = jnp.broadcast_to(jnp.sum(h_sums[0, 2:3, :], axis=-1, keepdims=True), (1, 128))
    out[49:51, :] = jnp.broadcast_to(jnp.sum(f_sums[...], axis=-1, keepdims=True), (2, 128))
    out[51:64, :] = jnp.zeros((13, 128), F32)


def coords(i):
    return [i // 16, (i // 4) % 4, i % 4]


def partner_pairs(axis, step):
    pairs = []
    for chip in range(64):
        for core in range(2):
            flip = (1, 3)[(step + core) % 2]
            there = coords(chip)
            there[axis] ^= flip
            pairs.append((2 * chip + core, 2 * (there[0] * 16 + there[1] * 4 + there[2]) + core))
    return pairs


def trade(x, axis, step):
    return lax.ppermute(x, ("dp", "seq"), partner_pairs(axis, step))


class Chain:
    def __init__(self, order, place, axes, keep, send):
        self.order, self.place, self.axes = order, place, axes
        self.phase, self.vec = 0, None
        self.send_first(keep, send)

    def send_first(self, keep, send):
        self.keep = keep
        self.order.hold(keep)
        self.got = trade(send, self.axes[self.phase], 0)

    def near(self, vec=None):
        width = self.keep.shape[2]
        self.order.hold(self.got)
        if self.phase == 0:
            ins, outs = [self.keep, self.got], [vm((192, width), BF)]
            if vec is not None:
                ins += vec
                outs = [vm((208, width), BF), vm((64, 128), F32)]
            result = self.order.call(
                partial(near_first_kernel, vec is not None), outs, ins, [V_SPEC] * len(ins), name="near_first"
            )
            other = result[0]
            if vec is not None:
                self.vec = result[1]
        else:
            rows = (48, 16)[self.phase - 1]
            ins, outs = [self.keep, self.got], [vm((rows, width), BF)]
            if self.vec is not None:
                ins.append(self.vec)
                outs = [vm((rows + 16, width), BF), vm((64, 128), F32)]
            result = self.order.call(
                partial(near_kernel, rows, self.vec is not None), outs, ins, [V_SPEC] * len(ins), name="near_sum"
            )
            other = result[0]
            if self.vec is not None:
                self.vec = result[1]
        self.got2 = trade(other, self.axes[self.phase], 1)

    def fin(self):
        width = self.keep.shape[2]
        self.order.drop(self.keep, self.got)
        ins, outs = [self.keep, self.got, self.got2], [vm((192, width), BF)]
        if self.vec is not None:
            ins.append(self.vec)
            outs.append(vm((64, 128), F32))
        result = self.order.call(
            partial(axis_total_kernel, self.vec is not None), outs, ins, [V_SPEC] * len(ins), name="axis_total"
        )
        self.total = result[0]
        if self.vec is not None:
            self.vec = result[1]
        self.order.hold(self.total)

    def second(self, *joined, vec=None):
        self.order.drop(*[part.total for part in (self,) + joined])
        ins = [part.total for part in (self,) + joined]
        widths = [x.shape[1] for x in ins]
        total = sum(widths)
        if vec is not None:
            ins.append(vec)
            self.vec = vec
        keep, send = self.order.call(
            partial(second_axis_kernel, self.axes[1], widths, vec is not None),
            [vm((2, 48, total), BF), vm((112 if vec is not None else 96, total), BF)],
            [self.place] + ins, [S_SPEC] + [V_SPEC] * len(ins), name="second_axis",
        )
        self.phase = 1
        self.send_first(keep, send)

    def third(self, *joined):
        parts = (self,) + joined
        for part in parts:
            self.order.drop(part.keep, part.got)
        widths = [part.keep.shape[2] for part in parts]
        width = sum(widths)
        ins = [x for part in parts for x in (part.keep, part.got, part.got2)]
        outs = [vm((2, 16, width), BF), vm((32, width), BF)]
        if self.vec is not None:
            ins.append(self.vec)
            outs = [vm((2, 16, width), BF), vm((48, width), BF), vm((64, 128), F32)]
        result = self.order.call(
            partial(third_axis_kernel, self.axes[2], widths, self.vec is not None), outs, [self.place] + ins,
            [S_SPEC] + [V_SPEC] * len(ins), [VMEM((4, 16, width), F32)], name="third_axis",
        )
        if self.vec is not None:
            self.vec = result[2]
        self.phase = 2
        self.send_first(result[0], result[1])

    def end(self):
        self.order.drop(self.keep, self.got)
        ins, outs = [self.keep, self.got, self.got2], [vm((12, self.keep.shape[2]), F32)]
        if self.vec is not None:
            ins.append(self.vec)
            outs.append(vm((64, 128), F32))
        result = self.order.call(
            partial(last_kernel, self.vec is not None), outs, ins, [V_SPEC] * len(ins), name="last_sum"
        )
        return result if self.vec is not None else result[0]


def other_core(x):
    return lax.ppermute(x, "seq", [(0, 1), (1, 0)])


def shards(inputs, history, alpha_mid, alpha_last, attn_gains, mlp_gains, w_qkv, w_out, w_up, w_down,
           doc_lengths, cotangent):
    core = lax.axis_index("seq")
    chip = lax.axis_index("dp")
    place = jnp.stack([core, chip // 16, (chip // 4) % 4, chip % 4]).astype(jnp.int32)
    w_up, w_down, w_qkv_hbm = (pltpu.with_memory_space_constraint(w, pltpu.HBM) for w in (w_up, w_down, w_qkv))
    order = Order()
    call = order.call
    lengths = doc_lengths
    up_axes, down_axes, attn_axes = (2, 0, 1), (1, 2, 0), (0, 1, 2)
    in_peer = other_core(inputs)
    g_peer = other_core(cotangent)

    dma = pltpu.SemaphoreType.DMA
    inputs_hbm, gains_hbm = (pltpu.with_memory_space_constraint(x, pltpu.HBM) for x in (inputs, attn_gains))
    att_out = [vm((R, D), BF)] + [vm((R, HW), BF)] * 4 + [vm((2 * HW // 128, T, 3 * T), F32)]
    stream0, normed0, q0, k0, v0, m0, probs0, cos, sin = call(
        attend_first_kernel, [vm((R, D), F32)] + att_out + [vm((R, 128), F32)] * 2,
        (place, lengths, inputs_hbm, in_peer, gains_hbm, w_qkv_hbm),
        [S_SPEC] * 2 + [H_SPEC, V_SPEC, H_SPEC, H_SPEC],
        [VMEM((T, D), BF), VMEM((2, D), F32), VMEM((D, 3 * HW), BF), dma((5,))], name="attend_first",
    )
    m0p = other_core(m0)
    order.hold(normed0, q0, k0, v0, probs0, cos, sin, m0, history)
    h_mid, h_last = call(
        mix_kernel, [vm((T, D), F32)] * 2, (alpha_mid, alpha_last, history), [S_SPEC, S_SPEC, V_SPEC],
        name="mix_history",
    )
    h_peer = other_core(h_mid)
    order.drop(history)
    order.hold(h_last, w_out)
    order.hold(inputs, in_peer, cotangent, g_peer, attn_gains, mlp_gains)
    mlp_scratch = [VMEM((D, FH), BF), VMEM((D, FH), BF), dma((2 * NCH,))]
    after0, nm0, act0, slope0, part0, part0s = call(
        mlp_first_kernel,
        [vm((R, D), F32), vm((R, D), BF), vm((R, FH), BF), vm((R, FH), F32), vm((R, D), F32), vm((R, D), BF)],
        (place, stream0, m0, m0p, mlp_gains, w_out, w_up, w_down),
        [S_SPEC] + [V_SPEC] * 5 + [H_SPEC] * 2, mlp_scratch, name="mlp_first",
        after=(g_peer,),
    )
    part0p = other_core(part0s)
    up_order, down_order = call(
        partial(row_order_kernel, (up_axes, down_axes)), [vm((D, D), BF)] * 2, (place,), [S_SPEC], name="row_order"
    )
    order.hold(up_order, down_order)
    order.hold(m0p, w_qkv)
    order.hold(after0, nm0, act0, slope0)
    stream1, block0, normed1, q1, k1, v1, m1, probs1 = call(
        attend_second_kernel, [vm((R, D), F32)] * 2 + att_out,
        (place, alpha_mid, after0, part0, part0p, h_mid, h_peer, attn_gains, w_qkv, cos, sin, lengths),
        [S_SPEC, S_SPEC] + [V_SPEC] * 9 + [S_SPEC], name="attend_second",
    )
    m1p = other_core(m1)
    order.hold(block0, stream1, normed1, q1, k1, v1, probs1)
    after1, nm1, act1, branch1, gup1, e1, e1s, go1, part1, part1s = call(
        mlp_last_kernel,
        [vm((R, D), F32), vm((R, D), BF), vm((R, FH), BF), vm((R, D), BF), vm((R, FH), BF), vm((R, D), F32),
         vm((R, D), BF), vm((R, D), F32), vm((R, D), F32), vm((T, D), BF)],
        (place, alpha_last, stream1, m1, m1p, cotangent, g_peer, mlp_gains, w_out, w_up, w_down),
        [S_SPEC, S_SPEC] + [V_SPEC] * 7 + [H_SPEC] * 2, mlp_scratch, name="mlp_last",
    )
    e1p = other_core(e1s)
    part1p = other_core(part1s)
    order.hold(m1, m1p, after1, go1, part1, part1s)

    quarter = vm((2, 192, FH), BF)
    whole_grad = [VMEM((D, FH), BF)]

    def ordered_chain(axes, x, rows, y, name):
        keep, send = call(
            ordered_grad_kernel, [quarter] * 2, (x, rows, y), [V_SPEC] * 3, name=name,
        )
        return Chain(order, place, axes, keep, send)

    def down_chain(branch, act):
        return ordered_chain(down_axes, branch, down_order, act, "down_grad")

    def up_chain(nm, gup):
        return ordered_chain(up_axes, nm, up_order, gup, "up_grad")

    def attn_chain(normed, packed, m, mp, ga):
        keep, send = call(
            attn_grad_kernel, [quarter] * 2, (place, normed, packed, m, mp, ga), [S_SPEC] + [V_SPEC] * 5, whole_grad,
            name="attn_grad",
        )
        return Chain(order, place, attn_axes, keep, send)

    def attn_parts(normed, packed, m, mp, ga):
        widths = (2 * HW, HW, HW)
        refs = call(
            attn_parts_kernel, [vm((2, 192, w), BF) for w in widths for _ in range(2)],
            (place, normed, packed, m, mp, ga, down_order, up_order), [S_SPEC] + [V_SPEC] * 7,
            [VMEM((D, 2 * HW), BF)], name="attn_parts",
        )
        axes = (attn_axes, down_axes, up_axes)
        return [Chain(order, place, a, refs[2 * j], refs[2 * j + 1]) for j, a in enumerate(axes)]

    def attn_back(layer, e, ep, go, after, q, k, v, probs):
        return call(
            partial(attend_back_kernel, layer),
            [vm((R, D), F32), vm((R, D), BF), vm((R, 3 * HW), BF), vm((R, D), F32), vm((R if layer else T, D), BF),
             vm((1, D), F32)],
            (place, e, ep, go, after, mlp_gains, w_out, w_qkv, q, k, v, probs, cos, sin),
            [S_SPEC] + [V_SPEC] * 13, [VMEM((R, HW), BF), VMEM((2, T, 128), F32)],
            name="attend_back",
        )

    up1 = up_chain(nm1, gup1)
    down1 = down_chain(branch1, act1)
    ga1, gb1, packed1, x1, x1s, gain_mlp1 = attn_back(1, e1, e1p, go1, after1, q1, k1, v1, probs1)
    x1p = other_core(x1s)
    order.drop(q1, k1, v1, probs1, go1)
    order.hold(ga1)
    attn1 = attn_chain(normed1, packed1, m1, m1p, gb1)
    order.drop(normed1, m1, m1p)
    up1.near()
    down1.near()
    grad_mix, go0, branch0, gup0, e0, e0s, gain_attn1 = call(
        mlp_back_kernel,
        [vm((R, D), F32), vm((R, D), F32), vm((R, D), BF), vm((R, FH), BF), vm((R, D), F32), vm((R, D), BF),
         vm((1, D), F32)],
        (place, alpha_mid, alpha_last, x1, x1p, ga1, stream1, attn_gains, cotangent, g_peer, slope0, w_up, w_down),
        [S_SPEC] * 3 + [V_SPEC] * 8 + [H_SPEC] * 2,
        [VMEM((D, FH), BF), VMEM((D, FH), BF), dma((2 * NCH,))], name="mlp_back",
    )
    e0p = other_core(e0s)
    order.drop(ga1, stream1, slope0)
    order.hold(go0, grad_mix)
    up0 = up_chain(nm0, gup0)
    down0 = down_chain(branch0, act0)
    order.drop(nm0, act0)
    attn1.near()
    up1.fin()
    down1.fin()
    ga0, gb0, packed0, x0, x0s, gain_mlp0 = attn_back(0, e0, e0p, go0, after0, q0, k0, v0, probs0)
    x0p = other_core(x0s)
    order.drop(q0, k0, v0, probs0, cos, sin, go0, after0, w_qkv, w_out)
    order.hold(x0, ga0)
    attn1.fin()
    part_a, part_b, part_c = attn_parts(normed0, packed0, m0, m0p, gb0)
    order.drop(normed0, m0, m0p, up_order, down_order)
    up0.near()
    down0.near()
    history_grad, h_sums, f_sums = call(
        history_kernel, [jax.ShapeDtypeStruct((HIST, T, D), BF), vm((HIST, 3, D), F32), vm((2, D), F32)],
        (place, alpha_mid, alpha_last, history, cotangent, g_peer, grad_mix, block0, after1, part1),
        [S_SPEC] * 3 + [V_SPEC] * 7, [VMEM((T, D), F32)] * 2 + [VMEM((HIST, T, D), BF), dma((HIST,))],
        name="history_grad", out_specs=[H_SPEC, V_SPEC, V_SPEC],
    )
    order.drop(grad_mix, history)
    part_a.near()
    part_b.near()
    part_c.near()
    up0.fin()
    down0.fin()
    vec = call(
        vector_kernel, vm((64, 128), F32), (h_sums, f_sums, inputs, in_peer, x0, place, gain_attn1, gain_mlp0, gain_mlp1),
        [V_SPEC] * 5 + [S_SPEC] + [V_SPEC] * 3, name="pack_sums",
    )
    got = trade(vec, attn_axes[0], 0)
    part_a.fin()
    part_b.fin()
    part_c.fin()
    vec = call(add_kernel, vm((64, 128), F32), (vec, got), [V_SPEC] * 2, name="add_sums")
    got = trade(vec, attn_axes[0], 1)
    down1.second(down0, part_b)
    up1.second(up0, part_c)
    input_grad, _ = call(
        with_token(input_grad_kernel), [jax.ShapeDtypeStruct((T, D), F32), vm((8, 128), F32)],
        (place, x0, x0p, ga0, inputs, attn_gains), [S_SPEC] + [V_SPEC] * 5, name="input_grad",
    )
    final, _ = call(
        with_token(final_kernel), [jax.ShapeDtypeStruct((T, D), BF), vm((8, 128), F32)],
        (place, alpha_last, h_last, block0, after1, part1, part1p),
        [S_SPEC] * 2 + [V_SPEC] * 5, name="final_mix",
    )
    vec = call(add_kernel, vm((64, 128), F32), (vec, got), [V_SPEC] * 2, name="add_sums")
    attn1.second(part_a, vec=vec)
    order.drop(x0, ga0, block0, after1, part1, h_last)
    chains = (down1, up1, attn1)
    for chain in chains:
        chain.near()
    for chain in chains:
        chain.third()
    for chain in chains:
        chain.near()
    down_sum, up_sum = down1.end(), up1.end()
    attn_sum, vec = attn1.end()
    vec_got = other_core(vec)
    pairs = lambda n: pltpu.HBM((6, 2, n), F32)
    flat = lambda *shape: pltpu.HBM(shape, F32)
    sums = (down_sum, up_sum, attn_sum)
    packed = call(
        pack_rows_kernel, vm((6, sum(x.shape[1] for x in sums)), F32), (place,) + sums, [S_SPEC] + [V_SPEC] * 3,
        name="pack_rows",
    )
    got = other_core(packed)
    up_grad, down_grad, value_grad, attn_out_grad = call(
        write_mlp_kernel, [pairs(2 * FH), pairs(2 * FH), vm((6, D), F32), vm((6, D), F32)],
        (place, down_sum, up_sum, got), [S_SPEC] + [V_SPEC] * 3, name="write_mlp",
    )
    qkv_grad, out_grad, attn_gains_grad, mlp_gains_grad, mid_grad, last_grad = call(
        write_attn_kernel,
        [pairs(3 * D), pairs(D), flat(2, D), flat(2, D), flat(1, HIST + 1), flat(1, HIST + 2)],
        (place, attn_sum, got, vec, vec_got, value_grad, attn_out_grad), [S_SPEC] + [V_SPEC] * 6,
        name="write_attn",
    )
    swap = lambda x: jnp.transpose(x, (1, 0, 2))
    return (
        final,
        input_grad,
        history_grad,
        mid_grad.reshape(HIST + 1),
        last_grad.reshape(HIST + 2),
        attn_gains_grad,
        mlp_gains_grad,
        swap(qkv_grad),
        swap(out_grad),
        swap(up_grad),
        swap(down_grad),
    )


def solution(mesh):
    both = P(("dp", "seq"), None)
    spread = P(None, ("dp", "seq"), None)
    return jax.shard_map(
        shards,
        mesh=mesh,
        in_specs=(both, spread) + (P(),) * 8 + (P("dp", None), both),
        out_specs=(both, both, spread) + (P(),) * 4 + (spread,) * 4,
        check_vma=False,
    )
```

```python
import math
from functools import partial

import jax
import jax.numpy as jnp
from jax import lax
from jax.experimental import pallas as pl
from jax.experimental.pallas import tpu as pltpu
from jax.sharding import PartitionSpec as P

BF = jnp.bfloat16
F32 = jnp.float32
NN = (((1,), (0,)), ((), ()))
NT = (((1,), (1,)), ((), ()))
TN = (((0,), (0,)), ((), ()))
EPS = 1e-5
MASKED = -1e30
ROT_BASE = 10000.0
HEAD = 64
GELU_C = math.sqrt(2.0 / math.pi)

R = 256
T = 128
D = 768
HW = 384
FH = 1536
CH = 512
NCH = FH // CH
HIST = 12
LN_ROWS = 64

VMEM = pltpu.VMEM
V_SPEC = pl.BlockSpec(memory_space=pltpu.VMEM)
S_SPEC = pl.BlockSpec(memory_space=pltpu.SMEM)
H_SPEC = pl.BlockSpec(memory_space=pl.ANY)
COSTS = {
    "attend_first": 2.0, "mlp_first": 2.0, "attend_second": 2.0, "mlp_last": 2.0, "attend_back": 8.0, "mlp_back": 8.0,
    "up_grad": 1.0, "down_grad": 1.0, "attn_grad": 1.0, "attn_parts": 1.0,
    "near_first": 1.5, "near_sum": 1.5, "axis_total": 0.5, "second_axis": 0.5, "third_axis": 1.5, "last_sum": 0.5,
}
LIMIT = 10 * 2**20


def dot(a, b, dims):
    return lax.dot_general(a, b, dims, preferred_element_type=F32)


def vm(shape, dtype):
    return pltpu.VMEM(shape, dtype)


class Order:
    def __init__(self):
        self.token = None
        self.held = []

    def hold(self, *arrays):
        self.held += arrays

    def drop(self, *arrays):
        self.held = [x for x in self.held if not any(x is y for y in arrays)]

    def call(self, kernel, outs, ins, in_specs, scratch=(), name=None, out_specs=None, after=()):
        many = isinstance(outs, (list, tuple))
        shapes = list(outs) if many else [outs]
        ins, in_specs = list(ins), list(in_specs)
        count = len(ins)
        after = list(after) + ([] if self.token is None else [self.token])
        in_specs += [H_SPEC] * len(after)
        kept = [x for x in self.held if not any(x is y for y in ins)]
        ins += after + kept
        in_specs += [V_SPEC] * len(kept)
        total = len(ins)
        ins = [pltpu.with_memory_space_constraint(x, VMEM) if spec is V_SPEC else x for x, spec in zip(ins, in_specs)]

        def body(*refs):
            kernel(*refs[:count], *refs[total:])

        result = pl.pallas_call(
            body,
            out_shape=shapes,
            in_specs=in_specs,
            out_specs=out_specs or [V_SPEC] * len(shapes),
            scratch_shapes=list(scratch),
            compiler_params=pltpu.CompilerParams(vmem_limit_bytes=LIMIT),
            cost_estimate=pl.CostEstimate(flops=int(1e9 * COSTS.get(name, 0.01)), bytes_accessed=1000, transcendentals=0),
            name=name,
        )(*ins)
        sizes = [math.prod(shape.shape) for shape in shapes]
        self.token = result[sizes.index(min(sizes))]
        return result if many else result[0]


def normalized(v):
    mean = jnp.mean(v, axis=-1, keepdims=True)
    shifted = v - mean
    var = jnp.mean(shifted * shifted, axis=-1, keepdims=True)
    rstd = lax.rsqrt(var + EPS)
    return shifted * rstd, rstd


def norm_back(v, e, gain):
    n, rstd = normalized(v)
    q = e * gain
    back = (
        q - jnp.mean(q, axis=-1, keepdims=True) - n * jnp.mean(q * n, axis=-1, keepdims=True)
    ) * rstd
    return back, jnp.sum(e * n, axis=0, keepdims=True)


def swap_halves(x):
    lane = lax.broadcasted_iota(jnp.int32, x.shape, 1) % HEAD
    return jnp.where(lane < HEAD // 2, pltpu.roll(x, 128 - 32, 1), pltpu.roll(x, 32, 1))


def head_lanes(shape, head):
    lane = lax.broadcasted_iota(jnp.int32, shape, 1)
    return (lane >= HEAD * head) & (lane < HEAD * (head + 1))


def first_place(lengths, t):
    second = lengths[0, 0]
    third = second + lengths[0, 1]
    return jnp.where(t >= third, third, jnp.where(t >= second, second, 0))


def allowed_block(lengths, half):
    shape = (T, T * (half + 1))
    t = lax.broadcasted_iota(jnp.int32, shape, 0) + T * half
    u = lax.broadcasted_iota(jnp.int32, shape, 1)
    first = first_place(lengths, lax.broadcasted_iota(jnp.int32, (T, 1), 0) + T * half)
    return (u >= first) & (u <= t)


def write_tables(lengths, cos, sin):
    t = lax.broadcasted_iota(jnp.int32, (R, 1), 0)
    offset = (t - first_place(lengths, t)).astype(F32)
    lane = lax.broadcasted_iota(jnp.int32, (1, 128), 1) % HEAD
    freq = jnp.exp((-math.log(ROT_BASE) * 2.0 / HEAD) * (lane % 32).astype(F32))
    angles = offset * freq
    cos[...] = jnp.cos(angles)
    sin[...] = jnp.sin(angles) * jnp.where(lane < 32, -1.0, 1.0)


def probs_columns(half):
    return slice(T * half, T * (2 * half + 1))


def softmax_block(q, k, allowed):
    scores = jnp.where(allowed, dot(q, k, NT), MASKED)
    top = jnp.max(scores, axis=-1, keepdims=True)
    weights = jnp.exp(scores - top)
    return weights * (1.0 / jnp.sum(weights, axis=-1, keepdims=True))


def gelu_and_slope(v):
    square = v * v
    t = jnp.tanh(GELU_C * v * (1.0 + 0.044715 * square))
    half = 0.5 * (1.0 + t)
    slope = half + 0.5 * v * (1.0 - t * t) * (GELU_C * (1.0 + 3.0 * 0.044715 * square))
    return v * half, slope


def qkv_copies(core, layer, w_qkv, wq, sem):
    return [
        pltpu.make_async_copy(
            w_qkv.at[layer, :, pl.ds(pl.multiple_of(D * j + HW * core, 128), HW)],
            wq.at[:, pl.ds(HW * j, HW)],
            sem.at[j],
        )
        for j in range(3)
    ]


def qkv_columns(w_qkv, layer, core, j, lo=0, width=HW):
    return w_qkv[layer, :, pl.ds(pl.multiple_of(D * j + HW * core + lo, 128), width)]


def out_rows(w_out, layer, part):
    return w_out[layer, pl.ds(pl.multiple_of(part * HW, 128), HW), :]


def ff_copies(core, layer, w, dst, sem, base):
    return [
        pltpu.make_async_copy(
            w.at[layer, :, pl.ds(pl.multiple_of(FH * core + CH * j, 128), CH)],
            dst.at[:, pl.ds(CH * j, CH)],
            sem.at[base + j],
        )
        for j in range(NCH)
    ]


def mix_kernel(am, al, history, mid, last):
    for r in range(0, T, 16):
        sl = slice(r, r + 16)
        acc_mid = jnp.zeros((16, D), F32)
        acc_last = jnp.zeros((16, D), F32)
        for k in range(HIST):
            h = history[k, sl, :].astype(F32)
            acc_mid += am[k] * h
            acc_last += al[k] * h
        mid[sl, :] = acc_mid
        last[sl, :] = acc_last


def attend_tail(layer, s_out, gain, columns, cos, sin, lengths, normed, q, k, v, mixed, probs_out):
    g = gain[layer : layer + 1, :]
    for r in range(0, R, LN_ROWS):
        sl = slice(r, r + LN_ROWS)
        n, _ = normalized(s_out[sl, :])
        normed[sl, :] = (n * g).astype(BF)
    x = normed[...]
    for j, dst in enumerate((q, k, v)):
        for p in range(HW // 128):
            lanes = slice(128 * p, 128 * (p + 1))
            packed = dot(x, columns(j, p), NN).astype(BF)
            if j == 2:
                dst[:, lanes] = packed
            else:
                f = packed.astype(F32)
                rot = f * cos[...] + swap_halves(f) * sin[...]
                if j == 0:
                    rot = rot * (1.0 / math.sqrt(HEAD))
                dst[:, lanes] = rot.astype(BF)
    for half in range(2):
        rows = slice(T * half, T * (half + 1))
        cols = slice(0, T * (half + 1))
        allowed = allowed_block(lengths, half)
        for p in range(HW // 128):
            lanes = slice(128 * p, 128 * (p + 1))
            qp = q[rows, lanes]
            kp = k[cols, lanes]
            vp = v[cols, lanes]
            acc = None
            for h in range(2):
                qh = jnp.where(head_lanes(qp.shape, h), qp, jnp.zeros_like(qp))
                vh = jnp.where(head_lanes(vp.shape, h), vp, jnp.zeros_like(vp))
                probs = softmax_block(qh, kp, allowed)
                probs_out[2 * p + h, :, probs_columns(half)] = probs
                part = dot(probs.astype(BF), vh, NN)
                acc = part if acc is None else acc + part
            mixed[rows, lanes] = acc.astype(BF)


def attend_first_kernel(place, lengths, inputs, peer, gains, w_qkv, stream, normed, q, k, v, mixed, probs,
                        cos, sin, own, gain, wq, sem):
    core = place[0]
    first = [pltpu.make_async_copy(inputs, own, sem.at[3]), pltpu.make_async_copy(gains, gain, sem.at[4])]
    copies = qkv_copies(core, 0, w_qkv, wq, sem)
    for cp in first + copies:
        cp.start()
    write_tables(lengths, cos, sin)
    for cp in first:
        cp.wait()
    stream[pl.ds(pl.multiple_of(core * T, T), T), :] = own[...].astype(F32)
    stream[pl.ds(pl.multiple_of((1 - core) * T, T), T), :] = peer[...].astype(F32)

    def columns(j, p):
        if p == 0:
            copies[j].wait()
        return wq[:, HW * j + 128 * p : HW * j + 128 * (p + 1)]

    attend_tail(0, stream, gain, columns, cos, sin, lengths, normed, q, k, v, mixed, probs)


def attend_second_kernel(place, am, after, p_own, p_peer, h_own, h_peer, gain, w_qkv, cos, sin, lengths,
                         stream, block, normed, q, k, v, mixed, probs):
    core = place[0]
    scale = am[HIST]
    stream[pl.ds(pl.multiple_of(core * T, T), T), :] = h_own[...]
    stream[pl.ds(pl.multiple_of((1 - core) * T, T), T), :] = h_peer[...]
    for r in range(0, R, LN_ROWS):
        sl = slice(r, r + LN_ROWS)
        b = after[sl, :] + (p_own[sl, :] + p_peer[sl, :].astype(F32))
        block[sl, :] = b
        stream[sl, :] = stream[sl, :] + scale * b
    columns = lambda j, p: qkv_columns(w_qkv, 1, core, j, 128 * p, 128)
    attend_tail(1, stream, gain, columns, cos, sin, lengths, normed, q, k, v, mixed, probs)


def mlp_front(core, layer, stream, m_own, m_peer, gain, after, normed, w_out):
    g = gain[layer : layer + 1, :]
    wo_own, wo_peer = out_rows(w_out, layer, core), out_rows(w_out, layer, 1 - core)
    for r in range(0, R, 128):
        sl = slice(r, r + 128)
        a = stream[sl, :] + (
            dot(m_own[sl, :], wo_own, NN) + dot(m_peer[sl, :], wo_peer, NN)
        )
        after[sl, :] = a
        n, _ = normalized(a)
        normed[sl, :] = (n * g).astype(BF)


def mlp_first_kernel(place, stream, m_own, m_peer, gain, w_out, w_up, w_down,
                     after, normed, act, slope, part, sent, wu, wd, sem):
    core = place[0]
    up_cp = ff_copies(core, 0, w_up, wu, sem, 0)
    down_cp = ff_copies(core, 0, w_down, wd, sem, NCH)
    for cp in up_cp + down_cp:
        cp.start()
    mlp_front(core, 0, stream, m_own, m_peer, gain, after, normed, w_out)
    x = normed[...]
    for j in range(NCH):
        up_cp[j].wait()
        for i in range(0, CH, 256):
            cols = slice(CH * j + i, CH * j + i + 256)
            u = dot(x, wu[:, cols], NN)
            a, s = gelu_and_slope(u)
            act[:, cols] = a.astype(BF)
            slope[:, cols] = s
    for cp in down_cp:
        cp.wait()
    total = dot(act[...], wd[...], NT)
    part[...] = total
    sent[...] = total.astype(BF)


def mlp_last_kernel(place, al, stream, m_own, m_peer, g_own, g_peer, gain, w_out, w_up, w_down,
                    after, normed, act, branch, gup, part, sent, go, down, down_sent, wu, wd, sem):
    core = place[0]
    up_cp = ff_copies(core, 1, w_up, wu, sem, 0)
    down_cp = ff_copies(core, 1, w_down, wd, sem, NCH)
    for pair in zip(up_cp, down_cp):
        for cp in pair:
            cp.start()
    scale = al[HIST + 1]
    own_rows = pl.ds(pl.multiple_of(core * T, T), T)
    peer_rows = pl.ds(pl.multiple_of((1 - core) * T, T), T)
    go[own_rows, :] = scale * g_own[...].astype(F32)
    go[peer_rows, :] = scale * g_peer[...].astype(F32)
    branch[...] = go[...].astype(BF)
    mlp_front(core, 1, stream, m_own, m_peer, gain, after, normed, w_out)
    x = normed[...]
    gb = branch[...]
    for j in range(NCH):
        up_cp[j].wait()
        down_cp[j].wait()
        for i in range(0, CH, 256):
            cols = slice(CH * j + i, CH * j + i + 256)
            u = dot(x, wu[:, cols], NN)
            a, s = gelu_and_slope(u)
            act[:, cols] = a.astype(BF)
            gup[:, cols] = (s * dot(gb, wd[:, cols], NN)).astype(BF)
    total = dot(gup[...], wu[...], NT)
    part[...] = total
    sent[...] = total.astype(BF)
    down[...] = dot(act[...], wd[...], NT)
    down_sent[...] = down[peer_rows, :].astype(BF)


def attend_back_kernel(layer, place, e_own, e_peer, go, after, gain, w_out, w_qkv, q, k, v, probs_in, cos, sin,
                       grad_after, grad_attn, grad_packed, part, sent, gain_grad, gm, acc):
    core = place[0]
    g = gain[layer : layer + 1, :]
    total = jnp.zeros((1, D), F32)
    for r in range(0, R, LN_ROWS):
        sl = slice(r, r + LN_ROWS)
        back, piece = norm_back(after[sl, :], e_own[sl, :] + e_peer[sl, :].astype(F32), g)
        total += piece
        ga = go[sl, :] + back
        grad_after[sl, :] = ga
        grad_attn[sl, :] = ga.astype(BF)
    gain_grad[...] = total
    gm[...] = dot(grad_attn[...], out_rows(w_out, layer, core), NT).astype(BF)
    scale = 1.0 / math.sqrt(HEAD)
    for p in range(HW // 128):
        lanes = slice(128 * p, 128 * (p + 1))
        for half in range(2):
            rows = slice(T * half, T * (half + 1))
            cols = slice(0, T * (half + 1))
            qp = q[rows, lanes]
            gp = gm[rows, lanes]
            kp = k[cols, lanes]
            vp = v[cols, lanes]
            dq = None
            for h in range(2):
                lane_q = head_lanes(qp.shape, h)
                qh = jnp.where(lane_q, qp, jnp.zeros_like(qp))
                gh = jnp.where(lane_q, gp, jnp.zeros_like(gp))
                kh = jnp.where(head_lanes(kp.shape, h), kp, jnp.zeros_like(kp))
                probs = probs_in[2 * p + h, :, probs_columns(half)]
                dprob = dot(gh, vp, NT)
                center = jnp.sum(probs * dprob, axis=-1, keepdims=True)
                ds = (probs * (dprob - center)).astype(BF)
                dqh = dot(ds, kh, NN)
                dkh = dot(ds, qh, TN)
                dvh = dot(probs.astype(BF), gh, TN)
                dq = dqh if dq is None else dq + dqh
                if half == 0 and h == 0:
                    dk, dv = dkh, dvh
                elif half == 0:
                    dk, dv = dk + dkh, dv + dvh
                    acc[0, :T, :] = dk
                    acc[1, :T, :] = dv
                elif h == 0:
                    dk, dv = dkh, dvh
                else:
                    dk, dv = dk + dkh, dv + dvh
            dq = dq * scale
            rot = dq * cos[rows, :] - swap_halves(dq) * sin[rows, :]
            grad_packed[rows, lanes] = rot.astype(BF)
        for half in range(2):
            rows = slice(T * half, T * (half + 1))
            dkr, dvr = dk[rows, :], dv[rows, :]
            if half == 0:
                dkr = dkr + acc[0, :T, :]
                dvr = dvr + acc[1, :T, :]
            rot = dkr * cos[rows, :] - swap_halves(dkr) * sin[rows, :]
            grad_packed[rows, HW + 128 * p : HW + 128 * (p + 1)] = rot.astype(BF)
            grad_packed[rows, 2 * HW + 128 * p : 2 * HW + 128 * (p + 1)] = dvr.astype(BF)
    total = dot(grad_packed[:, :HW], qkv_columns(w_qkv, layer, core, 0), NT)
    for j in range(1, 3):
        total += dot(grad_packed[:, HW * j : HW * (j + 1)], qkv_columns(w_qkv, layer, core, j), NT)
    part[...] = total
    if layer == 0:
        sent[...] = part[pl.ds(pl.multiple_of((1 - core) * T, T), T), :].astype(BF)
    else:
        sent[...] = total.astype(BF)


def mlp_back_kernel(place, am, al, e_own, e_peer, grad_after, stream, gain, g_own, g_peer, slope, w_up, w_down,
                    grad_mix, go, branch, gup, part, sent, gain_grad, wu, wd, sem):
    core = place[0]
    down_cp = ff_copies(core, 0, w_down, wd, sem, 0)
    up_cp = ff_copies(core, 0, w_up, wu, sem, NCH)
    for cp in down_cp + up_cp:
        cp.start()
    a_last = al[HIST]
    a_mid = am[HIST]
    go[pl.ds(pl.multiple_of(core * T, T), T), :] = a_last * g_own[...].astype(F32)
    go[pl.ds(pl.multiple_of((1 - core) * T, T), T), :] = a_last * g_peer[...].astype(F32)
    g = gain[1:2, :]
    total = jnp.zeros((1, D), F32)
    for r in range(0, R, LN_ROWS):
        sl = slice(r, r + LN_ROWS)
        back, piece = norm_back(stream[sl, :], e_own[sl, :] + e_peer[sl, :].astype(F32), g)
        total += piece
        gx = grad_after[sl, :] + back
        grad_mix[sl, :] = gx
        out = go[sl, :] + a_mid * gx
        go[sl, :] = out
        branch[sl, :] = out.astype(BF)
    gain_grad[...] = total
    gb = branch[...]
    for j in range(NCH):
        down_cp[j].wait()
        for i in range(0, CH, 256):
            cols = slice(CH * j + i, CH * j + i + 256)
            gup[:, cols] = (slope[:, cols] * dot(gb, wd[:, cols], NN)).astype(BF)
    for cp in up_cp:
        cp.wait()
    total = dot(gup[...], wu[...], NT)
    part[...] = total
    sent[...] = total.astype(BF)


def relations(place, axis):
    here = place[1 + axis]
    near = 1 + 2 * place[0]
    far = 3 - 2 * place[0]
    return here, here ^ far, here ^ near, here ^ 2


def rows_at(index, size):
    return pl.ds(pl.multiple_of(index * size, 16), size)


def split_rows(place, axis, grad, keep, send):
    for slot, quarter in enumerate(relations(place, axis)):
        dst = (keep, send)[slot // 2]
        dst[slot % 2] = grad[rows_at(quarter, 192), :]


def row_order_kernel(all_axes, place, *outs):
    r = lax.broadcasted_iota(jnp.int32, (1, D), 1)
    for axes, out in zip(all_axes, outs):
        slots = relations(place, axes[0])
        first = jnp.where(r < 192, slots[0], jnp.where(r < 384, slots[1], jnp.where(r < 576, slots[2], slots[3])))
        digit = {axes[0]: first, axes[1]: (r // 48) % 4, axes[2]: (r // 12) % 4}
        source = 12 * (16 * digit[0] + 4 * digit[1] + digit[2]) + r % 12
        for base in range(0, D, 64):
            row = lax.broadcasted_iota(jnp.int32, (64, D), 0) + base
            out[base : base + 64, :] = jnp.where(row == source, 1.0, 0.0).astype(BF)


def ordered_grad_kernel(x, order, y, keep, send):
    ordered = dot(x[...], order[...], NN).astype(BF)
    for j, dst in enumerate((keep, send)):
        half = dot(ordered[:, 384 * j : 384 * (j + 1)], y[...], TN).astype(BF)
        dst[0] = half[:192]
        dst[1] = half[192:]


def attn_grad_kernel(place, normed, grad_packed, m_own, m_peer, grad_attn, keep, send, grad):
    core = place[0]
    grad[:, : 3 * HW] = dot(normed[...], grad_packed[...], TN).astype(BF)
    ga = grad_attn[:, pl.ds(pl.multiple_of(HW * core, 128), HW)]
    grad[rows_at(core, HW), 3 * HW :] = dot(m_own[...], ga, TN).astype(BF)
    grad[rows_at(1 - core, HW), 3 * HW :] = dot(m_peer[...], ga, TN).astype(BF)
    split_rows(place, 0, grad, keep, send)


def attn_parts_kernel(place, normed, grad_packed, m_own, m_peer, grad_attn, by_x, by_z,
                      keep_a, send_a, keep_b, send_b, keep_c, send_c, grad):
    core = place[0]
    x = normed[...]
    grad[...] = dot(x, grad_packed[:, : 2 * HW], TN).astype(BF)
    split_rows(place, 0, grad, keep_a, send_a)
    values = dot(x, by_x[...], NN).astype(BF)
    mixed = (dot(m_own[...], by_z[rows_at(core, HW), :], NN) + dot(m_peer[...], by_z[rows_at(1 - core, HW), :], NN)).astype(BF)
    ga = grad_attn[:, pl.ds(pl.multiple_of(HW * core, 128), HW)]
    for left, right, keep, send in (
        (values, grad_packed[:, 2 * HW :], keep_b, send_b),
        (mixed, ga, keep_c, send_c),
    ):
        for j, dst in enumerate((keep, send)):
            half = dot(left[:, 384 * j : 384 * (j + 1)], right, TN).astype(BF)
            dst[0] = half[:192]
            dst[1] = half[192:]


def vec_rows(width):
    return 16 * math.ceil(12 * 128 / width)


def vec_tile(ref, row, c, j):
    per = ref.shape[1] // 128
    down, right = (4 * c + j) // per, (4 * c + j) % per
    return slice(row + 16 * down, row + 16 * (down + 1)), slice(128 * right, 128 * (right + 1))


def encode(vec, dst, row):
    rest = vec
    for c in range(3):
        piece = rest.astype(BF)
        rest = rest - piece.astype(F32)
        for j in range(4):
            dst[vec_tile(dst, row, c, j)] = piece[16 * j : 16 * (j + 1), :]


def decode(src, row):
    parts = []
    for j in range(4):
        block = [src[vec_tile(src, row, c, j)].astype(F32) for c in range(3)]
        parts.append((block[0] + block[1]) + block[2])
    return jnp.concatenate(parts, axis=0)


def near_first_kernel(with_vec, *refs):
    if with_vec:
        keep, got, vec, vec_got, out, vec_out = refs
        total = vec[...] + vec_got[...]
        vec_out[...] = total
        encode(total, out, 192)
    else:
        keep, got, out = refs
    out[0:192, :] = (keep[1].astype(F32) + got[1].astype(F32)).astype(BF)


def near_kernel(rows, with_vec, *refs):
    if with_vec:
        keep, got, vec, out, vec_out = refs
        total = vec[...] + decode(got, 2 * rows)
        vec_out[...] = total
        encode(total, out, rows)
    else:
        keep, got, out = refs
    out[0:rows, :] = (keep[1].astype(F32) + got[rows : 2 * rows, :].astype(F32)).astype(BF)


def last_kernel(with_vec, *refs):
    if with_vec:
        keep, got, got2, vec, out, vec_out = refs
        vec_out[...] = vec[...] + decode(got2, 16)
    else:
        keep, got, got2, out = refs
    out[...] = keep[0, 0:12, :].astype(F32) + got[0:12, :].astype(F32) + got2[0:12, :].astype(F32)


def axis_total_kernel(with_vec, *refs):
    if with_vec:
        keep, got, got2, vec, out, vec_out = refs
        vec_out[...] = vec[...] + decode(got2, 192)
    else:
        keep, got, got2, out = refs
    out[...] = (keep[0].astype(F32) + got[0].astype(F32) + got2[0:192, :].astype(F32)).astype(BF)


def second_axis_kernel(axis, widths, with_vec, place, *refs):
    keep, send = refs[-2:]
    if with_vec:
        encode(refs[len(widths)][...], send, 96)
    for slot, index in enumerate(relations(place, axis)):
        lo = 0
        for total, width in zip(refs, widths):
            lanes = slice(lo, lo + width)
            lo += width
            value = total[rows_at(index, 48), :]
            if slot < 2:
                keep[slot, :, lanes] = value
            else:
                send[48 * (slot - 2) : 48 * (slot - 1), lanes] = value


def third_axis_kernel(axis, widths, with_vec, place, *refs):
    count = 3 * len(widths)
    keep, send = refs[count + with_vec : count + with_vec + 2]
    scr = refs[-1]
    lo = 0
    for j, width in enumerate(widths):
        kept, got, got2 = refs[3 * j : 3 * j + 3]
        total = kept[0].astype(F32) + got[0:48, :].astype(F32) + got2[0:48, :].astype(F32)
        for i in range(4):
            scr[i, 0:12, lo : lo + width] = total[12 * i : 12 * (i + 1), :]
            scr[i, 12:16, lo : lo + width] = jnp.zeros((4, width), F32)
        lo += width
    for slot, index in enumerate(relations(place, axis)):
        value = scr[index].astype(BF)
        if slot < 2:
            keep[slot] = value
        else:
            send[16 * (slot - 2) : 16 * (slot - 1), :] = value
    if with_vec:
        vec, vec_out = refs[count], refs[-2]
        total = vec[...] + decode(refs[2], 48)
        vec_out[...] = total
        encode(total, send, 32)


def pack_rows_kernel(place, *refs):
    out = refs[-1]
    lo = 0
    for ref in refs[:-1]:
        width = ref.shape[1]
        out[:, lo : lo + width] = jnp.where(place[0] == 0, ref[6:12, :], ref[0:6, :])
        lo += width


def with_token(kernel):
    def body(*refs):
        kernel(*refs[:-1])
        refs[-1][...] = jnp.zeros_like(refs[-1])

    return body


def put(dst, layer, lo, value):
    for row in range(6):
        dst[row, layer : layer + 1, lo : lo + value.shape[1]] = value[row : row + 1, :]


def both_cores(first, ref, got):
    own = jnp.where(first, ref[0:6, :], ref[6:12, :])
    other = got[...]
    return jnp.where(first, own, other), jnp.where(first, other, own)


def write_mlp_kernel(place, down, up, got, up_out, down_out, value_out, attn_out_out):
    first = place[0] == 0
    width = 2 * FH + HW
    for ref, other, dst, rest in (
        (down, got.at[:, :width], down_out, value_out),
        (up, got.at[:, width : 2 * width], up_out, attn_out_out),
    ):
        for c, both in enumerate(both_cores(first, ref, other)):
            for layer in range(2):
                put(dst, layer, FH * c, both[:, FH * (1 - layer) : FH * (2 - layer)])
            rest[:, HW * c : HW * (c + 1)] = both[:, 2 * FH :]


def write_attn_kernel(place, attn, got, vec, vec_got, value_in, out_in,
                      qkv_out, out_out, attn_gains, mlp_gains, mid_out, last_out):
    for c, both in enumerate(both_cores(place[0] == 0, attn, got.at[:, 2 * (2 * FH + HW) :])):
        for i in range(3):
            put(qkv_out, 1, D * i + HW * c, both[:, HW * i : HW * (i + 1)])
        put(out_out, 1, HW * c, both[:, 3 * HW : 4 * HW])
        for i in range(2):
            put(qkv_out, 0, D * i + HW * c, both[:, FH + HW * i : FH + HW * (i + 1)])
    put(qkv_out, 0, 2 * D, value_in[...])
    put(out_out, 0, 0, out_in[...])
    total = vec[...] + vec_got[...]
    for j in range(D // 128):
        lanes = slice(128 * j, 128 * (j + 1))
        attn_gains[:, lanes] = total[4 * j : 4 * j + 2, :]
        mlp_gains[:, lanes] = total[4 * j + 2 : 4 * j + 4, :]
    for dst, base, count in ((mid_out, 24, HIST + 1), (last_out, 37, HIST + 2)):
        lane = lax.broadcasted_iota(jnp.int32, (1, 128), 1)
        row = jnp.zeros((1, 128), F32)
        for i in range(count):
            row = jnp.where(lane == i, total[base + i : base + i + 1, :], row)
        dst[...] = row[:, :count]


def input_grad_kernel(place, e_part, e_peer, grad_after, own, gain, out):
    core = place[0]
    rows = pl.ds(pl.multiple_of(core * T, T), T)
    back, _ = norm_back(own[...].astype(F32), e_part[rows, :] + e_peer[...].astype(F32), gain[0:1, :])
    out[...] = grad_after[rows, :] + back


def final_kernel(place, al, h_last, block, after, p_own, p_peer, out):
    core = place[0]
    rows = pl.ds(pl.multiple_of(core * T, T), T)
    b_last = after[rows, :] + (p_own[rows, :] + p_peer[...].astype(F32))
    out[...] = (h_last[...] + al[HIST] * block[rows, :] + al[HIST + 1] * b_last).astype(BF)


def history_kernel(place, am, al, history, g_own, g_peer, grad_mix, block, after, part, out, sums, f_sums, g32, gm32, staged,
                   sem):
    own = pl.ds(pl.multiple_of(place[0] * T, T), T)
    peer = pl.ds(pl.multiple_of((1 - place[0]) * T, T), T)
    g32[...] = g_own[...].astype(F32)
    gm32[...] = grad_mix[own, :]
    copies = []
    for k in range(HIST):
        mid = jnp.zeros((8, D), F32)
        last = jnp.zeros((8, D), F32)
        for r in range(0, T, 16):
            sl = slice(r, r + 16)
            gm, g = gm32[sl, :], g32[sl, :]
            staged[k, sl, :] = (al[k] * g + am[k] * gm).astype(BF)
            h = history[k, sl, :].astype(F32)
            a, b = h * gm, h * g
            mid += a[:8] + a[8:]
            last += b[:8] + b[8:]
        copies.append(pltpu.make_async_copy(staged.at[k], out.at[k], sem.at[k]))
        copies[k].start()
        sums[k, 0:1, :] = jnp.sum(mid, axis=0, keepdims=True)
        sums[k, 1:2, :] = jnp.sum(last, axis=0, keepdims=True)
    b_own = block[own, :]
    sums[0, 2:3, :] = jnp.sum(b_own * gm32[...], axis=0, keepdims=True)
    f_sums[0:1, :] = jnp.sum(g32[...] * b_own, axis=0, keepdims=True)
    f_sums[1:2, :] = jnp.sum(g32[...] * (after[own, :] + part[own, :]), axis=0, keepdims=True) + jnp.sum(
        g_peer[...].astype(F32) * part[peer, :], axis=0, keepdims=True
    )
    for copy in copies:
        copy.wait()


def vector_kernel(h_sums, f_sums, own, peer, x_part, place, ga1, gm0, gm1, out):
    ga0 = jnp.zeros((1, D), F32)
    for ref, core in ((own, place[0]), (peer, 1 - place[0])):
        n, _ = normalized(ref[...].astype(F32))
        ga0 += jnp.sum(x_part[pl.ds(pl.multiple_of(core * T, T), T), :] * n, axis=0, keepdims=True)
    for j in range(D // 128):
        lanes = slice(128 * j, 128 * (j + 1))
        out[4 * j : 4 * j + 1, :] = ga0[:, lanes]
        out[4 * j + 1 : 4 * j + 2, :] = 0.5 * ga1[:, lanes]
        out[4 * j + 2 : 4 * j + 3, :] = 0.5 * gm0[:, lanes]
        out[4 * j + 3 : 4 * j + 4, :] = 0.5 * gm1[:, lanes]
    for k in range(HIST):
        out[24 + k : 25 + k, :] = jnp.broadcast_to(
            jnp.sum(h_sums[k, 0:1, :], axis=-1, keepdims=True), (1, 128)
        )
        out[37 + k : 38 + k, :] = jnp.broadcast_to(
            jnp.sum(h_sums[k, 1:2, :], axis=-1, keepdims=True), (1, 128)
        )
    out[36:37, :] = jnp.broadcast_to(jnp.sum(h_sums[0, 2:3, :], axis=-1, keepdims=True), (1, 128))
    out[49:51, :] = jnp.broadcast_to(jnp.sum(f_sums[...], axis=-1, keepdims=True), (2, 128))
    out[51:64, :] = jnp.zeros((13, 128), F32)


def coords(i):
    return [i // 16, (i // 4) % 4, i % 4]


def partner_pairs(axis, step):
    pairs = []
    for chip in range(64):
        for core in range(2):
            flip = (1, 3)[(step + core) % 2]
            there = coords(chip)
            there[axis] ^= flip
            pairs.append((2 * chip + core, 2 * (there[0] * 16 + there[1] * 4 + there[2]) + core))
    return pairs


def trade(x, axis, step):
    return lax.ppermute(x, ("dp", "seq"), partner_pairs(axis, step))


class Chain:
    def __init__(self, order, place, axes, keep, send):
        self.order, self.place, self.axes = order, place, axes
        self.phase, self.vec = 0, None
        self.send_first(keep, send)

    def send_first(self, keep, send):
        self.keep = keep
        self.order.hold(keep)
        self.got = trade(send, self.axes[self.phase], 0)

    def near(self, vec=None):
        width = self.keep.shape[2]
        self.order.hold(self.got)
        if self.phase == 0:
            ins, outs = [self.keep, self.got], [vm((192, width), BF)]
            if vec is not None:
                ins += vec
                outs = [vm((192 + vec_rows(width), width), BF), vm((64, 128), F32)]
            result = self.order.call(
                partial(near_first_kernel, vec is not None), outs, ins, [V_SPEC] * len(ins), name="near_first"
            )
            other = result[0]
            if vec is not None:
                self.vec = result[1]
        else:
            rows = (48, 16)[self.phase - 1]
            ins, outs = [self.keep, self.got], [vm((rows, width), BF)]
            if self.vec is not None:
                ins.append(self.vec)
                outs = [vm((rows + 16, width), BF), vm((64, 128), F32)]
            result = self.order.call(
                partial(near_kernel, rows, self.vec is not None), outs, ins, [V_SPEC] * len(ins), name="near_sum"
            )
            other = result[0]
            if self.vec is not None:
                self.vec = result[1]
        self.got2 = trade(other, self.axes[self.phase], 1)

    def fin(self):
        width = self.keep.shape[2]
        self.order.drop(self.keep, self.got)
        ins, outs = [self.keep, self.got, self.got2], [vm((192, width), BF)]
        if self.vec is not None:
            ins.append(self.vec)
            outs.append(vm((64, 128), F32))
        result = self.order.call(
            partial(axis_total_kernel, self.vec is not None), outs, ins, [V_SPEC] * len(ins), name="axis_total"
        )
        self.total = result[0]
        if self.vec is not None:
            self.vec = result[1]
        self.order.hold(self.total)

    def second(self, *joined, vec=None):
        self.order.drop(*[part.total for part in (self,) + joined])
        ins = [part.total for part in (self,) + joined]
        widths = [x.shape[1] for x in ins]
        total = sum(widths)
        if vec is not None:
            ins.append(vec)
            self.vec = vec
        keep, send = self.order.call(
            partial(second_axis_kernel, self.axes[1], widths, vec is not None),
            [vm((2, 48, total), BF), vm((112 if vec is not None else 96, total), BF)],
            [self.place] + ins, [S_SPEC] + [V_SPEC] * len(ins), name="second_axis",
        )
        self.phase = 1
        self.send_first(keep, send)

    def third(self, *joined):
        parts = (self,) + joined
        for part in parts:
            self.order.drop(part.keep, part.got)
        widths = [part.keep.shape[2] for part in parts]
        width = sum(widths)
        ins = [x for part in parts for x in (part.keep, part.got, part.got2)]
        outs = [vm((2, 16, width), BF), vm((32, width), BF)]
        if self.vec is not None:
            ins.append(self.vec)
            outs = [vm((2, 16, width), BF), vm((48, width), BF), vm((64, 128), F32)]
        result = self.order.call(
            partial(third_axis_kernel, self.axes[2], widths, self.vec is not None), outs, [self.place] + ins,
            [S_SPEC] + [V_SPEC] * len(ins), [VMEM((4, 16, width), F32)], name="third_axis",
        )
        if self.vec is not None:
            self.vec = result[2]
        self.phase = 2
        self.send_first(result[0], result[1])

    def end(self):
        self.order.drop(self.keep, self.got)
        ins, outs = [self.keep, self.got, self.got2], [vm((12, self.keep.shape[2]), F32)]
        if self.vec is not None:
            ins.append(self.vec)
            outs.append(vm((64, 128), F32))
        result = self.order.call(
            partial(last_kernel, self.vec is not None), outs, ins, [V_SPEC] * len(ins), name="last_sum"
        )
        return result if self.vec is not None else result[0]


def other_core(x):
    return lax.ppermute(x, "seq", [(0, 1), (1, 0)])


def shards(inputs, history, alpha_mid, alpha_last, attn_gains, mlp_gains, w_qkv, w_out, w_up, w_down,
           doc_lengths, cotangent):
    core = lax.axis_index("seq")
    chip = lax.axis_index("dp")
    place = jnp.stack([core, chip // 16, (chip // 4) % 4, chip % 4]).astype(jnp.int32)
    w_up, w_down, w_qkv_hbm = (pltpu.with_memory_space_constraint(w, pltpu.HBM) for w in (w_up, w_down, w_qkv))
    order = Order()
    call = order.call
    lengths = doc_lengths
    up_axes, down_axes, attn_axes = (2, 0, 1), (1, 2, 0), (0, 1, 2)
    in_peer = other_core(inputs)
    g_peer = other_core(cotangent)

    dma = pltpu.SemaphoreType.DMA
    inputs_hbm, gains_hbm = (pltpu.with_memory_space_constraint(x, pltpu.HBM) for x in (inputs, attn_gains))
    att_out = [vm((R, D), BF)] + [vm((R, HW), BF)] * 4 + [vm((2 * HW // 128, T, 3 * T), F32)]
    stream0, normed0, q0, k0, v0, m0, probs0, cos, sin = call(
        attend_first_kernel, [vm((R, D), F32)] + att_out + [vm((R, 128), F32)] * 2,
        (place, lengths, inputs_hbm, in_peer, gains_hbm, w_qkv_hbm),
        [S_SPEC] * 2 + [H_SPEC, V_SPEC, H_SPEC, H_SPEC],
        [VMEM((T, D), BF), VMEM((2, D), F32), VMEM((D, 3 * HW), BF), dma((5,))], name="attend_first",
    )
    m0p = other_core(m0)
    order.hold(normed0, q0, k0, v0, probs0, cos, sin, m0, history)
    h_mid, h_last = call(
        mix_kernel, [vm((T, D), F32)] * 2, (alpha_mid, alpha_last, history), [S_SPEC, S_SPEC, V_SPEC],
        name="mix_history",
    )
    h_peer = other_core(h_mid)
    order.drop(history)
    order.hold(h_last, w_out)
    order.hold(inputs, in_peer, cotangent, g_peer, attn_gains, mlp_gains)
    mlp_scratch = [VMEM((D, FH), BF), VMEM((D, FH), BF), dma((2 * NCH,))]
    after0, nm0, act0, slope0, part0, part0s = call(
        mlp_first_kernel,
        [vm((R, D), F32), vm((R, D), BF), vm((R, FH), BF), vm((R, FH), F32), vm((R, D), F32), vm((R, D), BF)],
        (place, stream0, m0, m0p, mlp_gains, w_out, w_up, w_down),
        [S_SPEC] + [V_SPEC] * 5 + [H_SPEC] * 2, mlp_scratch, name="mlp_first",
        after=(g_peer,),
    )
    part0p = other_core(part0s)
    up_order, down_order = call(
        partial(row_order_kernel, (up_axes, down_axes)), [vm((D, D), BF)] * 2, (place,), [S_SPEC], name="row_order"
    )
    order.hold(up_order, down_order)
    order.hold(m0p, w_qkv)
    order.hold(after0, nm0, act0, slope0)
    stream1, block0, normed1, q1, k1, v1, m1, probs1 = call(
        attend_second_kernel, [vm((R, D), F32)] * 2 + att_out,
        (place, alpha_mid, after0, part0, part0p, h_mid, h_peer, attn_gains, w_qkv, cos, sin, lengths),
        [S_SPEC, S_SPEC] + [V_SPEC] * 9 + [S_SPEC], name="attend_second",
    )
    m1p = other_core(m1)
    order.hold(block0, stream1, normed1, q1, k1, v1, probs1)
    after1, nm1, act1, branch1, gup1, e1, e1s, go1, part1, part1s = call(
        mlp_last_kernel,
        [vm((R, D), F32), vm((R, D), BF), vm((R, FH), BF), vm((R, D), BF), vm((R, FH), BF), vm((R, D), F32),
         vm((R, D), BF), vm((R, D), F32), vm((R, D), F32), vm((T, D), BF)],
        (place, alpha_last, stream1, m1, m1p, cotangent, g_peer, mlp_gains, w_out, w_up, w_down),
        [S_SPEC, S_SPEC] + [V_SPEC] * 7 + [H_SPEC] * 2, mlp_scratch, name="mlp_last",
    )
    e1p = other_core(e1s)
    part1p = other_core(part1s)
    order.hold(m1, m1p, after1, go1, part1, part1s)

    quarter = vm((2, 192, FH), BF)
    whole_grad = [VMEM((D, FH), BF)]

    def ordered_chain(axes, x, rows, y, name):
        keep, send = call(
            ordered_grad_kernel, [quarter] * 2, (x, rows, y), [V_SPEC] * 3, name=name,
        )
        return Chain(order, place, axes, keep, send)

    def down_chain(branch, act):
        return ordered_chain(down_axes, branch, down_order, act, "down_grad")

    def up_chain(nm, gup):
        return ordered_chain(up_axes, nm, up_order, gup, "up_grad")

    def attn_chain(normed, packed, m, mp, ga):
        keep, send = call(
            attn_grad_kernel, [quarter] * 2, (place, normed, packed, m, mp, ga), [S_SPEC] + [V_SPEC] * 5, whole_grad,
            name="attn_grad",
        )
        return Chain(order, place, attn_axes, keep, send)

    def attn_parts(normed, packed, m, mp, ga):
        widths = (2 * HW, HW, HW)
        refs = call(
            attn_parts_kernel, [vm((2, 192, w), BF) for w in widths for _ in range(2)],
            (place, normed, packed, m, mp, ga, down_order, up_order), [S_SPEC] + [V_SPEC] * 7,
            [VMEM((D, 2 * HW), BF)], name="attn_parts",
        )
        axes = (attn_axes, down_axes, up_axes)
        return [Chain(order, place, a, refs[2 * j], refs[2 * j + 1]) for j, a in enumerate(axes)]

    def attn_back(layer, e, ep, go, after, q, k, v, probs):
        return call(
            partial(attend_back_kernel, layer),
            [vm((R, D), F32), vm((R, D), BF), vm((R, 3 * HW), BF), vm((R, D), F32), vm((R if layer else T, D), BF),
             vm((1, D), F32)],
            (place, e, ep, go, after, mlp_gains, w_out, w_qkv, q, k, v, probs, cos, sin),
            [S_SPEC] + [V_SPEC] * 13, [VMEM((R, HW), BF), VMEM((2, T, 128), F32)],
            name="attend_back",
        )

    up1 = up_chain(nm1, gup1)
    down1 = down_chain(branch1, act1)
    ga1, gb1, packed1, x1, x1s, gain_mlp1 = attn_back(1, e1, e1p, go1, after1, q1, k1, v1, probs1)
    x1p = other_core(x1s)
    order.drop(q1, k1, v1, probs1, go1)
    order.hold(ga1)
    attn1 = attn_chain(normed1, packed1, m1, m1p, gb1)
    order.drop(normed1, m1, m1p)
    up1.near()
    down1.near()
    grad_mix, go0, branch0, gup0, e0, e0s, gain_attn1 = call(
        mlp_back_kernel,
        [vm((R, D), F32), vm((R, D), F32), vm((R, D), BF), vm((R, FH), BF), vm((R, D), F32), vm((R, D), BF),
         vm((1, D), F32)],
        (place, alpha_mid, alpha_last, x1, x1p, ga1, stream1, attn_gains, cotangent, g_peer, slope0, w_up, w_down),
        [S_SPEC] * 3 + [V_SPEC] * 8 + [H_SPEC] * 2,
        [VMEM((D, FH), BF), VMEM((D, FH), BF), dma((2 * NCH,))], name="mlp_back",
    )
    e0p = other_core(e0s)
    order.drop(ga1, stream1, slope0)
    order.hold(go0, grad_mix)
    up0 = up_chain(nm0, gup0)
    down0 = down_chain(branch0, act0)
    order.drop(nm0, act0)
    attn1.near()
    up1.fin()
    down1.fin()
    ga0, gb0, packed0, x0, x0s, gain_mlp0 = attn_back(0, e0, e0p, go0, after0, q0, k0, v0, probs0)
    x0p = other_core(x0s)
    order.drop(q0, k0, v0, probs0, cos, sin, go0, after0, w_qkv, w_out)
    order.hold(x0, ga0)
    history_grad, h_sums, f_sums = call(
        history_kernel, [jax.ShapeDtypeStruct((HIST, T, D), BF), vm((HIST, 3, D), F32), vm((2, D), F32)],
        (place, alpha_mid, alpha_last, history, cotangent, g_peer, grad_mix, block0, after1, part1),
        [S_SPEC] * 3 + [V_SPEC] * 7, [VMEM((T, D), F32)] * 2 + [VMEM((HIST, T, D), BF), dma((HIST,))],
        name="history_grad", out_specs=[H_SPEC, V_SPEC, V_SPEC],
    )
    order.drop(grad_mix, history)
    attn1.fin()
    part_a, part_b, part_c = attn_parts(normed0, packed0, m0, m0p, gb0)
    order.drop(normed0, m0, m0p, up_order, down_order)
    vec = call(
        vector_kernel, vm((64, 128), F32), (h_sums, f_sums, inputs, in_peer, x0, place, gain_attn1, gain_mlp0, gain_mlp1),
        [V_SPEC] * 5 + [S_SPEC] + [V_SPEC] * 3, name="pack_sums",
    )
    got = trade(vec, attn_axes[0], 0)
    up0.near()
    down0.near()
    part_a.near(vec=[vec, got])
    part_b.near()
    part_c.near()
    up0.fin()
    down0.fin()
    part_a.fin()
    attn1.second(part_a, vec=part_a.vec)
    part_b.fin()
    down1.second(down0, part_b)
    part_c.fin()
    up1.second(up0, part_c)
    input_grad, _ = call(
        with_token(input_grad_kernel), [jax.ShapeDtypeStruct((T, D), F32), vm((8, 128), F32)],
        (place, x0, x0p, ga0, inputs, attn_gains), [S_SPEC] + [V_SPEC] * 5, name="input_grad",
    )
    final, _ = call(
        with_token(final_kernel), [jax.ShapeDtypeStruct((T, D), BF), vm((8, 128), F32)],
        (place, alpha_last, h_last, block0, after1, part1, part1p),
        [S_SPEC] * 2 + [V_SPEC] * 5, name="final_mix",
    )
    order.drop(x0, ga0, block0, after1, part1, h_last)
    chains = (attn1, down1, up1)
    for chain in chains:
        chain.near()
    for chain in chains:
        chain.third()
    for chain in chains:
        chain.near()
    down_sum, up_sum = down1.end(), up1.end()
    attn_sum, vec = attn1.end()
    vec_got = other_core(vec)
    pairs = lambda n: pltpu.HBM((6, 2, n), F32)
    flat = lambda *shape: pltpu.HBM(shape, F32)
    sums = (down_sum, up_sum, attn_sum)
    packed = call(
        pack_rows_kernel, vm((6, sum(x.shape[1] for x in sums)), F32), (place,) + sums, [S_SPEC] + [V_SPEC] * 3,
        name="pack_rows",
    )
    got = other_core(packed)
    up_grad, down_grad, value_grad, attn_out_grad = call(
        write_mlp_kernel, [pairs(2 * FH), pairs(2 * FH), vm((6, D), F32), vm((6, D), F32)],
        (place, down_sum, up_sum, got), [S_SPEC] + [V_SPEC] * 3, name="write_mlp",
    )
    qkv_grad, out_grad, attn_gains_grad, mlp_gains_grad, mid_grad, last_grad = call(
        write_attn_kernel,
        [pairs(3 * D), pairs(D), flat(2, D), flat(2, D), flat(1, HIST + 1), flat(1, HIST + 2)],
        (place, attn_sum, got, vec, vec_got, value_grad, attn_out_grad), [S_SPEC] + [V_SPEC] * 6,
        name="write_attn",
    )
    swap = lambda x: jnp.transpose(x, (1, 0, 2))
    return (
        final,
        input_grad,
        history_grad,
        mid_grad.reshape(HIST + 1),
        last_grad.reshape(HIST + 2),
        attn_gains_grad,
        mlp_gains_grad,
        swap(qkv_grad),
        swap(out_grad),
        swap(up_grad),
        swap(down_grad),
    )


def solution(mesh):
    both = P(("dp", "seq"), None)
    spread = P(None, ("dp", "seq"), None)
    return jax.shard_map(
        shards,
        mesh=mesh,
        in_specs=(both, spread) + (P(),) * 8 + (P("dp", None), both),
        out_specs=(both, both, spread) + (P(),) * 4 + (spread,) * 4,
        check_vma=False,
    )
```

```python
import math
from functools import partial

import jax
import jax.numpy as jnp
from jax import lax
from jax.experimental import pallas as pl
from jax.experimental.pallas import tpu as pltpu
from jax.sharding import PartitionSpec as P

BF = jnp.bfloat16
F32 = jnp.float32
NN = (((1,), (0,)), ((), ()))
NT = (((1,), (1,)), ((), ()))
TN = (((0,), (0,)), ((), ()))
EPS = 1e-5
MASKED = -1e30
ROT_BASE = 10000.0
HEAD = 64
GELU_C = math.sqrt(2.0 / math.pi)

R = 256
T = 128
D = 768
HW = 384
FH = 1536
CH = 512
NCH = FH // CH
HIST = 12
LN_ROWS = 64

VMEM = pltpu.VMEM
V_SPEC = pl.BlockSpec(memory_space=pltpu.VMEM)
S_SPEC = pl.BlockSpec(memory_space=pltpu.SMEM)
H_SPEC = pl.BlockSpec(memory_space=pl.ANY)
COSTS = {
    "attend_first": 2.0, "mlp_first": 2.0, "attend_second": 2.0, "mlp_last": 2.0, "attend_back": 8.0, "mlp_back": 8.0,
    "up_grad": 1.0, "down_grad": 1.0, "attn_grad": 1.0, "attn_parts": 1.0,
    "near_first": 1.5, "near_sum": 1.5, "axis_total": 0.5, "second_axis": 0.5, "third_axis": 1.5, "last_sum": 0.5,
}
LIMIT = 10 * 2**20


def dot(a, b, dims):
    return lax.dot_general(a, b, dims, preferred_element_type=F32)


def vm(shape, dtype):
    return pltpu.VMEM(shape, dtype)


class Order:
    def __init__(self):
        self.token = None
        self.held = []

    def hold(self, *arrays):
        self.held += arrays

    def drop(self, *arrays):
        self.held = [x for x in self.held if not any(x is y for y in arrays)]

    def call(self, kernel, outs, ins, in_specs, scratch=(), name=None, out_specs=None, after=()):
        many = isinstance(outs, (list, tuple))
        shapes = list(outs) if many else [outs]
        ins, in_specs = list(ins), list(in_specs)
        count = len(ins)
        after = list(after) + ([] if self.token is None else [self.token])
        in_specs += [H_SPEC] * len(after)
        kept = [x for x in self.held if not any(x is y for y in ins)]
        ins += after + kept
        in_specs += [V_SPEC] * len(kept)
        total = len(ins)
        ins = [pltpu.with_memory_space_constraint(x, VMEM) if spec is V_SPEC else x for x, spec in zip(ins, in_specs)]

        def body(*refs):
            kernel(*refs[:count], *refs[total:])

        result = pl.pallas_call(
            body,
            out_shape=shapes,
            in_specs=in_specs,
            out_specs=out_specs or [V_SPEC] * len(shapes),
            scratch_shapes=list(scratch),
            compiler_params=pltpu.CompilerParams(vmem_limit_bytes=LIMIT),
            cost_estimate=pl.CostEstimate(flops=int(1e9 * COSTS.get(name, 0.01)), bytes_accessed=1000, transcendentals=0),
            name=name,
        )(*ins)
        sizes = [math.prod(shape.shape) for shape in shapes]
        self.token = result[sizes.index(min(sizes))]
        return result if many else result[0]


def normalized(v):
    mean = jnp.mean(v, axis=-1, keepdims=True)
    shifted = v - mean
    var = jnp.mean(shifted * shifted, axis=-1, keepdims=True)
    rstd = lax.rsqrt(var + EPS)
    return shifted * rstd, rstd


def norm_back(v, e, gain):
    n, rstd = normalized(v)
    q = e * gain
    back = (
        q - jnp.mean(q, axis=-1, keepdims=True) - n * jnp.mean(q * n, axis=-1, keepdims=True)
    ) * rstd
    return back, jnp.sum(e * n, axis=0, keepdims=True)


def swap_halves(x):
    lane = lax.broadcasted_iota(jnp.int32, x.shape, 1) % HEAD
    return jnp.where(lane < HEAD // 2, pltpu.roll(x, 128 - 32, 1), pltpu.roll(x, 32, 1))


def head_lanes(shape, head):
    lane = lax.broadcasted_iota(jnp.int32, shape, 1)
    return (lane >= HEAD * head) & (lane < HEAD * (head + 1))


def first_place(lengths, t):
    second = lengths[0, 0]
    third = second + lengths[0, 1]
    return jnp.where(t >= third, third, jnp.where(t >= second, second, 0))


def allowed_block(lengths, half):
    shape = (T, T * (half + 1))
    t = lax.broadcasted_iota(jnp.int32, shape, 0) + T * half
    u = lax.broadcasted_iota(jnp.int32, shape, 1)
    first = first_place(lengths, lax.broadcasted_iota(jnp.int32, (T, 1), 0) + T * half)
    return (u >= first) & (u <= t)


def write_tables(lengths, cos, sin):
    t = lax.broadcasted_iota(jnp.int32, (R, 1), 0)
    offset = (t - first_place(lengths, t)).astype(F32)
    lane = lax.broadcasted_iota(jnp.int32, (1, 128), 1) % HEAD
    freq = jnp.exp((-math.log(ROT_BASE) * 2.0 / HEAD) * (lane % 32).astype(F32))
    angles = offset * freq
    cos[...] = jnp.cos(angles)
    sin[...] = jnp.sin(angles) * jnp.where(lane < 32, -1.0, 1.0)


def probs_columns(half):
    return slice(T * half, T * (2 * half + 1))


def softmax_block(q, k, allowed):
    scores = jnp.where(allowed, dot(q, k, NT), MASKED)
    top = jnp.max(scores, axis=-1, keepdims=True)
    weights = jnp.exp(scores - top)
    return weights * (1.0 / jnp.sum(weights, axis=-1, keepdims=True))


def gelu_and_slope(v):
    square = v * v
    t = jnp.tanh(GELU_C * v * (1.0 + 0.044715 * square))
    half = 0.5 * (1.0 + t)
    slope = half + 0.5 * v * (1.0 - t * t) * (GELU_C * (1.0 + 3.0 * 0.044715 * square))
    return v * half, slope


def qkv_copies(core, layer, w_qkv, wq, sem):
    return [
        pltpu.make_async_copy(
            w_qkv.at[layer, :, pl.ds(pl.multiple_of(D * j + HW * core, 128), HW)],
            wq.at[:, pl.ds(HW * j, HW)],
            sem.at[j],
        )
        for j in range(3)
    ]


def qkv_columns(w_qkv, layer, core, j, lo=0, width=HW):
    return w_qkv[layer, :, pl.ds(pl.multiple_of(D * j + HW * core + lo, 128), width)]


def out_rows(w_out, layer, part):
    return w_out[layer, pl.ds(pl.multiple_of(part * HW, 128), HW), :]


def ff_copies(core, layer, w, dst, sem, base):
    return [
        pltpu.make_async_copy(
            w.at[layer, :, pl.ds(pl.multiple_of(FH * core + CH * j, 128), CH)],
            dst.at[:, pl.ds(CH * j, CH)],
            sem.at[base + j],
        )
        for j in range(NCH)
    ]


def mix_kernel(am, al, history, mid, last):
    for r in range(0, T, 16):
        sl = slice(r, r + 16)
        acc_mid = jnp.zeros((16, D), F32)
        acc_last = jnp.zeros((16, D), F32)
        for k in range(HIST):
            h = history[k, sl, :].astype(F32)
            acc_mid += am[k] * h
            acc_last += al[k] * h
        mid[sl, :] = acc_mid
        last[sl, :] = acc_last


def attend_tail(layer, s_out, gain, columns, cos, sin, lengths, normed, q, k, v, mixed, probs_out):
    g = gain[layer : layer + 1, :]
    for r in range(0, R, LN_ROWS):
        sl = slice(r, r + LN_ROWS)
        n, _ = normalized(s_out[sl, :])
        normed[sl, :] = (n * g).astype(BF)
    x = normed[...]
    for j, dst in enumerate((q, k, v)):
        for p in range(HW // 128):
            lanes = slice(128 * p, 128 * (p + 1))
            packed = dot(x, columns(j, p), NN).astype(BF)
            if j == 2:
                dst[:, lanes] = packed
            else:
                f = packed.astype(F32)
                rot = f * cos[...] + swap_halves(f) * sin[...]
                if j == 0:
                    rot = rot * (1.0 / math.sqrt(HEAD))
                dst[:, lanes] = rot.astype(BF)
    for half in range(2):
        rows = slice(T * half, T * (half + 1))
        cols = slice(0, T * (half + 1))
        allowed = allowed_block(lengths, half)
        for p in range(HW // 128):
            lanes = slice(128 * p, 128 * (p + 1))
            qp = q[rows, lanes]
            kp = k[cols, lanes]
            vp = v[cols, lanes]
            acc = None
            for h in range(2):
                qh = jnp.where(head_lanes(qp.shape, h), qp, jnp.zeros_like(qp))
                vh = jnp.where(head_lanes(vp.shape, h), vp, jnp.zeros_like(vp))
                probs = softmax_block(qh, kp, allowed)
                probs_out[2 * p + h, :, probs_columns(half)] = probs
                part = dot(probs.astype(BF), vh, NN)
                acc = part if acc is None else acc + part
            mixed[rows, lanes] = acc.astype(BF)


def attend_first_kernel(place, lengths, inputs, peer, gains, w_qkv, w_up, w_down, stream, normed, q, k, v, mixed,
                        probs, cos, sin, wu, wd, own, gain, wq, sem):
    core = place[0]
    first = [pltpu.make_async_copy(inputs, own, sem.at[3]), pltpu.make_async_copy(gains, gain, sem.at[4])]
    copies = qkv_copies(core, 0, w_qkv, wq, sem)
    later = ff_copies(core, 0, w_up, wu, sem, 5) + ff_copies(core, 0, w_down, wd, sem, 5 + NCH)
    for cp in first + copies + later:
        cp.start()
    write_tables(lengths, cos, sin)
    for cp in first:
        cp.wait()
    stream[pl.ds(pl.multiple_of(core * T, T), T), :] = own[...].astype(F32)
    stream[pl.ds(pl.multiple_of((1 - core) * T, T), T), :] = peer[...].astype(F32)

    def columns(j, p):
        if p == 0:
            copies[j].wait()
        return wq[:, HW * j + 128 * p : HW * j + 128 * (p + 1)]

    attend_tail(0, stream, gain, columns, cos, sin, lengths, normed, q, k, v, mixed, probs)
    for cp in later:
        cp.wait()


def attend_second_kernel(place, am, after, p_own, p_peer, h_own, h_peer, gain, w_qkv, cos, sin, lengths,
                         stream, block, normed, q, k, v, mixed, probs):
    core = place[0]
    scale = am[HIST]
    stream[pl.ds(pl.multiple_of(core * T, T), T), :] = h_own[...]
    stream[pl.ds(pl.multiple_of((1 - core) * T, T), T), :] = h_peer[...]
    for r in range(0, R, LN_ROWS):
        sl = slice(r, r + LN_ROWS)
        b = after[sl, :] + (p_own[sl, :] + p_peer[sl, :].astype(F32))
        block[sl, :] = b
        stream[sl, :] = stream[sl, :] + scale * b
    columns = lambda j, p: qkv_columns(w_qkv, 1, core, j, 128 * p, 128)
    attend_tail(1, stream, gain, columns, cos, sin, lengths, normed, q, k, v, mixed, probs)


def mlp_front(core, layer, stream, m_own, m_peer, gain, after, normed, w_out):
    g = gain[layer : layer + 1, :]
    wo_own, wo_peer = out_rows(w_out, layer, core), out_rows(w_out, layer, 1 - core)
    for r in range(0, R, 128):
        sl = slice(r, r + 128)
        a = stream[sl, :] + (
            dot(m_own[sl, :], wo_own, NN) + dot(m_peer[sl, :], wo_peer, NN)
        )
        after[sl, :] = a
        n, _ = normalized(a)
        normed[sl, :] = (n * g).astype(BF)


def mlp_first_kernel(place, stream, m_own, m_peer, gain, w_out, wu, wd,
                     after, normed, act, slope, part, sent):
    core = place[0]
    mlp_front(core, 0, stream, m_own, m_peer, gain, after, normed, w_out)
    x = normed[...]
    for j in range(NCH):
        for i in range(0, CH, 256):
            cols = slice(CH * j + i, CH * j + i + 256)
            u = dot(x, wu[:, cols], NN)
            a, s = gelu_and_slope(u)
            act[:, cols] = a.astype(BF)
            slope[:, cols] = s
    total = dot(act[...], wd[...], NT)
    part[...] = total
    sent[...] = total.astype(BF)


def mlp_last_kernel(place, al, stream, m_own, m_peer, g_own, g_peer, gain, w_out, w_up, w_down,
                    after, normed, act, branch, gup, part, sent, go, down, down_sent, wu, wd, sem):
    core = place[0]
    up_cp = ff_copies(core, 1, w_up, wu, sem, 0)
    down_cp = ff_copies(core, 1, w_down, wd, sem, NCH)
    for pair in zip(up_cp, down_cp):
        for cp in pair:
            cp.start()
    scale = al[HIST + 1]
    own_rows = pl.ds(pl.multiple_of(core * T, T), T)
    peer_rows = pl.ds(pl.multiple_of((1 - core) * T, T), T)
    go[own_rows, :] = scale * g_own[...].astype(F32)
    go[peer_rows, :] = scale * g_peer[...].astype(F32)
    branch[...] = go[...].astype(BF)
    mlp_front(core, 1, stream, m_own, m_peer, gain, after, normed, w_out)
    x = normed[...]
    gb = branch[...]
    for j in range(NCH):
        up_cp[j].wait()
        down_cp[j].wait()
        for i in range(0, CH, 256):
            cols = slice(CH * j + i, CH * j + i + 256)
            u = dot(x, wu[:, cols], NN)
            a, s = gelu_and_slope(u)
            act[:, cols] = a.astype(BF)
            gup[:, cols] = (s * dot(gb, wd[:, cols], NN)).astype(BF)
    total = dot(gup[...], wu[...], NT)
    part[...] = total
    sent[...] = total.astype(BF)
    down[...] = dot(act[...], wd[...], NT)
    down_sent[...] = down[peer_rows, :].astype(BF)


def attend_back_kernel(layer, place, e_own, e_peer, go, after, gain, w_out, w_qkv, q, k, v, probs_in, cos, sin,
                       grad_after, grad_attn, grad_packed, part, sent, gain_grad, gm, acc):
    core = place[0]
    g = gain[layer : layer + 1, :]
    total = jnp.zeros((1, D), F32)
    for r in range(0, R, LN_ROWS):
        sl = slice(r, r + LN_ROWS)
        back, piece = norm_back(after[sl, :], e_own[sl, :] + e_peer[sl, :].astype(F32), g)
        total += piece
        ga = go[sl, :] + back
        grad_after[sl, :] = ga
        grad_attn[sl, :] = ga.astype(BF)
    gain_grad[...] = total
    gm[...] = dot(grad_attn[...], out_rows(w_out, layer, core), NT).astype(BF)
    scale = 1.0 / math.sqrt(HEAD)
    for p in range(HW // 128):
        lanes = slice(128 * p, 128 * (p + 1))
        for half in range(2):
            rows = slice(T * half, T * (half + 1))
            cols = slice(0, T * (half + 1))
            qp = q[rows, lanes]
            gp = gm[rows, lanes]
            kp = k[cols, lanes]
            vp = v[cols, lanes]
            dq = None
            for h in range(2):
                lane_q = head_lanes(qp.shape, h)
                qh = jnp.where(lane_q, qp, jnp.zeros_like(qp))
                gh = jnp.where(lane_q, gp, jnp.zeros_like(gp))
                kh = jnp.where(head_lanes(kp.shape, h), kp, jnp.zeros_like(kp))
                probs = probs_in[2 * p + h, :, probs_columns(half)]
                dprob = dot(gh, vp, NT)
                center = jnp.sum(probs * dprob, axis=-1, keepdims=True)
                ds = (probs * (dprob - center)).astype(BF)
                dqh = dot(ds, kh, NN)
                dkh = dot(ds, qh, TN)
                dvh = dot(probs.astype(BF), gh, TN)
                dq = dqh if dq is None else dq + dqh
                if half == 0 and h == 0:
                    dk, dv = dkh, dvh
                elif half == 0:
                    dk, dv = dk + dkh, dv + dvh
                    acc[0, :T, :] = dk
                    acc[1, :T, :] = dv
                elif h == 0:
                    dk, dv = dkh, dvh
                else:
                    dk, dv = dk + dkh, dv + dvh
            dq = dq * scale
            rot = dq * cos[rows, :] - swap_halves(dq) * sin[rows, :]
            grad_packed[rows, lanes] = rot.astype(BF)
        for half in range(2):
            rows = slice(T * half, T * (half + 1))
            dkr, dvr = dk[rows, :], dv[rows, :]
            if half == 0:
                dkr = dkr + acc[0, :T, :]
                dvr = dvr + acc[1, :T, :]
            rot = dkr * cos[rows, :] - swap_halves(dkr) * sin[rows, :]
            grad_packed[rows, HW + 128 * p : HW + 128 * (p + 1)] = rot.astype(BF)
            grad_packed[rows, 2 * HW + 128 * p : 2 * HW + 128 * (p + 1)] = dvr.astype(BF)
    total = dot(grad_packed[:, :HW], qkv_columns(w_qkv, layer, core, 0), NT)
    for j in range(1, 3):
        total += dot(grad_packed[:, HW * j : HW * (j + 1)], qkv_columns(w_qkv, layer, core, j), NT)
    part[...] = total
    if layer == 0:
        sent[...] = part[pl.ds(pl.multiple_of((1 - core) * T, T), T), :].astype(BF)
    else:
        sent[...] = total.astype(BF)


def mlp_back_kernel(place, am, al, e_own, e_peer, grad_after, stream, gain, g_own, g_peer, slope, w_up, w_down,
                    grad_mix, go, branch, gup, part, sent, gain_grad, wu, wd, sem):
    core = place[0]
    down_cp = ff_copies(core, 0, w_down, wd, sem, 0)
    up_cp = ff_copies(core, 0, w_up, wu, sem, NCH)
    for cp in down_cp + up_cp:
        cp.start()
    a_last = al[HIST]
    a_mid = am[HIST]
    go[pl.ds(pl.multiple_of(core * T, T), T), :] = a_last * g_own[...].astype(F32)
    go[pl.ds(pl.multiple_of((1 - core) * T, T), T), :] = a_last * g_peer[...].astype(F32)
    g = gain[1:2, :]
    total = jnp.zeros((1, D), F32)
    for r in range(0, R, LN_ROWS):
        sl = slice(r, r + LN_ROWS)
        back, piece = norm_back(stream[sl, :], e_own[sl, :] + e_peer[sl, :].astype(F32), g)
        total += piece
        gx = grad_after[sl, :] + back
        grad_mix[sl, :] = gx
        out = go[sl, :] + a_mid * gx
        go[sl, :] = out
        branch[sl, :] = out.astype(BF)
    gain_grad[...] = total
    gb = branch[...]
    for j in range(NCH):
        down_cp[j].wait()
        for i in range(0, CH, 256):
            cols = slice(CH * j + i, CH * j + i + 256)
            gup[:, cols] = (slope[:, cols] * dot(gb, wd[:, cols], NN)).astype(BF)
    for cp in up_cp:
        cp.wait()
    total = dot(gup[...], wu[...], NT)
    part[...] = total
    sent[...] = total.astype(BF)


def relations(place, axis):
    here = place[1 + axis]
    near = 1 + 2 * place[0]
    far = 3 - 2 * place[0]
    return here, here ^ far, here ^ near, here ^ 2


def rows_at(index, size):
    return pl.ds(pl.multiple_of(index * size, 16), size)


def split_rows(place, axis, grad, keep, send):
    for slot, quarter in enumerate(relations(place, axis)):
        dst = (keep, send)[slot // 2]
        dst[slot % 2] = grad[rows_at(quarter, 192), :]


def row_order_kernel(all_axes, place, *outs):
    r = lax.broadcasted_iota(jnp.int32, (1, D), 1)
    for axes, out in zip(all_axes, outs):
        slots = relations(place, axes[0])
        first = jnp.where(r < 192, slots[0], jnp.where(r < 384, slots[1], jnp.where(r < 576, slots[2], slots[3])))
        digit = {axes[0]: first, axes[1]: (r // 48) % 4, axes[2]: (r // 12) % 4}
        source = 12 * (16 * digit[0] + 4 * digit[1] + digit[2]) + r % 12
        for base in range(0, D, 64):
            row = lax.broadcasted_iota(jnp.int32, (64, D), 0) + base
            out[base : base + 64, :] = jnp.where(row == source, 1.0, 0.0).astype(BF)


def ordered_grad_kernel(x, order, y, keep, send):
    ordered = dot(x[...], order[...], NN).astype(BF)
    for j, dst in enumerate((keep, send)):
        half = dot(ordered[:, 384 * j : 384 * (j + 1)], y[...], TN).astype(BF)
        dst[0] = half[:192]
        dst[1] = half[192:]


def attn_grad_kernel(place, normed, grad_packed, m_own, m_peer, grad_attn, keep, send, grad):
    core = place[0]
    grad[:, : 3 * HW] = dot(normed[...], grad_packed[...], TN).astype(BF)
    ga = grad_attn[:, pl.ds(pl.multiple_of(HW * core, 128), HW)]
    grad[rows_at(core, HW), 3 * HW :] = dot(m_own[...], ga, TN).astype(BF)
    grad[rows_at(1 - core, HW), 3 * HW :] = dot(m_peer[...], ga, TN).astype(BF)
    split_rows(place, 0, grad, keep, send)


def attn_parts_kernel(place, normed, grad_packed, m_own, m_peer, grad_attn, by_x, by_z,
                      keep_a, send_a, keep_b, send_b, keep_c, send_c, grad):
    core = place[0]
    x = normed[...]
    grad[...] = dot(x, grad_packed[:, : 2 * HW], TN).astype(BF)
    split_rows(place, 0, grad, keep_a, send_a)
    values = dot(x, by_x[...], NN).astype(BF)
    mixed = (dot(m_own[...], by_z[rows_at(core, HW), :], NN) + dot(m_peer[...], by_z[rows_at(1 - core, HW), :], NN)).astype(BF)
    ga = grad_attn[:, pl.ds(pl.multiple_of(HW * core, 128), HW)]
    for left, right, keep, send in (
        (values, grad_packed[:, 2 * HW :], keep_b, send_b),
        (mixed, ga, keep_c, send_c),
    ):
        for j, dst in enumerate((keep, send)):
            half = dot(left[:, 384 * j : 384 * (j + 1)], right, TN).astype(BF)
            dst[0] = half[:192]
            dst[1] = half[192:]


def vec_rows(width):
    return 16 * math.ceil(12 * 128 / width)


def vec_tile(ref, row, c, j):
    per = ref.shape[1] // 128
    down, right = (4 * c + j) // per, (4 * c + j) % per
    return slice(row + 16 * down, row + 16 * (down + 1)), slice(128 * right, 128 * (right + 1))


def encode(vec, dst, row):
    rest = vec
    for c in range(3):
        piece = rest.astype(BF)
        rest = rest - piece.astype(F32)
        for j in range(4):
            dst[vec_tile(dst, row, c, j)] = piece[16 * j : 16 * (j + 1), :]


def decode(src, row):
    parts = []
    for j in range(4):
        block = [src[vec_tile(src, row, c, j)].astype(F32) for c in range(3)]
        parts.append((block[0] + block[1]) + block[2])
    return jnp.concatenate(parts, axis=0)


def near_first_kernel(with_vec, *refs):
    if with_vec:
        keep, got, vec, vec_got, out, vec_out = refs
        total = vec[...] + vec_got[...]
        vec_out[...] = total
        encode(total, out, 192)
    else:
        keep, got, out = refs
    out[0:192, :] = (keep[1].astype(F32) + got[1].astype(F32)).astype(BF)


def near_kernel(rows, with_vec, *refs):
    if with_vec:
        keep, got, vec, out, vec_out = refs
        total = vec[...] + decode(got, 2 * rows)
        vec_out[...] = total
        encode(total, out, rows)
    else:
        keep, got, out = refs
    out[0:rows, :] = (keep[1].astype(F32) + got[rows : 2 * rows, :].astype(F32)).astype(BF)


def last_kernel(with_vec, *refs):
    if with_vec:
        keep, got, got2, vec, out, vec_out = refs
        vec_out[...] = vec[...] + decode(got2, 16)
    else:
        keep, got, got2, out = refs
    out[...] = keep[0, 0:12, :].astype(F32) + got[0:12, :].astype(F32) + got2[0:12, :].astype(F32)


def axis_total_kernel(with_vec, *refs):
    if with_vec:
        keep, got, got2, vec, out, vec_out = refs
        vec_out[...] = vec[...] + decode(got2, 192)
    else:
        keep, got, got2, out = refs
    out[...] = (keep[0].astype(F32) + got[0].astype(F32) + got2[0:192, :].astype(F32)).astype(BF)


def second_axis_kernel(axis, widths, with_vec, place, *refs):
    keep, send = refs[-2:]
    if with_vec:
        encode(refs[len(widths)][...], send, 96)
    for slot, index in enumerate(relations(place, axis)):
        lo = 0
        for total, width in zip(refs, widths):
            lanes = slice(lo, lo + width)
            lo += width
            value = total[rows_at(index, 48), :]
            if slot < 2:
                keep[slot, :, lanes] = value
            else:
                send[48 * (slot - 2) : 48 * (slot - 1), lanes] = value


def third_axis_kernel(axis, widths, with_vec, place, *refs):
    count = 3 * len(widths)
    keep, send = refs[count + with_vec : count + with_vec + 2]
    scr = refs[-1]
    lo = 0
    for j, width in enumerate(widths):
        kept, got, got2 = refs[3 * j : 3 * j + 3]
        total = kept[0].astype(F32) + got[0:48, :].astype(F32) + got2[0:48, :].astype(F32)
        for i in range(4):
            scr[i, 0:12, lo : lo + width] = total[12 * i : 12 * (i + 1), :]
            scr[i, 12:16, lo : lo + width] = jnp.zeros((4, width), F32)
        lo += width
    for slot, index in enumerate(relations(place, axis)):
        value = scr[index].astype(BF)
        if slot < 2:
            keep[slot] = value
        else:
            send[16 * (slot - 2) : 16 * (slot - 1), :] = value
    if with_vec:
        vec, vec_out = refs[count], refs[-2]
        total = vec[...] + decode(refs[2], 48)
        vec_out[...] = total
        encode(total, send, 32)


def pack_rows_kernel(place, *refs):
    out = refs[-1]
    lo = 0
    for ref in refs[:-1]:
        width = ref.shape[1]
        out[:, lo : lo + width] = jnp.where(place[0] == 0, ref[6:12, :], ref[0:6, :])
        lo += width


def with_token(kernel):
    def body(*refs):
        kernel(*refs[:-1])
        refs[-1][...] = jnp.zeros_like(refs[-1])

    return body


def put(dst, layer, lo, value):
    for row in range(6):
        dst[row, layer : layer + 1, lo : lo + value.shape[1]] = value[row : row + 1, :]


def both_cores(first, ref, got):
    own = jnp.where(first, ref[0:6, :], ref[6:12, :])
    other = got[...]
    return jnp.where(first, own, other), jnp.where(first, other, own)


def write_mlp_kernel(place, down, up, got, up_out, down_out, value_out, attn_out_out):
    first = place[0] == 0
    width = 2 * FH + HW
    for ref, other, dst, rest in (
        (down, got.at[:, :width], down_out, value_out),
        (up, got.at[:, width : 2 * width], up_out, attn_out_out),
    ):
        for c, both in enumerate(both_cores(first, ref, other)):
            for layer in range(2):
                put(dst, layer, FH * c, both[:, FH * (1 - layer) : FH * (2 - layer)])
            rest[:, HW * c : HW * (c + 1)] = both[:, 2 * FH :]


def write_attn_kernel(place, attn, got, vec, vec_got, value_in, out_in,
                      qkv_out, out_out, attn_gains, mlp_gains, mid_out, last_out):
    for c, both in enumerate(both_cores(place[0] == 0, attn, got.at[:, 2 * (2 * FH + HW) :])):
        for i in range(3):
            put(qkv_out, 1, D * i + HW * c, both[:, HW * i : HW * (i + 1)])
        put(out_out, 1, HW * c, both[:, 3 * HW : 4 * HW])
        for i in range(2):
            put(qkv_out, 0, D * i + HW * c, both[:, FH + HW * i : FH + HW * (i + 1)])
    put(qkv_out, 0, 2 * D, value_in[...])
    put(out_out, 0, 0, out_in[...])
    total = vec[...] + vec_got[...]
    for j in range(D // 128):
        lanes = slice(128 * j, 128 * (j + 1))
        attn_gains[:, lanes] = total[4 * j : 4 * j + 2, :]
        mlp_gains[:, lanes] = total[4 * j + 2 : 4 * j + 4, :]
    for dst, base, count in ((mid_out, 24, HIST + 1), (last_out, 37, HIST + 2)):
        lane = lax.broadcasted_iota(jnp.int32, (1, 128), 1)
        row = jnp.zeros((1, 128), F32)
        for i in range(count):
            row = jnp.where(lane == i, total[base + i : base + i + 1, :], row)
        dst[...] = row[:, :count]


def input_grad_kernel(place, e_part, e_peer, grad_after, own, gain, out):
    core = place[0]
    rows = pl.ds(pl.multiple_of(core * T, T), T)
    back, _ = norm_back(own[...].astype(F32), e_part[rows, :] + e_peer[...].astype(F32), gain[0:1, :])
    out[...] = grad_after[rows, :] + back


def final_kernel(place, al, h_last, block, after, p_own, p_peer, out):
    core = place[0]
    rows = pl.ds(pl.multiple_of(core * T, T), T)
    b_last = after[rows, :] + (p_own[rows, :] + p_peer[...].astype(F32))
    out[...] = (h_last[...] + al[HIST] * block[rows, :] + al[HIST + 1] * b_last).astype(BF)


def history_kernel(place, am, al, history, g_own, g_peer, grad_mix, block, after, part, out, sums, f_sums, g32, gm32, staged,
                   sem):
    own = pl.ds(pl.multiple_of(place[0] * T, T), T)
    peer = pl.ds(pl.multiple_of((1 - place[0]) * T, T), T)
    g32[...] = g_own[...].astype(F32)
    gm32[...] = grad_mix[own, :]
    copies = []
    for k in range(HIST):
        mid = jnp.zeros((8, D), F32)
        last = jnp.zeros((8, D), F32)
        for r in range(0, T, 16):
            sl = slice(r, r + 16)
            gm, g = gm32[sl, :], g32[sl, :]
            staged[k, sl, :] = (al[k] * g + am[k] * gm).astype(BF)
            h = history[k, sl, :].astype(F32)
            a, b = h * gm, h * g
            mid += a[:8] + a[8:]
            last += b[:8] + b[8:]
        copies.append(pltpu.make_async_copy(staged.at[k], out.at[k], sem.at[k]))
        copies[k].start()
        sums[k, 0:1, :] = jnp.sum(mid, axis=0, keepdims=True)
        sums[k, 1:2, :] = jnp.sum(last, axis=0, keepdims=True)
    b_own = block[own, :]
    sums[0, 2:3, :] = jnp.sum(b_own * gm32[...], axis=0, keepdims=True)
    f_sums[0:1, :] = jnp.sum(g32[...] * b_own, axis=0, keepdims=True)
    f_sums[1:2, :] = jnp.sum(g32[...] * (after[own, :] + part[own, :]), axis=0, keepdims=True) + jnp.sum(
        g_peer[...].astype(F32) * part[peer, :], axis=0, keepdims=True
    )
    for copy in copies:
        copy.wait()


def vector_kernel(h_sums, f_sums, own, peer, x_part, place, ga1, gm0, gm1, out):
    ga0 = jnp.zeros((1, D), F32)
    for ref, core in ((own, place[0]), (peer, 1 - place[0])):
        n, _ = normalized(ref[...].astype(F32))
        ga0 += jnp.sum(x_part[pl.ds(pl.multiple_of(core * T, T), T), :] * n, axis=0, keepdims=True)
    for j in range(D // 128):
        lanes = slice(128 * j, 128 * (j + 1))
        out[4 * j : 4 * j + 1, :] = ga0[:, lanes]
        out[4 * j + 1 : 4 * j + 2, :] = 0.5 * ga1[:, lanes]
        out[4 * j + 2 : 4 * j + 3, :] = 0.5 * gm0[:, lanes]
        out[4 * j + 3 : 4 * j + 4, :] = 0.5 * gm1[:, lanes]
    for k in range(HIST):
        out[24 + k : 25 + k, :] = jnp.broadcast_to(
            jnp.sum(h_sums[k, 0:1, :], axis=-1, keepdims=True), (1, 128)
        )
        out[37 + k : 38 + k, :] = jnp.broadcast_to(
            jnp.sum(h_sums[k, 1:2, :], axis=-1, keepdims=True), (1, 128)
        )
    out[36:37, :] = jnp.broadcast_to(jnp.sum(h_sums[0, 2:3, :], axis=-1, keepdims=True), (1, 128))
    out[49:51, :] = jnp.broadcast_to(jnp.sum(f_sums[...], axis=-1, keepdims=True), (2, 128))
    out[51:64, :] = jnp.zeros((13, 128), F32)


def coords(i):
    return [i // 16, (i // 4) % 4, i % 4]


def partner_pairs(axis, step):
    pairs = []
    for chip in range(64):
        for core in range(2):
            flip = (1, 3)[(step + core) % 2]
            there = coords(chip)
            there[axis] ^= flip
            pairs.append((2 * chip + core, 2 * (there[0] * 16 + there[1] * 4 + there[2]) + core))
    return pairs


def trade(x, axis, step):
    return lax.ppermute(x, ("dp", "seq"), partner_pairs(axis, step))


class Chain:
    def __init__(self, order, place, axes, keep, send):
        self.order, self.place, self.axes = order, place, axes
        self.phase, self.vec = 0, None
        self.send_first(keep, send)

    def send_first(self, keep, send):
        self.keep = keep
        self.order.hold(keep)
        self.got = trade(send, self.axes[self.phase], 0)

    def near(self, vec=None):
        width = self.keep.shape[2]
        self.order.hold(self.got)
        if self.phase == 0:
            ins, outs = [self.keep, self.got], [vm((192, width), BF)]
            if vec is not None:
                ins += vec
                outs = [vm((192 + vec_rows(width), width), BF), vm((64, 128), F32)]
            result = self.order.call(
                partial(near_first_kernel, vec is not None), outs, ins, [V_SPEC] * len(ins), name="near_first"
            )
            other = result[0]
            if vec is not None:
                self.vec = result[1]
        else:
            rows = (48, 16)[self.phase - 1]
            ins, outs = [self.keep, self.got], [vm((rows, width), BF)]
            if self.vec is not None:
                ins.append(self.vec)
                outs = [vm((rows + 16, width), BF), vm((64, 128), F32)]
            result = self.order.call(
                partial(near_kernel, rows, self.vec is not None), outs, ins, [V_SPEC] * len(ins), name="near_sum"
            )
            other = result[0]
            if self.vec is not None:
                self.vec = result[1]
        self.got2 = trade(other, self.axes[self.phase], 1)

    def fin(self):
        width = self.keep.shape[2]
        self.order.drop(self.keep, self.got)
        ins, outs = [self.keep, self.got, self.got2], [vm((192, width), BF)]
        if self.vec is not None:
            ins.append(self.vec)
            outs.append(vm((64, 128), F32))
        result = self.order.call(
            partial(axis_total_kernel, self.vec is not None), outs, ins, [V_SPEC] * len(ins), name="axis_total"
        )
        self.total = result[0]
        if self.vec is not None:
            self.vec = result[1]
        self.order.hold(self.total)

    def second(self, *joined, vec=None):
        self.order.drop(*[part.total for part in (self,) + joined])
        ins = [part.total for part in (self,) + joined]
        widths = [x.shape[1] for x in ins]
        total = sum(widths)
        if vec is not None:
            ins.append(vec)
            self.vec = vec
        keep, send = self.order.call(
            partial(second_axis_kernel, self.axes[1], widths, vec is not None),
            [vm((2, 48, total), BF), vm((112 if vec is not None else 96, total), BF)],
            [self.place] + ins, [S_SPEC] + [V_SPEC] * len(ins), name="second_axis",
        )
        self.phase = 1
        self.send_first(keep, send)

    def third(self, *joined):
        parts = (self,) + joined
        for part in parts:
            self.order.drop(part.keep, part.got)
        widths = [part.keep.shape[2] for part in parts]
        width = sum(widths)
        ins = [x for part in parts for x in (part.keep, part.got, part.got2)]
        outs = [vm((2, 16, width), BF), vm((32, width), BF)]
        if self.vec is not None:
            ins.append(self.vec)
            outs = [vm((2, 16, width), BF), vm((48, width), BF), vm((64, 128), F32)]
        result = self.order.call(
            partial(third_axis_kernel, self.axes[2], widths, self.vec is not None), outs, [self.place] + ins,
            [S_SPEC] + [V_SPEC] * len(ins), [VMEM((4, 16, width), F32)], name="third_axis",
        )
        if self.vec is not None:
            self.vec = result[2]
        self.phase = 2
        self.send_first(result[0], result[1])

    def end(self):
        self.order.drop(self.keep, self.got)
        ins, outs = [self.keep, self.got, self.got2], [vm((12, self.keep.shape[2]), F32)]
        if self.vec is not None:
            ins.append(self.vec)
            outs.append(vm((64, 128), F32))
        result = self.order.call(
            partial(last_kernel, self.vec is not None), outs, ins, [V_SPEC] * len(ins), name="last_sum"
        )
        return result if self.vec is not None else result[0]


def other_core(x):
    return lax.ppermute(x, "seq", [(0, 1), (1, 0)])


def shards(inputs, history, alpha_mid, alpha_last, attn_gains, mlp_gains, w_qkv, w_out, w_up, w_down,
           doc_lengths, cotangent):
    core = lax.axis_index("seq")
    chip = lax.axis_index("dp")
    place = jnp.stack([core, chip // 16, (chip // 4) % 4, chip % 4]).astype(jnp.int32)
    w_up, w_down, w_qkv_hbm = (pltpu.with_memory_space_constraint(w, pltpu.HBM) for w in (w_up, w_down, w_qkv))
    order = Order()
    call = order.call
    lengths = doc_lengths
    up_axes, down_axes, attn_axes = (2, 0, 1), (1, 2, 0), (0, 1, 2)
    in_peer = other_core(inputs)
    g_peer = other_core(cotangent)

    dma = pltpu.SemaphoreType.DMA
    inputs_hbm, gains_hbm = (pltpu.with_memory_space_constraint(x, pltpu.HBM) for x in (inputs, attn_gains))
    att_out = [vm((R, D), BF)] + [vm((R, HW), BF)] * 4 + [vm((2 * HW // 128, T, 3 * T), F32)]
    stream0, normed0, q0, k0, v0, m0, probs0, cos, sin, wu0, wd0 = call(
        attend_first_kernel, [vm((R, D), F32)] + att_out + [vm((R, 128), F32)] * 2 + [vm((D, FH), BF)] * 2,
        (place, lengths, inputs_hbm, in_peer, gains_hbm, w_qkv_hbm, w_up, w_down),
        [S_SPEC] * 2 + [H_SPEC, V_SPEC] + [H_SPEC] * 4,
        [VMEM((T, D), BF), VMEM((2, D), F32), VMEM((D, 3 * HW), BF), dma((5 + 2 * NCH,))], name="attend_first",
    )
    m0p = other_core(m0)
    order.hold(normed0, q0, k0, v0, probs0, cos, sin, m0, history, wu0, wd0)
    h_mid, h_last = call(
        mix_kernel, [vm((T, D), F32)] * 2, (alpha_mid, alpha_last, history), [S_SPEC, S_SPEC, V_SPEC],
        name="mix_history",
    )
    h_peer = other_core(h_mid)
    order.drop(history)
    order.hold(h_last, w_out)
    order.hold(inputs, in_peer, cotangent, g_peer, attn_gains, mlp_gains)
    mlp_scratch = [VMEM((D, FH), BF), VMEM((D, FH), BF), dma((2 * NCH,))]
    after0, nm0, act0, slope0, part0, part0s = call(
        mlp_first_kernel,
        [vm((R, D), F32), vm((R, D), BF), vm((R, FH), BF), vm((R, FH), F32), vm((R, D), F32), vm((R, D), BF)],
        (place, stream0, m0, m0p, mlp_gains, w_out, wu0, wd0),
        [S_SPEC] + [V_SPEC] * 7, name="mlp_first",
        after=(g_peer,),
    )
    part0p = other_core(part0s)
    up_order, down_order = call(
        partial(row_order_kernel, (up_axes, down_axes)), [vm((D, D), BF)] * 2, (place,), [S_SPEC], name="row_order"
    )
    order.hold(up_order, down_order)
    order.hold(m0p, w_qkv)
    order.drop(wu0, wd0)
    order.hold(after0, nm0, act0, slope0)
    stream1, block0, normed1, q1, k1, v1, m1, probs1 = call(
        attend_second_kernel, [vm((R, D), F32)] * 2 + att_out,
        (place, alpha_mid, after0, part0, part0p, h_mid, h_peer, attn_gains, w_qkv, cos, sin, lengths),
        [S_SPEC, S_SPEC] + [V_SPEC] * 9 + [S_SPEC], name="attend_second",
    )
    m1p = other_core(m1)
    order.hold(block0, stream1, normed1, q1, k1, v1, probs1)
    after1, nm1, act1, branch1, gup1, e1, e1s, go1, part1, part1s = call(
        mlp_last_kernel,
        [vm((R, D), F32), vm((R, D), BF), vm((R, FH), BF), vm((R, D), BF), vm((R, FH), BF), vm((R, D), F32),
         vm((R, D), BF), vm((R, D), F32), vm((R, D), F32), vm((T, D), BF)],
        (place, alpha_last, stream1, m1, m1p, cotangent, g_peer, mlp_gains, w_out, w_up, w_down),
        [S_SPEC, S_SPEC] + [V_SPEC] * 7 + [H_SPEC] * 2, mlp_scratch, name="mlp_last",
    )
    e1p = other_core(e1s)
    part1p = other_core(part1s)
    order.hold(m1, m1p, after1, go1, part1, part1s)

    quarter = vm((2, 192, FH), BF)
    whole_grad = [VMEM((D, FH), BF)]

    def ordered_chain(axes, x, rows, y, name):
        keep, send = call(
            ordered_grad_kernel, [quarter] * 2, (x, rows, y), [V_SPEC] * 3, name=name,
        )
        return Chain(order, place, axes, keep, send)

    def down_chain(branch, act):
        return ordered_chain(down_axes, branch, down_order, act, "down_grad")

    def up_chain(nm, gup):
        return ordered_chain(up_axes, nm, up_order, gup, "up_grad")

    def attn_chain(normed, packed, m, mp, ga):
        keep, send = call(
            attn_grad_kernel, [quarter] * 2, (place, normed, packed, m, mp, ga), [S_SPEC] + [V_SPEC] * 5, whole_grad,
            name="attn_grad",
        )
        return Chain(order, place, attn_axes, keep, send)

    def attn_parts(normed, packed, m, mp, ga):
        widths = (2 * HW, HW, HW)
        refs = call(
            attn_parts_kernel, [vm((2, 192, w), BF) for w in widths for _ in range(2)],
            (place, normed, packed, m, mp, ga, down_order, up_order), [S_SPEC] + [V_SPEC] * 7,
            [VMEM((D, 2 * HW), BF)], name="attn_parts",
        )
        axes = (attn_axes, down_axes, up_axes)
        return [Chain(order, place, a, refs[2 * j], refs[2 * j + 1]) for j, a in enumerate(axes)]

    def attn_back(layer, e, ep, go, after, q, k, v, probs):
        return call(
            partial(attend_back_kernel, layer),
            [vm((R, D), F32), vm((R, D), BF), vm((R, 3 * HW), BF), vm((R, D), F32), vm((R if layer else T, D), BF),
             vm((1, D), F32)],
            (place, e, ep, go, after, mlp_gains, w_out, w_qkv, q, k, v, probs, cos, sin),
            [S_SPEC] + [V_SPEC] * 13, [VMEM((R, HW), BF), VMEM((2, T, 128), F32)],
            name="attend_back",
        )

    up1 = up_chain(nm1, gup1)
    down1 = down_chain(branch1, act1)
    ga1, gb1, packed1, x1, x1s, gain_mlp1 = attn_back(1, e1, e1p, go1, after1, q1, k1, v1, probs1)
    x1p = other_core(x1s)
    order.drop(q1, k1, v1, probs1, go1)
    order.hold(ga1)
    attn1 = attn_chain(normed1, packed1, m1, m1p, gb1)
    order.drop(normed1, m1, m1p)
    up1.near()
    down1.near()
    grad_mix, go0, branch0, gup0, e0, e0s, gain_attn1 = call(
        mlp_back_kernel,
        [vm((R, D), F32), vm((R, D), F32), vm((R, D), BF), vm((R, FH), BF), vm((R, D), F32), vm((R, D), BF),
         vm((1, D), F32)],
        (place, alpha_mid, alpha_last, x1, x1p, ga1, stream1, attn_gains, cotangent, g_peer, slope0, w_up, w_down),
        [S_SPEC] * 3 + [V_SPEC] * 8 + [H_SPEC] * 2,
        [VMEM((D, FH), BF), VMEM((D, FH), BF), dma((2 * NCH,))], name="mlp_back",
    )
    e0p = other_core(e0s)
    order.drop(ga1, stream1, slope0)
    order.hold(go0, grad_mix)
    up0 = up_chain(nm0, gup0)
    down0 = down_chain(branch0, act0)
    order.drop(nm0, act0)
    attn1.near()
    up1.fin()
    down1.fin()
    ga0, gb0, packed0, x0, x0s, gain_mlp0 = attn_back(0, e0, e0p, go0, after0, q0, k0, v0, probs0)
    x0p = other_core(x0s)
    order.drop(q0, k0, v0, probs0, cos, sin, go0, after0, w_qkv, w_out)
    order.hold(x0, ga0)
    history_grad, h_sums, f_sums = call(
        history_kernel, [jax.ShapeDtypeStruct((HIST, T, D), BF), vm((HIST, 3, D), F32), vm((2, D), F32)],
        (place, alpha_mid, alpha_last, history, cotangent, g_peer, grad_mix, block0, after1, part1),
        [S_SPEC] * 3 + [V_SPEC] * 7, [VMEM((T, D), F32)] * 2 + [VMEM((HIST, T, D), BF), dma((HIST,))],
        name="history_grad", out_specs=[H_SPEC, V_SPEC, V_SPEC],
    )
    order.drop(grad_mix, history)
    attn1.fin()
    part_a, part_b, part_c = attn_parts(normed0, packed0, m0, m0p, gb0)
    order.drop(normed0, m0, m0p, up_order, down_order)
    vec = call(
        vector_kernel, vm((64, 128), F32), (h_sums, f_sums, inputs, in_peer, x0, place, gain_attn1, gain_mlp0, gain_mlp1),
        [V_SPEC] * 5 + [S_SPEC] + [V_SPEC] * 3, name="pack_sums",
    )
    got = trade(vec, attn_axes[0], 0)
    up0.near()
    down0.near()
    part_a.near(vec=[vec, got])
    part_b.near()
    part_c.near()
    up0.fin()
    down0.fin()
    part_a.fin()
    attn1.second(part_a, vec=part_a.vec)
    part_b.fin()
    down1.second(down0, part_b)
    part_c.fin()
    up1.second(up0, part_c)
    input_grad, _ = call(
        with_token(input_grad_kernel), [jax.ShapeDtypeStruct((T, D), F32), vm((8, 128), F32)],
        (place, x0, x0p, ga0, inputs, attn_gains), [S_SPEC] + [V_SPEC] * 5, name="input_grad",
    )
    final, _ = call(
        with_token(final_kernel), [jax.ShapeDtypeStruct((T, D), BF), vm((8, 128), F32)],
        (place, alpha_last, h_last, block0, after1, part1, part1p),
        [S_SPEC] * 2 + [V_SPEC] * 5, name="final_mix",
    )
    order.drop(x0, ga0, block0, after1, part1, h_last)
    chains = (attn1, down1, up1)
    for chain in chains:
        chain.near()
    for chain in chains:
        chain.third()
    for chain in chains:
        chain.near()
    down_sum, up_sum = down1.end(), up1.end()
    attn_sum, vec = attn1.end()
    vec_got = other_core(vec)
    pairs = lambda n: pltpu.HBM((6, 2, n), F32)
    flat = lambda *shape: pltpu.HBM(shape, F32)
    sums = (down_sum, up_sum, attn_sum)
    packed = call(
        pack_rows_kernel, vm((6, sum(x.shape[1] for x in sums)), F32), (place,) + sums, [S_SPEC] + [V_SPEC] * 3,
        name="pack_rows",
    )
    got = other_core(packed)
    up_grad, down_grad, value_grad, attn_out_grad = call(
        write_mlp_kernel, [pairs(2 * FH), pairs(2 * FH), vm((6, D), F32), vm((6, D), F32)],
        (place, down_sum, up_sum, got), [S_SPEC] + [V_SPEC] * 3, name="write_mlp",
    )
    qkv_grad, out_grad, attn_gains_grad, mlp_gains_grad, mid_grad, last_grad = call(
        write_attn_kernel,
        [pairs(3 * D), pairs(D), flat(2, D), flat(2, D), flat(1, HIST + 1), flat(1, HIST + 2)],
        (place, attn_sum, got, vec, vec_got, value_grad, attn_out_grad), [S_SPEC] + [V_SPEC] * 6,
        name="write_attn",
    )
    swap = lambda x: jnp.transpose(x, (1, 0, 2))
    return (
        final,
        input_grad,
        history_grad,
        mid_grad.reshape(HIST + 1),
        last_grad.reshape(HIST + 2),
        attn_gains_grad,
        mlp_gains_grad,
        swap(qkv_grad),
        swap(out_grad),
        swap(up_grad),
        swap(down_grad),
    )


def solution(mesh):
    both = P(("dp", "seq"), None)
    spread = P(None, ("dp", "seq"), None)
    return jax.shard_map(
        shards,
        mesh=mesh,
        in_specs=(both, spread) + (P(),) * 8 + (P("dp", None), both),
        out_specs=(both, both, spread) + (P(),) * 4 + (spread,) * 4,
        check_vma=False,
    )
```
